32 devices in a mesh: dp: 16 (over z, y, x), tensor: 2 (over core).
Axes of the slice: x: 2, y: 2, z: 4, core: 2. Of those that a mesh axis runs over, the one named last changes fastest.
Arguments:
- activations: bfloat16 [16384, 1024], P(('dp', 'tensor')), may hold values from -6 to 6
- targets: float32 [16384, 1024], P(('dp', 'tensor')), may hold values from -6 to 6
- lengths: int32 [16], P('dp'), may hold values from 1 to 1024, as said below
- token_mask: int32 [16384], P(('dp', 'tensor')), may hold values 0 or 1
- routes: int32 [16384, 8], P('dp'), may hold values from 0 to 31, all different within a row; in each aligned block of 1024 rows (0 to 1023, 1024 to 2047, ...) at most 384 rows name the same one
- route_weights: float32 [16384, 8], P('dp'), may hold values from 0.3 to 0.9
- norm_gains: float32 [2, 1024], replicated, may hold values from 0.5 to 1.5
- attention_master: float32 [1024, 3072], P('dp', 'tensor')
- expert_master: float32 [128, 3, 128, 1024], P('dp', None, 'tensor'), may hold values from -0.1875 to 0.1875
- attention_left: float32 [16, 12, 64, 64], P('dp', 'tensor'), as said below
- attention_right: float32 [16, 12, 256, 256], P('dp', 'tensor'), as said below
- attention_left_root: float32 [16, 12, 64, 64], P('dp', 'tensor'), as said below
- attention_right_root: float32 [16, 12, 256, 256], P('dp', 'tensor'), as said below
- expert_left: float32 [128, 3, 4, 128, 64], P('dp', None, None, 'tensor'), as said below
- expert_right: float32 [128, 3, 8, 256, 256], P('dp', None, 'tensor'), as said below
- expert_left_root: float32 [128, 3, 4, 128, 64], P('dp', None, None, 'tensor'), as said below
- expert_right_root: float32 [128, 3, 8, 256, 256], P('dp', None, 'tensor'), as said below
Outputs:
- output: float32 [16384, 1024], P(('dp', 'tensor'))
- mean_loss: float32 [], replicated
- input_grad: float32 [16384, 1024], P(('dp', 'tensor'))
- gain_grad: float32 [2, 1024], replicated
- gains_new: float32 [2, 1024], replicated
- attention_grad: float32 [1024, 3072], P('dp', 'tensor')
- attention_left_new: float32 [16, 12, 64, 64], P('dp', 'tensor')
- attention_right_new: float32 [16, 12, 256, 256], P('dp', 'tensor')
- attention_new: float32 [1024, 3072], P('dp', 'tensor')
- expert_grad: float32 [128, 3, 128, 1024], P('dp', None, 'tensor')
- expert_left_new: float32 [128, 3, 4, 128, 64], P('dp', None, None, 'tensor')
- expert_right_new: float32 [128, 3, 8, 256, 256], P('dp', None, 'tensor')
- expert_new: float32 [128, 3, 128, 1024], P('dp', None, 'tensor')
The draws below stay inside these ranges and needn't reach their ends.
Inputs may be any that keep to these rules, and one draw needn't show every extreme that they name: `lengths`: at least one sequence is 1024 tokens long. `routes`: each row names 8 different experts. Among the rows of one sequence no expert is named more than 384 times, and in every draw some expert is named exactly 384 times in some sequence. `attention_left`: symmetric matrices. `attention_right`: symmetric matrices. `attention_left_root`: symmetric matrices. `attention_right_root`: symmetric matrices. `expert_left`: symmetric matrices. `expert_right`: symmetric matrices. `expert_left_root`: symmetric matrices. `expert_right_root`: symmetric matrices.
All inputs are finite; a program needn't handle non-finite values. No bound on the sum of `token_mask` on one device may be relied on, other than what follows from the above.
Results may differ from the reference program's by a relative error of at most 0.013.
Values may be sent and summed in bfloat16 or wider, within the bound.
No kernel may reach another device: no remote copies, remote signals or barrier semaphores. Data moves between devices by JAX's collectives and lax.ppermute only.
A program may use at most 832 MiB of HBM per device.

```python
import math
import jax
import jax.numpy as jnp
import numpy as np
from jax import lax

D = 1024
HEADS = 16
KV_HEADS = 8
HEAD_DIM = 64
EXPERTS = 32
TOPK = 8
FF = 512
LEN = 1024
BLK = 256
GROUPS = 4
BLOCK = 256
CAP = 384
UNITS = 128
SEQS = 16
TOKENS = 16384
ATTN_COLS = 1536
ATTN_BLOCKS = 6
N_DP = 16
N_TENSOR = 2


stat_decay = 0.9


def symmetric(key, shape):
    noise = jax.random.normal(key, shape, jnp.float32)
    return (noise + jnp.swapaxes(noise, -1, -2)) * 0.7071


def statistic(key, shape, columns):
    size = shape[-1]
    pieces = jax.random.split(key, 2)
    level = jax.random.uniform(pieces[0], shape[:-2] + (1, 1), jnp.float32, 1.0, 4.0)
    identity = jnp.eye(size, dtype=jnp.float32)
    amount = (1.0 - stat_decay) / stat_decay * columns / TOKENS
    return amount * (level * identity + 0.05 * symmetric(pieces[1], shape) / size ** 0.5)


def attention_statistic(key, shape, columns):
    size = shape[-1]
    pieces = jax.random.split(key, 3)
    level = jax.random.uniform(pieces[0], shape[:-2] + (1, 1), jnp.float32, 1.0, 4.0)
    spread = jnp.exp(jax.random.uniform(pieces[1], shape[:-1], jnp.float32, -0.6931, 0.6931))
    identity = jnp.eye(size, dtype=jnp.float32)
    strength = 64.0
    amount = (1.0 - stat_decay) / stat_decay * columns * strength / TOKENS
    return amount * level * (spread[..., None] * identity + 0.3 * symmetric(pieces[2], shape) / size ** 0.5)


def inverse_root(key, shape):
    size = shape[-1]
    pieces = jax.random.split(key, 2)
    diagonal = jax.random.uniform(pieces[0], shape[:-1], jnp.float32, 0.7, 1.3)
    identity = jnp.eye(size, dtype=jnp.float32)
    return TOKENS ** 0.25 * (diagonal[..., None] * identity + 0.25 * symmetric(pieces[1], shape) / size ** 0.5)


def draw_lengths(key, part):
    own_key = jax.random.fold_in(key, 11)
    index = jnp.arange(SEQS, dtype=jnp.int32)
    base = LEN // 4 + 3 * LEN // 4 * (index + 1) // SEQS
    jitter = jax.random.randint(own_key, (SEQS,), 0, LEN // 8 + 1, dtype=jnp.int32)
    return jnp.where(index == SEQS - 1, LEN, base - jitter).astype(jnp.int32)


def draw_attention_master(key, part):
    own_key = jax.random.fold_in(key, 12)
    noise = jax.random.normal(own_key, (D, N_TENSOR * ATTN_COLS), jnp.float32)
    column = jnp.arange(N_TENSOR * ATTN_COLS, dtype=jnp.int32) % ATTN_COLS
    inner_cols = (HEADS + 2 * KV_HEADS) * HEAD_DIM // N_TENSOR
    factor = jnp.where(column >= inner_cols, 4.0, 1.0)
    return noise * factor[None, :] * D ** (-0.5)


def draw_attention_left(key, part):
    return attention_statistic(jax.random.fold_in(key, 13), (N_DP, N_TENSOR * ATTN_BLOCKS, D // N_DP, D // N_DP), BLOCK)


def draw_attention_right(key, part):
    return attention_statistic(jax.random.fold_in(key, 14), (N_DP, N_TENSOR * ATTN_BLOCKS, BLOCK, BLOCK), D // N_DP)


def draw_attention_left_root(key, part):
    return inverse_root(jax.random.fold_in(key, 15), (N_DP, N_TENSOR * ATTN_BLOCKS, D // N_DP, D // N_DP))


def draw_attention_right_root(key, part):
    return inverse_root(jax.random.fold_in(key, 16), (N_DP, N_TENSOR * ATTN_BLOCKS, BLOCK, BLOCK))


def draw_expert_left(key, part):
    slice_rows = FF // (GROUPS * N_TENSOR)
    square = statistic(jax.random.fold_in(key, 17), (UNITS, 3, D // BLOCK, N_TENSOR, slice_rows, slice_rows), BLOCK)
    return square.reshape(UNITS, 3, D // BLOCK, N_TENSOR * slice_rows, slice_rows)


def draw_expert_right(key, part):
    return statistic(jax.random.fold_in(key, 18), (UNITS, 3, N_TENSOR * (D // BLOCK), BLOCK, BLOCK), FF // (GROUPS * N_TENSOR))


def draw_expert_left_root(key, part):
    slice_rows = FF // (GROUPS * N_TENSOR)
    square = inverse_root(jax.random.fold_in(key, 19), (UNITS, 3, D // BLOCK, N_TENSOR, slice_rows, slice_rows))
    return square.reshape(UNITS, 3, D // BLOCK, N_TENSOR * slice_rows, slice_rows)


def draw_expert_right_root(key, part):
    return inverse_root(jax.random.fold_in(key, 20), (UNITS, 3, N_TENSOR * (D // BLOCK), BLOCK, BLOCK))


def with_ends(drawn, key, low, high):
    extent = drawn.shape
    index_at = [jax.random.randint(jax.random.fold_in(key, axis), (), 0, extent[axis]) for axis in range(len(extent))]
    drawn = drawn.at[tuple(index_at)].set(low)
    longest = extent.index(max(extent))
    index_at[longest] = (index_at[longest] + 1) % extent[longest]
    return drawn.at[tuple(index_at)].set(high)


def block_scale(key, dims, cuts, least, high):
    factor_of = 1.0
    for dim, shards_of in cuts:
        draws = jax.random.uniform(jax.random.fold_in(jax.random.fold_in(key, 6), dim), (shards_of,), jnp.float32, least / len(cuts), high / len(cuts))
        factor_of = factor_of * jnp.repeat(jnp.exp(draws), dims[dim] // shards_of).reshape((-1,) + (1,) * (len(dims) - 1 - dim))
    return factor_of


def assign_block(stream_key, own, number, rows, number_of, top, reach, slope):
    sequence = jax.random.permutation(stream_key, number_of)
    heavy_load, usual = shares(number_of, rows * top, reach, slope, True), shares(number_of, rows * top, reach, slope, False)
    places = jnp.arange(number_of)

    def named(sizes, offset_by):
        used = int((sizes > 0).sum())
        fixed = max(1, used // 4)
        moved = fixed + (places - fixed + offset_by * (used - fixed)) % max(1, number_of - fixed)
        return jnp.zeros((number_of,), jnp.int32).at[sequence[jnp.where(places < fixed, places, moved)]].set(jnp.asarray(sizes, jnp.int32))

    sizes = jnp.where(number % 4 == 0, named(heavy_load, number // 4), named(usual, number - number // 4 - 1))
    mixed = jax.random.permutation(jax.random.fold_in(own, 3), number_of)
    source_of, receiver = mixed[0:number_of // 2 * 2:2], mixed[1:number_of // 2 * 2:2]
    room = jnp.minimum(sizes[source_of] - 1, reach - sizes[receiver]) // 2
    room = jnp.where((source_of == sequence[0]) | (receiver == sequence[0]) | (sizes[receiver] == 0), 0, jnp.maximum(room, 0))
    moved = jax.random.randint(jax.random.fold_in(own, 4), (number_of // 2,), 0, 1 << 20) % (room + 1)
    sizes = sizes.at[source_of].add(-moved).at[receiver].add(moved)
    items = jnp.searchsorted(jnp.cumsum(sizes), jnp.arange(rows * top), side="right").astype(jnp.int32)
    listing = items.reshape(top, rows).T
    listing = listing[jax.random.permutation(jax.random.fold_in(own, 1), rows)]
    offset_by = jax.random.randint(jax.random.fold_in(own, 2), (rows, 1), 0, top)
    return jnp.take_along_axis(listing, (jnp.arange(top)[None, :] + offset_by) % top, axis=1)


def shares(count, total, reach, slope, full):
    portions = [(1 << 20) // math.isqrt(standing ** slope) + 1 for standing in range(1, count + 1)]
    largest = reach if full else min(reach, max(-(-total // count), total * portions[0] // sum(portions)))
    least = 1 if total - largest >= count - 1 else 0
    holding, surplus = [largest] + [least] * (count - 1), total - largest - least * (count - 1)
    while surplus > 0:
        movable = [i for i in range(1, count) if holding[i] < largest] or [i for i in range(1, count) if holding[i] < reach]
        pool, remaining = sum([portions[i] for i in movable]), surplus
        for i in movable:
            extra = min(reach - holding[i], max(1, remaining * portions[i] // pool), surplus)
            holding[i] = holding[i] + extra
            surplus = surplus - extra
    return np.array(holding)


def scatter_about(key, extent, scale, limit, cuts=(), kind=jnp.bfloat16):
    entries = jax.random.normal(key, extent, jnp.float32) * scale
    if len(cuts) > 0:
        entries = block_scale(key, extent, cuts, -0.22, 0.18) * entries
    return jnp.clip(entries, min=-limit, max=limit).astype(kind)


def setup_inputs(seed: int = 0) -> dict:
    key_list = jax.random.split(jax.random.key(seed), 18)
    activations = scatter_about(key_list[0], (TOKENS, D), 1.0, 6.0, ((0, 32),))
    targets = scatter_about(key_list[1], (TOKENS, D), 1.0, 6.0, ((0, 32),), jnp.float32)
    lengths = draw_lengths(jax.random.fold_in(key_list[17], 71), 0)
    token_mask = with_ends((jax.random.randint(key_list[3], (TOKENS,), 0, 5) < 4).astype(jnp.int32), jax.random.fold_in(key_list[3], 1), 0, 1)
    routes_keys = jax.random.split(jax.random.fold_in(key_list[4], 1), TOKENS // LEN)
    routes_turns = jax.random.permutation(jax.random.fold_in(key_list[4], 3), TOKENS // LEN)
    routes = jax.vmap(lambda own, number: assign_block(jax.random.fold_in(key_list[4], 2), own, number, LEN, EXPERTS, TOPK, CAP, 1))(routes_keys, routes_turns).reshape((TOKENS, TOPK))
    route_weights = jnp.clip(0.3 + 0.59999996 * jax.random.uniform(key_list[5], (TOKENS, TOPK), jnp.float32) ** block_scale(key_list[5], (TOKENS, TOPK), ((0, 16),), -0.2, 0.2), 0.3, 0.9)
    norm_gains = jnp.clip(1.0 + 0.1 * jax.random.normal(key_list[6], (2, D), jnp.float32), 0.5, 1.5)
    attention_master = draw_attention_master(jax.random.fold_in(key_list[17], 71), 0)
    expert_master = scatter_about(key_list[8], (UNITS, 3, FF // GROUPS, D), D ** -0.5, 0.1875, ((0, 16), (2, 2)), jnp.float32)
    attention_left = draw_attention_left(jax.random.fold_in(key_list[17], 71), 0)
    attention_right = draw_attention_right(jax.random.fold_in(key_list[17], 71), 0)
    attention_left_root = draw_attention_left_root(jax.random.fold_in(key_list[17], 71), 0)
    attention_right_root = draw_attention_right_root(jax.random.fold_in(key_list[17], 71), 0)
    expert_left = draw_expert_left(jax.random.fold_in(key_list[17], 71), 0)
    expert_right = draw_expert_right(jax.random.fold_in(key_list[17], 71), 0)
    expert_left_root = draw_expert_left_root(jax.random.fold_in(key_list[17], 71), 0)
    expert_right_root = draw_expert_right_root(jax.random.fold_in(key_list[17], 71), 0)
    return dict(activations=activations, targets=targets, lengths=lengths, token_mask=token_mask, routes=routes, route_weights=route_weights, norm_gains=norm_gains, attention_master=attention_master, expert_master=expert_master, attention_left=attention_left, attention_right=attention_right, attention_left_root=attention_left_root, attention_right_root=attention_right_root, expert_left=expert_left, expert_right=expert_right, expert_left_root=expert_left_root, expert_right_root=expert_right_root)


@jax.custom_vjp
def low(v):
    return lax.optimization_barrier(v.astype(jnp.bfloat16)).astype(jnp.float32)

@jax.custom_vjp
def low_back(v):
    return v

def low_keep(v):
    return (low(v), None)

def low_pass(kept, grad):
    return (grad,)

def back_keep(v):
    return (v, None)

def back_low(kept, grad):
    return (low(grad),)
low.defvjp(low_keep, low_pass)
low_back.defvjp(back_keep, back_low)
epsilon = 1e-05
stat_decay = 0.9
gain_rate = 0.02
theta_base = 10000.0
masked_score = -1e+30
highest = lax.Precision.HIGHEST

def product(left_side, right_side):
    return jnp.dot(left_side, right_side, precision=highest, preferred_element_type=jnp.float32)

def rope_tables():
    half_width = HEAD_DIM // 2
    frequency = theta_base ** (-jnp.arange(half_width, dtype=jnp.float32) * 2.0 / HEAD_DIM)
    angles = jnp.arange(LEN, dtype=jnp.float32)[:, None] * frequency[None, :]
    return (jnp.cos(angles)[:, None, :], jnp.sin(angles)[:, None, :])

def rotate(values, cosine, sine):
    half_width = values.shape[-1] // 2
    first_half = values[..., :half_width]
    second_half = values[..., half_width:]
    return jnp.concatenate([first_half * cosine - second_half * sine, second_half * cosine + first_half * sine], axis=-1)

def normalize(hidden, gain):
    return hidden * lax.rsqrt(lax.optimization_barrier(jnp.mean(hidden * hidden, axis=-1, keepdims=True)) + epsilon) * gain

def layer_loss(hidden, norm_gains, attention_master, expert_master, targets, valid_rows, combine, lengths):
    cosine, sine = rope_tables()
    query_cols = HEADS * HEAD_DIM // N_TENSOR
    key_cols = KV_HEADS * HEAD_DIM // N_TENSOR
    group_size = HEADS // KV_HEADS
    score_scale = HEAD_DIM ** (-0.5)
    normed = low(normalize(hidden, norm_gains[0]))
    packed = low(attention_master).reshape(D, N_TENSOR, ATTN_COLS)
    w_query = packed[:, :, :query_cols].reshape(D, HEADS * HEAD_DIM)
    w_key = packed[:, :, query_cols:query_cols + key_cols].reshape(D, KV_HEADS * HEAD_DIM)
    w_value = packed[:, :, query_cols + key_cols:query_cols + 2 * key_cols].reshape(D, KV_HEADS * HEAD_DIM)
    w_output = packed[:, :, query_cols + 2 * key_cols:].reshape(D, HEADS * HEAD_DIM)
    position = jnp.arange(LEN, dtype=jnp.int32)
    block_visible = position[None, :] // BLK <= position[:, None] // BLK

    def attend(operands):
        seq_rows, seq_length = operands
        queries = low_back(product(seq_rows, w_query)).reshape(LEN, HEADS, HEAD_DIM)
        key_vectors = low_back(product(seq_rows, w_key)).reshape(LEN, KV_HEADS, HEAD_DIM)
        value_vectors = low(low_back(product(seq_rows, w_value))).reshape(LEN, KV_HEADS, HEAD_DIM)
        queries = low(rotate(queries, cosine, sine)).reshape(LEN, KV_HEADS, group_size, HEAD_DIM)
        key_vectors = low(rotate(key_vectors, cosine, sine))
        scores = jnp.einsum('qkgd,skd->kgqs', queries, key_vectors, precision=highest) * score_scale
        visible = block_visible & (position[None, :] < seq_length)
        scores = low_back(jnp.where(visible, scores, masked_score))
        weights = low(jax.nn.softmax(scores, axis=-1))
        attended = jnp.einsum('kgqs,skd->qkgd', weights, value_vectors, precision=highest)
        return low(low_back(attended.reshape(LEN, HEADS * HEAD_DIM)))
    attended = lax.map(jax.checkpoint(attend), (normed.reshape(SEQS, LEN, D), lengths))
    branch = low_back(product(attended.reshape(TOKENS, HEADS * HEAD_DIM), w_output.T))
    middle = hidden + branch
    normed_mix = low(normalize(middle, norm_gains[1]))
    experts = low(expert_master).reshape(EXPERTS, GROUPS, 3, FF // GROUPS, D)
    experts = experts.transpose(0, 2, 1, 3, 4).reshape(EXPERTS, 3, FF, D)

    def expert_block(operands):
        block_rows, block_weights = operands

        def one_expert(running, expert_operands):
            matrices, column = expert_operands
            gate_value = low_back(product(block_rows, matrices[0].T))
            upper_value = low_back(product(block_rows, matrices[1].T))
            inner_value = low(jax.nn.silu(gate_value) * upper_value)
            result = low_back(product(inner_value, matrices[2]))
            return (running + column[:, None] * result, None)
        mixed_block, _ = lax.scan(jax.checkpoint(one_expert), jnp.zeros(block_rows.shape, jnp.float32), (experts, block_weights.T))
        return mixed_block
    mixed_rows = lax.map(jax.checkpoint(expert_block), (normed_mix.reshape(SEQS, LEN, D), combine.reshape(SEQS, LEN, EXPERTS)))
    output = middle + low_back(mixed_rows.reshape(TOKENS, D))
    residual_error = output - targets
    mean_loss = jnp.sum(valid_rows[:, None] * residual_error * residual_error) / jnp.sum(valid_rows)
    return (mean_loss, output)

def reference(activations, targets, lengths, token_mask, routes, route_weights, norm_gains, attention_master, expert_master, attention_left, attention_right, attention_left_root, attention_right_root, expert_left, expert_right, expert_left_root, expert_right_root):
    token_index = jnp.arange(TOKENS, dtype=jnp.int32)
    sequence_of = token_index // LEN
    valid_rows = ((token_mask == 1) & (token_index % LEN < jnp.take(lengths, sequence_of))).astype(jnp.float32)
    expert_ids = jnp.arange(EXPERTS, dtype=jnp.int32)
    combine = lax.optimization_barrier(jnp.sum(jnp.where(routes[:, :, None] == expert_ids[None, None, :], route_weights[:, :, None], 0.0), axis=1))

    def closed_loss(hidden, gain_values, attention_values, expert_values):
        return layer_loss(hidden, gain_values, attention_values, expert_values, targets, valid_rows, combine, lengths)
    mean_loss, pullback, output = jax.vjp(closed_loss, activations.astype(jnp.float32), norm_gains, attention_master, expert_master, has_aux=True)
    input_grad, gain_grad, attention_grad, expert_grad = pullback(jnp.ones_like(mean_loss))
    gains_new = norm_gains - gain_rate * TOKENS ** 0.5 * gain_grad
    row_count = D // N_DP
    attention_blocks = attention_grad.reshape(N_DP, row_count, N_TENSOR * ATTN_BLOCKS, BLOCK).transpose(0, 2, 1, 3)
    attention_left_new = stat_decay * attention_left + jnp.einsum('nbik,nbjk->nbij', attention_blocks, attention_blocks, precision=highest)
    attention_right_new = stat_decay * attention_right + jnp.einsum('nbki,nbkj->nbij', attention_blocks, attention_blocks, precision=highest)
    attention_step = jnp.einsum('nbij,nbjk->nbik', attention_left_root, attention_blocks, precision=highest)
    attention_step = jnp.einsum('nbik,nbkl->nbil', attention_step, attention_right_root, precision=highest)
    attention_new = attention_master - D ** (-0.5) * attention_step.transpose(0, 2, 1, 3).reshape(D, N_TENSOR * ATTN_COLS)
    slice_rows = FF // (GROUPS * N_TENSOR)
    block_count = D // BLOCK
    expert_blocks = expert_grad.reshape(UNITS, 3, N_TENSOR, slice_rows, block_count, BLOCK).transpose(0, 1, 2, 4, 3, 5)
    left_old = expert_left.reshape(UNITS, 3, block_count, N_TENSOR, slice_rows, slice_rows).transpose(0, 1, 3, 2, 4, 5)
    left_root = expert_left_root.reshape(UNITS, 3, block_count, N_TENSOR, slice_rows, slice_rows).transpose(0, 1, 3, 2, 4, 5)
    right_old = expert_right.reshape(UNITS, 3, N_TENSOR, block_count, BLOCK, BLOCK)
    right_root = expert_right_root.reshape(UNITS, 3, N_TENSOR, block_count, BLOCK, BLOCK)
    left_new = stat_decay * left_old + jnp.einsum('...ik,...jk->...ij', expert_blocks, expert_blocks, precision=highest)
    right_new = stat_decay * right_old + jnp.einsum('...ki,...kj->...ij', expert_blocks, expert_blocks, precision=highest)
    expert_step = jnp.einsum('...ij,...jk->...ik', left_root, expert_blocks, precision=highest)
    expert_step = jnp.einsum('...ik,...kl->...il', expert_step, right_root, precision=highest)
    expert_new = expert_master - D ** (-0.5) * expert_step.transpose(0, 1, 2, 4, 3, 5).reshape(UNITS, 3, FF // GROUPS, D)
    expert_left_new = left_new.transpose(0, 1, 3, 2, 4, 5).reshape(UNITS, 3, block_count, FF // GROUPS, slice_rows)
    expert_right_new = right_new.reshape(UNITS, 3, N_TENSOR * block_count, BLOCK, BLOCK)
    return (output, mean_loss, input_grad, gain_grad, gains_new, attention_grad, attention_left_new, attention_right_new, attention_new, expert_grad, expert_left_new, expert_right_new, expert_new)
```

```python
import functools

import jax
import jax.numpy as jnp
from jax import lax
from jax.experimental import pallas as pl
from jax.experimental.pallas import tpu as pltpu
from jax.sharding import PartitionSpec as P

D = 1024
HEADS = 16
KV_HEADS = 8
HEAD_DIM = 64
EXPERTS = 32
TOPK = 8
BLK = 256
GROUPS = 4
BLOCK = 256
LANES = 128

epsilon = 1e-05
stat_decay = 0.9
gain_rate = 0.02
theta_base = 10000.0
masked_score = -1e30
MIB = 1 << 20

TOKEN_MASKS = (0, 1, 2, 3)
WEIGHT_BITS = (4, 8)


def dot(left, right, left_dim, right_dim):
    return lax.dot_general(
        left, right, (((left_dim,), (right_dim,)), ((), ())), preferred_element_type=jnp.float32
    )


def normalize(hidden, gain):
    scaling = lax.rsqrt(jnp.mean(hidden * hidden, axis=-1, keepdims=True) + epsilon)
    return (hidden * scaling * gain, scaling)


def normalize_back(hidden, scaling, gain, upstream):
    weighted = upstream * gain
    center = jnp.mean(weighted * hidden, axis=-1, keepdims=True)
    input_part = scaling * weighted - hidden * (scaling * scaling * scaling) * center
    return (input_part, jnp.sum(upstream * hidden * scaling, axis=0))


def swap_dp(values, mask):
    count = lax.axis_size("dp")
    return lax.ppermute(values, "dp", [(i, i ^ mask) for i in range(count)])


def swap_core(values):
    count = lax.axis_size("tensor")
    return lax.ppermute(values, "tensor", [(i, i ^ 1) for i in range(count)])


def sum_everywhere(values):
    values = values + swap_core(values)
    mask = 1
    while mask < lax.axis_size("dp"):
        values = values + swap_dp(values, mask)
        mask *= 2
    return values


def in_order(own, other):
    first = lax.axis_index("tensor") == 0
    return jnp.concatenate([jnp.where(first, own, other), jnp.where(first, other, own)], axis=0)


def own_half(values):
    half = values.shape[0] // 2
    return lax.dynamic_slice_in_dim(values, lax.axis_index("tensor") * half, half, 0)


def other_half(values):
    half = values.shape[0] // 2
    return lax.dynamic_slice_in_dim(values, (1 - lax.axis_index("tensor")) * half, half, 0)


def turn(values):
    lane = lax.broadcasted_iota(jnp.int32, values.shape, 1)
    half = HEAD_DIM // 2
    return jnp.where(
        lane % HEAD_DIM < half,
        -pltpu.roll(values, LANES - half, 1),
        pltpu.roll(values, half, 1),
    )


def attention_forward_kernel(
    length_ref, x_ref, w_ref, cos_ref, sin_ref, q_ref, k_ref, v_ref, att_ref, lse_ref
):
    rows = x_ref.shape[0]
    low = jnp.bfloat16
    cosine, sine = cos_ref[...], sin_ref[...]
    lane = lax.broadcasted_iota(jnp.int32, (rows, LANES), 1)
    left = lane < HEAD_DIM
    projected = dot(x_ref[...], w_ref[...], 1, 0)
    q_raw = projected[:, :LANES]
    q_turn = turn(q_raw)
    scale = HEAD_DIM ** (-0.5)
    q_rot = (q_raw * cosine + q_turn * sine) * scale
    q_rot_turn = (q_turn * cosine - q_raw * sine) * scale
    q_ref[:, :LANES] = jnp.where(left, q_rot, pltpu.roll(q_rot_turn, HEAD_DIM, 1)).astype(low)
    q_ref[:, LANES:] = jnp.where(left, pltpu.roll(q_rot, HEAD_DIM, 1), q_rot_turn).astype(low)
    kv_raw = projected[:, LANES:]
    k_turn = turn(kv_raw)
    k_rot = kv_raw * cosine + k_turn * sine
    k_rot_turn = k_turn * cosine - kv_raw * sine
    k_ref[...] = jnp.where(left, k_rot, pltpu.roll(k_rot_turn, HEAD_DIM, 1)).astype(low)
    v_high = jnp.where(left, 0.0, kv_raw)
    v_ref[...] = v_high.astype(low)
    v_low = pltpu.roll(v_high, HEAD_DIM, 1).astype(low)
    v_high = v_high.astype(low)
    k_only = jnp.where(left, k_rot, 0.0).astype(low)
    place = lax.broadcasted_iota(jnp.int32, (1, rows), 1)
    bias = jnp.where(place < length_ref[0], 0.0, masked_score)
    for block in range(rows // BLK):
        here = pl.ds(block * BLK, BLK)
        keys = (block + 1) * BLK
        total = None
        for head in range(2):
            q_block = q_ref[here, head * LANES : (head + 1) * LANES]
            scores = dot(q_block, k_only[:keys], 1, 1) + bias[:, :keys]
            top = jnp.max(scores, axis=1, keepdims=True)
            exponent = jnp.exp(scores - top)
            denominator = jnp.sum(exponent, axis=1, keepdims=True)
            weights = (exponent * (1.0 / denominator)).astype(low)
            value = v_high if head else v_low
            part = dot(weights, value[:keys], 1, 0)
            total = part if total is None else total + part
            log_total = jnp.broadcast_to(top + jnp.log(denominator), (BLK, LANES))
            lse_ref[head * 8 : (head + 1) * 8, here] = log_total.T[:8]
        att_ref[here, :] = total.astype(low)


def attention_backward_kernel(
    length_ref,
    branch_ref,
    wo_ref,
    q_ref,
    k_ref,
    v_ref,
    lse_ref,
    cos_ref,
    sin_ref,
    dq_ref,
    dkv_ref,
    dk_sum,
    d0_sum,
    d1_sum,
):
    rows = branch_ref.shape[0]
    low = jnp.bfloat16
    lane = lax.broadcasted_iota(jnp.int32, (rows, LANES), 1)
    left = lane < HEAD_DIM
    grad = dot(branch_ref[...], wo_ref[...], 1, 0).astype(low)
    k_only = jnp.where(left, k_ref[...].astype(jnp.float32), 0.0).astype(low)
    v_high = v_ref[...]
    v_low = pltpu.roll(v_high.astype(jnp.float32), HEAD_DIM, 1).astype(low)
    place = lax.broadcasted_iota(jnp.int32, (rows, BLK), 0)
    seen = place < length_ref[0]
    dk_sum[...] = jnp.zeros_like(dk_sum)
    d0_sum[...] = jnp.zeros_like(d0_sum)
    d1_sum[...] = jnp.zeros_like(d1_sum)
    scale = HEAD_DIM ** (-0.5)
    for block in range(rows // BLK):
        here = pl.ds(block * BLK, BLK)
        keys = (block + 1) * BLK
        grad_block = grad[block * BLK : keys]
        query_grads = []
        for head in range(2):
            q_block = q_ref[here, head * LANES : (head + 1) * LANES]
            value = v_high if head else v_low
            scores = dot(k_only[:keys], q_block, 1, 1)
            log_total = lse_ref[head * 8 : head * 8 + 1, here]
            scores = jnp.where(seen[:keys], scores, masked_score)
            probability = jnp.exp(scores - log_total)
            prob_grad = dot(value[:keys], grad_block, 1, 1)
            weighted = probability * prob_grad
            center = jnp.sum(weighted, axis=0, keepdims=True)
            score_grad = (weighted - probability * center).astype(low)
            d_sum = d1_sum if head else d0_sum
            d_sum[:keys] += dot(probability.astype(low), grad_block, 1, 0)
            dk_sum[:keys] += dot(score_grad, q_block, 1, 0)
            query_grads.append(dot(score_grad, k_ref[:keys], 0, 0))
        cosine, sine = cos_ref[here, :] * scale, sin_ref[here, :] * scale
        zero, one = query_grads
        left_here = left[:BLK]
        straight = jnp.where(left_here, zero, pltpu.roll(one, HEAD_DIM, 1))
        turned = jnp.where(left_here, pltpu.roll(zero, HEAD_DIM, 1), one)
        dq_ref[here, :] = (straight * cosine - turned * sine).astype(low)
    dk_all = dk_sum[...]
    dk_rot = dk_all * cos_ref[...] - pltpu.roll(dk_all, HEAD_DIM, 1) * sin_ref[...]
    dv_all = pltpu.roll(d0_sum[...], HEAD_DIM, 1) + d1_sum[...]
    dkv_ref[...] = jnp.where(left, dk_rot, dv_all).astype(low)


def whole(shape):
    return pl.BlockSpec(shape, lambda h: (0,) * len(shape))


def columns(rows, width):
    return pl.BlockSpec((rows, width), lambda h: (0, h))


def attention_forward(length, normed, w_qkv, cosine, sine):
    rows = normed.shape[0]
    kv_here = w_qkv.shape[1] // 256
    low = jnp.bfloat16
    return pl.pallas_call(
        attention_forward_kernel,
        grid=(kv_here,),
        in_specs=[
            pl.BlockSpec(memory_space=pltpu.SMEM),
            whole((rows, D)),
            columns(D, 256),
            whole((rows, LANES)),
            whole((rows, LANES)),
        ],
        out_specs=[
            columns(rows, 256),
            columns(rows, LANES),
            columns(rows, LANES),
            columns(rows, LANES),
            pl.BlockSpec((16, rows), lambda h: (h, 0)),
        ],
        out_shape=[
            jax.ShapeDtypeStruct((rows, kv_here * 256), low),
            jax.ShapeDtypeStruct((rows, kv_here * LANES), low),
            jax.ShapeDtypeStruct((rows, kv_here * LANES), low),
            jax.ShapeDtypeStruct((rows, kv_here * LANES), low),
            jax.ShapeDtypeStruct((kv_here * 16, rows), jnp.float32),
        ],
        compiler_params=pltpu.CompilerParams(vmem_limit_bytes=50 * MIB),
        cost_estimate=pl.CostEstimate(
            flops=8_000_000_000, bytes_accessed=12_000_000, transcendentals=5_000_000
        ),
        name="attention_forward",
    )(length, normed, w_qkv, cosine, sine)


def attention_backward(length, branch_low, w_output, q2, k2, v, lse, cosine, sine):
    rows = branch_low.shape[0]
    kv_here = k2.shape[1] // LANES
    low = jnp.bfloat16
    return pl.pallas_call(
        attention_backward_kernel,
        grid=(kv_here,),
        in_specs=[
            pl.BlockSpec(memory_space=pltpu.SMEM),
            whole((rows, D)),
            columns(D, LANES),
            columns(rows, 256),
            columns(rows, LANES),
            columns(rows, LANES),
            pl.BlockSpec((16, rows), lambda h: (h, 0)),
            whole((rows, LANES)),
            whole((rows, LANES)),
        ],
        out_specs=[columns(rows, LANES), columns(rows, LANES)],
        out_shape=[
            jax.ShapeDtypeStruct((rows, kv_here * LANES), low),
            jax.ShapeDtypeStruct((rows, kv_here * LANES), low),
        ],
        scratch_shapes=[pltpu.VMEM((rows, LANES), jnp.float32)] * 3,
        compiler_params=pltpu.CompilerParams(vmem_limit_bytes=50 * MIB),
        cost_estimate=pl.CostEstimate(
            flops=20_000_000_000, bytes_accessed=12_000_000, transcendentals=5_000_000
        ),
        name="attention_backward",
    )(length, branch_low, w_output, q2, k2, v, lse, cosine, sine)


CHUNK = 256
TILE = 512


def chunk_weights(shard_refs, chunk, kind):
    units = shard_refs[0].shape[0]
    per_shard = units // 4
    ref = shard_refs[chunk // per_shard]
    start = (chunk % per_shard) * 4
    return ref[start : start + 4, kind].reshape(CHUNK, D)


def spread_weights(route_ref, chunk, per_chunk):
    if per_chunk == 1:
        return route_ref[:, chunk : chunk + 1]
    rows = route_ref.shape[0]
    pieces = [
        jnp.broadcast_to(route_ref[:, chunk * 4 + j : chunk * 4 + j + 1], (rows, CHUNK // 4))
        for j in range(4)
    ]
    return jnp.concatenate(pieces, axis=1)


def expert_forward_kernel(
    chunks, per_chunk, x_ref, route_ref, s0, s1, s2, s3, mixed_ref, slope_ref, silu_ref, inner_ref
):
    shards = (s0, s1, s2, s3)
    low = jnp.bfloat16
    x = x_ref[...]
    total = None
    for chunk in range(chunks):
        here = slice(chunk * CHUNK, (chunk + 1) * CHUNK)
        gate = dot(x, chunk_weights(shards, chunk, 0), 1, 1)
        upper = dot(x, chunk_weights(shards, chunk, 1), 1, 1)
        weight = spread_weights(route_ref, chunk, per_chunk)
        sigmoid = 0.5 * jnp.tanh(0.5 * gate) + 0.5
        silu = gate * sigmoid
        weighted_upper = weight * upper
        slope_ref[:, here] = (weighted_upper * (sigmoid + silu * (1.0 - sigmoid))).astype(low)
        silu_ref[:, here] = (weight * silu).astype(low)
        inner = (silu * weighted_upper).astype(low)
        inner_ref[:, here] = inner
        part = dot(inner, chunk_weights(shards, chunk, 2), 1, 0)
        total = part if total is None else total + part
    mixed_ref[...] = total.astype(low)


def expert_backward_kernel(
    chunks, grad_ref, slope_ref, silu_ref, s0, s1, s2, s3, input_ref, gate_ref, upper_ref
):
    shards = (s0, s1, s2, s3)
    low = jnp.bfloat16
    grad = grad_ref[...]
    total = None
    for chunk in range(chunks):
        here = slice(chunk * CHUNK, (chunk + 1) * CHUNK)
        inner_grad = dot(grad, chunk_weights(shards, chunk, 2), 1, 1)
        gate_grad = (inner_grad * slope_ref[:, here].astype(jnp.float32)).astype(low)
        upper_grad = (inner_grad * silu_ref[:, here].astype(jnp.float32)).astype(low)
        gate_ref[:, here] = gate_grad
        upper_ref[:, here] = upper_grad
        part = dot(gate_grad, chunk_weights(shards, chunk, 0), 1, 0)
        part = part + dot(upper_grad, chunk_weights(shards, chunk, 1), 1, 0)
        total = part if total is None else total + part
    input_ref[...] = total.astype(low)


def token_rows(width):
    return pl.BlockSpec((TILE, width), lambda i: (i, 0))


def shard_spec(shard):
    return pl.BlockSpec(shard.shape, lambda i: (0, 0, 0, 0), pipeline_mode=pl.Buffered(1))


def expert_forward(x, route_columns, shards):
    rows = x.shape[0]
    hidden_width = sum(s.shape[0] * s.shape[2] for s in shards)
    chunks = hidden_width // CHUNK
    per_chunk = route_columns.shape[1] // chunks
    low = jnp.bfloat16
    wide = jax.ShapeDtypeStruct((rows, hidden_width), low)
    return pl.pallas_call(
        functools.partial(expert_forward_kernel, chunks, per_chunk),
        grid=(rows // TILE,),
        in_specs=[token_rows(D), token_rows(route_columns.shape[1])]
        + [shard_spec(s) for s in shards],
        out_specs=[token_rows(D)] + [token_rows(hidden_width)] * 3,
        out_shape=[jax.ShapeDtypeStruct((rows, D), low), wide, wide, wide],
        compiler_params=pltpu.CompilerParams(vmem_limit_bytes=58 * MIB),
        cost_estimate=pl.CostEstimate(
            flops=6 * rows * hidden_width * D,
            bytes_accessed=80_000_000,
            transcendentals=rows * hidden_width,
        ),
        name="expert_forward",
    )(x, route_columns, *shards)


def expert_backward(grad, slope, silu, shards):
    rows, hidden_width = slope.shape
    low = jnp.bfloat16
    wide = jax.ShapeDtypeStruct((rows, hidden_width), low)
    return pl.pallas_call(
        functools.partial(expert_backward_kernel, hidden_width // CHUNK),
        grid=(rows // TILE,),
        in_specs=[token_rows(D), token_rows(hidden_width), token_rows(hidden_width)]
        + [shard_spec(s) for s in shards],
        out_specs=[token_rows(D)] + [token_rows(hidden_width)] * 2,
        out_shape=[jax.ShapeDtypeStruct((rows, D), low), wide, wide],
        compiler_params=pltpu.CompilerParams(vmem_limit_bytes=58 * MIB),
        cost_estimate=pl.CostEstimate(
            flops=6 * rows * hidden_width * D, bytes_accessed=100_000_000, transcendentals=0
        ),
        name="expert_backward",
    )(grad, slope, silu, *shards)


def spread_tokens(own):
    parts = jnp.stack([own] + [swap_dp(own, mask) for mask in TOKEN_MASKS[1:]])
    return jnp.concatenate([parts, swap_core(parts)], axis=0).reshape(-1, own.shape[-1])


def collect_tokens(partial, own_rows):
    partial = partial.reshape(2, len(TOKEN_MASKS), own_rows, -1)
    mine = partial[0].astype(jnp.float32) + swap_core(partial[1]).astype(jnp.float32)
    total = mine[0]
    for place, mask in enumerate(TOKEN_MASKS[1:], 1):
        total = total + swap_dp(mine[place].astype(jnp.bfloat16), mask).astype(jnp.float32)
    return total


def extra_masks():
    count = lax.axis_size("dp")
    used = sum(WEIGHT_BITS) + TOKEN_MASKS[-1]
    masks = []
    mask = 1
    while mask < count:
        if not mask & used:
            masks.append(mask)
        mask *= 2
    return masks


def gather_weights(own):
    for mask in extra_masks():
        own = jnp.concatenate([own, swap_dp(own, mask)], axis=0)
    first, second = WEIGHT_BITS
    far = swap_dp(own, second)
    return [own, swap_dp(own, first), far, swap_dp(far, first)]


def unit_owners():
    masks = [0]
    for mask in extra_masks():
        masks = masks + [m ^ mask for m in masks]
    first, second = WEIGHT_BITS
    masks = [m ^ k for k in (0, first, second, first ^ second) for m in masks]
    return lax.axis_index("dp") ^ jnp.array(masks, jnp.int32)


def scatter_grads(parts):
    first, second = WEIGHT_BITS
    far = parts[2] + swap_dp(parts[3].astype(jnp.bfloat16), first).astype(jnp.float32)
    near = parts[0] + swap_dp(parts[1].astype(jnp.bfloat16), first).astype(jnp.float32)
    total = near + swap_dp(far.astype(jnp.bfloat16), second).astype(jnp.float32)
    for mask in reversed(extra_masks()):
        half = total.shape[0] // 2
        total = total[:half] + swap_dp(total[half:].astype(jnp.bfloat16), mask).astype(jnp.float32)
    return total


def on_device(
    activations,
    targets,
    lengths,
    token_mask,
    routes,
    route_weights,
    norm_gains,
    attention_master,
    expert_master,
    attention_left,
    attention_right,
    attention_left_root,
    attention_right_root,
    expert_left,
    expert_right,
    expert_left_root,
    expert_right_root,
):
    low = jnp.bfloat16
    own_rows = activations.shape[0]
    tensor_size = lax.axis_size("tensor")
    core = lax.axis_index("tensor")
    tokens_total = own_rows * tensor_size * lax.axis_size("dp")
    seq_length = lengths[0]
    position = core * own_rows + jnp.arange(own_rows, dtype=jnp.int32)
    valid_rows = ((token_mask == 1) & (position < seq_length)).astype(jnp.float32)
    valid_total = sum_everywhere(jnp.sum(valid_rows).reshape(1, 1))[0, 0]

    heads_here = HEADS // tensor_size
    kv_here = KV_HEADS // tensor_size
    query_cols = heads_here * HEAD_DIM
    key_cols = kv_here * HEAD_DIM
    qkv_cols = query_cols + 2 * key_cols
    rows_here = attention_master.shape[0]

    def by_head(values):
        rows = values.shape[0]
        query = values[:, :query_cols].reshape(rows, kv_here, LANES)
        key = values[:, query_cols : query_cols + key_cols].reshape(rows, kv_here, HEAD_DIM)
        value = values[:, query_cols + key_cols : qkv_cols].reshape(rows, kv_here, HEAD_DIM)
        return jnp.concatenate([query, key, value], axis=2).reshape(rows, qkv_cols)

    def from_heads(values):
        rows = values.shape[0]
        values = values.reshape(rows, kv_here, 256)
        return jnp.concatenate(
            [
                values[:, :, :LANES].reshape(rows, query_cols),
                values[:, :, LANES : LANES + HEAD_DIM].reshape(rows, key_cols),
                values[:, :, LANES + HEAD_DIM :].reshape(rows, key_cols),
            ],
            axis=1,
        )

    attention_low = attention_master.astype(low)
    w_qkv = lax.all_gather(by_head(attention_low), "dp", axis=0, tiled=True)
    w_output = lax.all_gather(attention_low[:, qkv_cols:], "dp", axis=0, tiled=True)
    hidden = activations.astype(jnp.float32)
    normed_own, attention_scaling = normalize(hidden, norm_gains[0])
    normed_own = normed_own.astype(low)
    normed = in_order(normed_own, swap_core(normed_own))

    shards = gather_weights(expert_master.astype(low))

    seq_rows = normed.shape[0]
    half_width = HEAD_DIM // 2
    frequency = theta_base ** (-jnp.arange(half_width, dtype=jnp.float32) * 2.0 / HEAD_DIM)
    angles = jnp.arange(seq_rows, dtype=jnp.float32)[:, None] * frequency[None, :]
    cosine = jnp.tile(jnp.cos(angles), (1, LANES // half_width))
    sine = jnp.tile(jnp.sin(angles), (1, LANES // half_width))
    q2, k2, v_high, attended, log_totals = attention_forward(
        lengths, normed, w_qkv, cosine, sine
    )
    branch = dot(attended, w_output, 1, 1)
    branch = own_half(branch) + swap_core(other_half(branch).astype(low)).astype(jnp.float32)
    middle = hidden + branch
    mix_own, mix_scaling = normalize(middle, norm_gains[1])
    mix = spread_tokens(mix_own.astype(low))

    routing = jnp.concatenate([routes.astype(jnp.float32), route_weights], axis=1)
    routing = jnp.stack([routing] + [swap_dp(routing, mask) for mask in TOKEN_MASKS[1:]])
    routing = routing.reshape(len(TOKEN_MASKS), 2, own_rows, 2 * TOPK)
    routing = jnp.concatenate(
        [
            lax.dynamic_index_in_dim(routing, core, 1, keepdims=False),
            lax.dynamic_index_in_dim(routing, 1 - core, 1, keepdims=False),
        ],
        axis=0,
    ).reshape(-1, 2 * TOPK)
    unit_here = expert_master.shape[0]
    slice_rows = expert_master.shape[2]
    unit_ids = (unit_owners()[:, None] * unit_here + jnp.arange(unit_here)[None, :]).reshape(-1)
    expert_of = unit_ids // GROUPS
    if unit_here % 4 == 0:
        expert_of = expert_of[::4]
    named = routing[:, None, :TOPK] == expert_of.astype(jnp.float32)[None, :, None]
    route_columns = jnp.sum(jnp.where(named, routing[:, None, TOPK:], 0.0), axis=2)

    mixed, slope, silu, inner = expert_forward(mix, route_columns, shards)
    output = middle + collect_tokens(mixed, own_rows)
    residual_error = output - targets
    loss_part = jnp.sum(valid_rows[:, None] * residual_error * residual_error)
    output_grad = 2.0 / valid_total * valid_rows[:, None] * residual_error
    output_low = spread_tokens(output_grad.astype(low))
    mix_part, gate_grad, upper_grad = expert_backward(output_low, slope, silu, shards)
    shard_units = shards[0].shape[0]

    def weight_grad(left, right):
        full = dot(left, right, 0, 0).reshape(4, shard_units, slice_rows, D)
        return scatter_grads([full[k] for k in range(4)])

    down_grad = weight_grad(inner, output_low)
    gate_weight_grad = weight_grad(gate_grad, mix)
    upper_weight_grad = weight_grad(upper_grad, mix)
    expert_grad = jnp.stack([gate_weight_grad, upper_weight_grad, down_grad], axis=1)

    mix_back, gain_mix = normalize_back(
        middle, mix_scaling, norm_gains[1], collect_tokens(mix_part, own_rows)
    )
    middle_grad = output_grad + mix_back
    branch_own = middle_grad.astype(low)
    branch_low = in_order(branch_own, swap_core(branch_own))
    dq, dkv = attention_backward(
        lengths, branch_low, w_output, q2, k2, v_high, log_totals, cosine, sine
    )
    qkv_grad = jnp.concatenate(
        [dq.reshape(seq_rows, kv_here, LANES), dkv.reshape(seq_rows, kv_here, LANES)], axis=2
    ).reshape(seq_rows, qkv_cols)
    normed_grad = dot(qkv_grad, w_qkv, 1, 1)
    normed_grad = own_half(normed_grad) + swap_core(
        other_half(normed_grad).astype(low)
    ).astype(jnp.float32)
    attention_back, gain_attention = normalize_back(
        hidden, attention_scaling, norm_gains[0], normed_grad
    )
    input_grad = middle_grad + attention_back
    qkv_part = dot(normed, qkv_grad, 0, 0).astype(low)
    output_part = dot(branch_low, attended, 0, 0).astype(low)
    qkv_part = lax.psum_scatter(qkv_part, "dp", scatter_dimension=0, tiled=True)
    output_part = lax.psum_scatter(output_part, "dp", scatter_dimension=0, tiled=True)
    attention_grad = jnp.concatenate([from_heads(qkv_part), output_part], axis=1).astype(
        jnp.float32
    )

    loss_row = jnp.full((1, D), loss_part)
    sums = sum_everywhere(jnp.concatenate([gain_attention[None], gain_mix[None], loss_row], axis=0))
    gain_grad = sums[:2]
    mean_loss = sums[2, 0] / valid_total
    gains_new = norm_gains - gain_rate * tokens_total**0.5 * gain_grad

    attention_blocks = attention_grad.reshape(rows_here, -1, BLOCK).transpose(1, 0, 2)
    attention_left_new = stat_decay * attention_left[0] + jnp.einsum(
        "bik,bjk->bij", attention_blocks, attention_blocks
    )
    attention_right_new = stat_decay * attention_right[0] + jnp.einsum(
        "bki,bkj->bij", attention_blocks, attention_blocks
    )
    attention_step = jnp.einsum("bij,bjk->bik", attention_left_root[0], attention_blocks)
    attention_step = jnp.einsum("bik,bkl->bil", attention_step, attention_right_root[0])
    attention_new = attention_master - D ** (-0.5) * attention_step.transpose(1, 0, 2).reshape(
        rows_here, -1
    )
    block_count = D // BLOCK
    expert_blocks = expert_grad.reshape(unit_here, 3, slice_rows, block_count, BLOCK).transpose(
        0, 1, 3, 2, 4
    )
    expert_left_new = stat_decay * expert_left + jnp.einsum(
        "...ik,...jk->...ij", expert_blocks, expert_blocks
    )
    expert_right_new = stat_decay * expert_right + jnp.einsum(
        "...ki,...kj->...ij", expert_blocks, expert_blocks
    )
    expert_step = jnp.einsum("...ij,...jk->...ik", expert_left_root, expert_blocks)
    expert_step = jnp.einsum("...ik,...kl->...il", expert_step, expert_right_root)
    expert_new = expert_master - D ** (-0.5) * expert_step.transpose(0, 1, 3, 2, 4).reshape(
        expert_master.shape
    )
    return (
        output,
        mean_loss,
        input_grad,
        gain_grad,
        gains_new,
        attention_grad,
        attention_left_new[None],
        attention_right_new[None],
        attention_new,
        expert_grad,
        expert_left_new,
        expert_right_new,
        expert_new,
    )


def solution(mesh):
    return jax.shard_map(
        on_device,
        mesh=mesh,
        in_specs=(
            P(("dp", "tensor"), None),
            P(("dp", "tensor"), None),
            P("dp"),
            P(("dp", "tensor")),
            P("dp", None),
            P("dp", None),
            P(),
            P("dp", "tensor"),
            P("dp", None, "tensor", None),
            P("dp", "tensor", None, None),
            P("dp", "tensor", None, None),
            P("dp", "tensor", None, None),
            P("dp", "tensor", None, None),
            P("dp", None, None, "tensor", None),
            P("dp", None, "tensor", None, None),
            P("dp", None, None, "tensor", None),
            P("dp", None, "tensor", None, None),
        ),
        out_specs=(
            P(("dp", "tensor"), None),
            P(),
            P(("dp", "tensor"), None),
            P(),
            P(),
            P("dp", "tensor"),
            P("dp", "tensor", None, None),
            P("dp", "tensor", None, None),
            P("dp", "tensor"),
            P("dp", None, "tensor", None),
            P("dp", None, None, "tensor", None),
            P("dp", None, "tensor", None, None),
            P("dp", None, "tensor", None),
        ),
        check_vma=False,
    )
```

```python
import functools

import jax
import jax.numpy as jnp
from jax import lax
from jax.experimental import pallas as pl
from jax.experimental.pallas import tpu as pltpu
from jax.sharding import PartitionSpec as P

D = 1024
HEADS = 16
KV_HEADS = 8
HEAD_DIM = 64
EXPERTS = 32
TOPK = 8
BLK = 256
GROUPS = 4
BLOCK = 256
LANES = 128

epsilon = 1e-05
stat_decay = 0.9
gain_rate = 0.02
theta_base = 10000.0
masked_score = -1e30
MIB = 1 << 20
SMALL = pl.CostEstimate(flops=1000, bytes_accessed=1000, transcendentals=0)


def cost(flops):
    return pl.CostEstimate(flops=int(flops), bytes_accessed=1000, transcendentals=0)


ANYWHERE = pl.BlockSpec(memory_space=pl.ANY)
SCALARS = pl.BlockSpec(memory_space=pltpu.SMEM)

TOKEN_MASKS = (0, 1, 4, 5)
WEIGHT_BITS = (2, 8)


def dot(left, right, left_dim, right_dim):
    return lax.dot_general(
        left, right, (((left_dim,), (right_dim,)), ((), ())), preferred_element_type=jnp.float32
    )


def normalize(hidden, gain):
    scaling = lax.rsqrt(jnp.mean(hidden * hidden, axis=-1, keepdims=True) + epsilon)
    return (hidden * scaling * gain, scaling)


def normalize_back(hidden, scaling, gain, upstream):
    weighted = upstream * gain
    center = jnp.mean(weighted * hidden, axis=-1, keepdims=True)
    input_part = scaling * weighted - hidden * (scaling * scaling * scaling) * center
    return (input_part, jnp.sum(upstream * hidden * scaling, axis=0))


def swap_dp(values, mask):
    count = lax.axis_size("dp")
    return lax.ppermute(values, "dp", [(i, i ^ mask) for i in range(count)])


def swap_core(values):
    count = lax.axis_size("tensor")
    return lax.ppermute(values, "tensor", [(i, i ^ 1) for i in range(count)])


def sum_everywhere(values):
    values = values + swap_core(values)
    own = sum(values if mask == 0 else swap_dp(values, mask) for mask in TOKEN_MASKS)
    masks = [m for m in range(1, lax.axis_size("dp")) if not m & TOKEN_MASKS[-1]]
    return own + sum(swap_dp(own, mask) for mask in masks)


def in_order(own, other):
    first = lax.axis_index("tensor") == 0
    return jnp.concatenate([jnp.where(first, own, other), jnp.where(first, other, own)], axis=0)


def own_half(values):
    half = values.shape[0] // 2
    return lax.dynamic_slice_in_dim(values, lax.axis_index("tensor") * half, half, 0)


def other_half(values):
    half = values.shape[0] // 2
    return lax.dynamic_slice_in_dim(values, (1 - lax.axis_index("tensor")) * half, half, 0)


def turn(values):
    lane = lax.broadcasted_iota(jnp.int32, values.shape, 1)
    half = HEAD_DIM // 2
    return jnp.where(
        lane % HEAD_DIM < half,
        -pltpu.roll(values, LANES - half, 1),
        pltpu.roll(values, half, 1),
    )


def place_rows(starts_ref, source_refs, target_ref):
    for group, source_ref in enumerate(source_refs):
        count = starts_ref.shape[1]
        slot_rows = source_ref.shape[0] // count
        rows = target_ref.shape[0] // count // len(source_refs)
        for slot in range(count):
            start = pl.multiple_of(starts_ref[group, slot], rows)
            begin = slot * slot_rows
            target_ref[pl.ds(start, rows), :] = source_ref[begin : begin + rows, :]


def attention_forward_kernel(*refs):
    length_ref, starts_ref, x_ref, w0_ref, w1_ref, w2_ref, w3_ref, cos_ref, sin_ref = refs[:9]
    q_ref, k_ref, v_ref, att_ref, w_ref, lse_ref = refs[-6:]
    rows = x_ref.shape[0]
    place_rows(starts_ref, (w0_ref, w1_ref, w2_ref, w3_ref), w_ref)
    low = jnp.bfloat16
    cosine, sine = cos_ref[...], sin_ref[...]
    lane = lax.broadcasted_iota(jnp.int32, (rows, LANES), 1)
    left = lane < HEAD_DIM
    projected = dot(x_ref[...], w_ref[...], 1, 0)
    q_raw = projected[:, :LANES]
    q_turn = turn(q_raw)
    scale = HEAD_DIM ** (-0.5)
    q_rot = (q_raw * cosine + q_turn * sine) * scale
    q_rot_turn = (q_turn * cosine - q_raw * sine) * scale
    q_ref[:, :LANES] = jnp.where(left, q_rot, pltpu.roll(q_rot_turn, HEAD_DIM, 1)).astype(low)
    q_ref[:, LANES:] = jnp.where(left, pltpu.roll(q_rot, HEAD_DIM, 1), q_rot_turn).astype(low)
    kv_raw = projected[:, LANES:]
    k_turn = turn(kv_raw)
    k_rot = kv_raw * cosine + k_turn * sine
    k_rot_turn = k_turn * cosine - kv_raw * sine
    k_ref[...] = jnp.where(left, k_rot, pltpu.roll(k_rot_turn, HEAD_DIM, 1)).astype(low)
    v_high = jnp.where(left, 0.0, kv_raw)
    v_ref[...] = v_high.astype(low)
    v_low = pltpu.roll(v_high, HEAD_DIM, 1).astype(low)
    v_high = v_high.astype(low)
    k_only = jnp.where(left, k_rot, 0.0).astype(low)
    place = lax.broadcasted_iota(jnp.int32, (1, rows), 1)
    bias = jnp.where(place < length_ref[0], 0.0, masked_score)
    for block in range(rows // BLK):
        here = pl.ds(block * BLK, BLK)
        keys = (block + 1) * BLK
        total = None
        for head in range(2):
            q_block = q_ref[here, head * LANES : (head + 1) * LANES]
            scores = dot(q_block, k_only[:keys], 1, 1) + bias[:, :keys]
            top = jnp.max(scores, axis=1, keepdims=True)
            exponent = jnp.exp(scores - top)
            denominator = jnp.sum(exponent, axis=1, keepdims=True)
            weights = (exponent * (1.0 / denominator)).astype(low)
            value = v_high if head else v_low
            part = dot(weights, value[:keys], 1, 0)
            total = part if total is None else total + part
            log_total = jnp.broadcast_to(top + jnp.log(denominator), (BLK, LANES))
            lse_ref[head * 8 : (head + 1) * 8, here] = log_total.T[:8]
        att_ref[here, :] = total.astype(low)


def attention_backward_kernel(*refs):
    length_ref, branch_ref, wo_ref, q_ref, k_ref, v_ref, lse_ref, cos_ref, sin_ref = refs[:9]
    dq_ref, dkv_ref, dk_sum, d0_sum, d1_sum = refs[-5:]
    rows = branch_ref.shape[0]
    low = jnp.bfloat16
    lane = lax.broadcasted_iota(jnp.int32, (rows, LANES), 1)
    left = lane < HEAD_DIM
    grad = dot(branch_ref[...], wo_ref[...], 1, 0).astype(low)
    k_only = jnp.where(left, k_ref[...].astype(jnp.float32), 0.0).astype(low)
    v_high = v_ref[...]
    v_low = pltpu.roll(v_high.astype(jnp.float32), HEAD_DIM, 1).astype(low)
    place = lax.broadcasted_iota(jnp.int32, (rows, BLK), 0)
    seen = place < length_ref[0]
    dk_sum[...] = jnp.zeros_like(dk_sum)
    d0_sum[...] = jnp.zeros_like(d0_sum)
    d1_sum[...] = jnp.zeros_like(d1_sum)
    scale = HEAD_DIM ** (-0.5)
    for block in range(rows // BLK):
        here = pl.ds(block * BLK, BLK)
        keys = (block + 1) * BLK
        grad_block = grad[block * BLK : keys]
        query_grads = []
        for head in range(2):
            q_block = q_ref[here, head * LANES : (head + 1) * LANES]
            value = v_high if head else v_low
            scores = dot(k_only[:keys], q_block, 1, 1)
            log_total = lse_ref[head * 8 : head * 8 + 1, here]
            scores = jnp.where(seen[:keys], scores, masked_score)
            probability = jnp.exp(scores - log_total)
            prob_grad = dot(value[:keys], grad_block, 1, 1)
            weighted = probability * prob_grad
            center = jnp.sum(weighted, axis=0, keepdims=True)
            score_grad = (weighted - probability * center).astype(low)
            d_sum = d1_sum if head else d0_sum
            d_sum[:keys] += dot(probability.astype(low), grad_block, 1, 0)
            dk_sum[:keys] += dot(score_grad, q_block, 1, 0)
            query_grads.append(dot(score_grad, k_ref[:keys], 0, 0))
        cosine, sine = cos_ref[here, :] * scale, sin_ref[here, :] * scale
        zero, one = query_grads
        left_here = left[:BLK]
        straight = jnp.where(left_here, zero, pltpu.roll(one, HEAD_DIM, 1))
        turned = jnp.where(left_here, pltpu.roll(zero, HEAD_DIM, 1), one)
        dq_ref[here, :] = (straight * cosine - turned * sine).astype(low)
    dk_all = dk_sum[...]
    dk_rot = dk_all * cos_ref[...] - pltpu.roll(dk_all, HEAD_DIM, 1) * sin_ref[...]
    dv_all = pltpu.roll(d0_sum[...], HEAD_DIM, 1) + d1_sum[...]
    dkv_ref[...] = jnp.where(left, dk_rot, dv_all).astype(low)


def whole(shape):
    return pl.BlockSpec(shape, lambda h: (0,) * len(shape))


def columns(rows, width):
    return pl.BlockSpec((rows, width), lambda h: (0, h))


def attention_forward(length, starts, normed, w_groups, cosine, sine, deps=()):
    rows = normed.shape[0]
    kv_here = w_groups[0].shape[1] // 256
    low = jnp.bfloat16
    return pl.pallas_call(
        attention_forward_kernel,
        grid=(kv_here,),
        in_specs=[SCALARS, SCALARS, whole((rows, D))]
        + [columns(w.shape[0], 256) for w in w_groups]
        + [whole((rows, LANES))] * 2
        + [ANYWHERE] * len(deps),
        out_specs=[
            columns(rows, 256),
            columns(rows, LANES),
            columns(rows, LANES),
            columns(rows, LANES),
            columns(D, 256),
            pl.BlockSpec((16, rows), lambda h: (h, 0)),
        ],
        out_shape=[
            jax.ShapeDtypeStruct((rows, kv_here * 256), low),
            jax.ShapeDtypeStruct((rows, kv_here * LANES), low),
            jax.ShapeDtypeStruct((rows, kv_here * LANES), low),
            jax.ShapeDtypeStruct((rows, kv_here * LANES), low),
            jax.ShapeDtypeStruct((D, kv_here * 256), low),
            jax.ShapeDtypeStruct((kv_here * 16, rows), jnp.float32),
        ],
        compiler_params=pltpu.CompilerParams(vmem_limit_bytes=50 * MIB),
        cost_estimate=SMALL,
        name="attention_forward",
    )(length, starts, normed, *w_groups, cosine, sine, *deps)


def output_projection_kernel(*refs):
    starts_ref, core_ref, att_ref, w0_ref, w1_ref, w2_ref, w3_ref = refs[:7]
    own_ref, other_ref, w_ref = refs[-3:]
    place_rows(starts_ref, (w0_ref, w1_ref, w2_ref, w3_ref), w_ref)
    half = own_ref.shape[0]
    mine = pl.multiple_of(core_ref[0] * half, half)
    others = pl.multiple_of((1 - core_ref[0]) * half, half)
    other_ref[...] = dot(att_ref[pl.ds(others, half), :], w_ref[...], 1, 1).astype(jnp.bfloat16)
    own_ref[...] = dot(att_ref[pl.ds(mine, half), :], w_ref[...], 1, 1)


def output_projection(starts, core, attended, w_groups, deps=()):
    rows, width = attended.shape
    inside = pl.BlockSpec(memory_space=pltpu.VMEM)
    return pl.pallas_call(
        output_projection_kernel,
        in_specs=[SCALARS, SCALARS] + [inside] * 5 + [ANYWHERE] * len(deps),
        out_specs=[inside] * 3,
        out_shape=[
            jax.ShapeDtypeStruct((rows // 2, D), jnp.float32),
            jax.ShapeDtypeStruct((rows // 2, D), jnp.bfloat16),
            jax.ShapeDtypeStruct((D, width), jnp.bfloat16),
        ],
        compiler_params=pltpu.CompilerParams(vmem_limit_bytes=32 * MIB),
        cost_estimate=SMALL,
        name="output_projection",
    )(starts, core, attended, *w_groups, *deps)


def nothing(*refs):
    return None


def after(values, *deps):
    return pl.pallas_call(
        nothing,
        in_specs=[ANYWHERE] * (1 + len(deps)),
        out_specs=ANYWHERE,
        out_shape=jax.ShapeDtypeStruct(values.shape, values.dtype),
        input_output_aliases={0: 0},
        cost_estimate=SMALL,
        name="after",
    )(values, *deps)


def round_kernel(bounds, values_ref, whole_ref, *piece_refs):
    step = pl.program_id(0)
    rounded = values_ref[...].astype(jnp.bfloat16)
    whole_ref[...] = rounded
    for (begin, end), piece_ref in zip(bounds, piece_refs):

        @pl.when((step >= begin) & (step < end))
        def _(piece_ref=piece_ref):
            piece_ref[...] = rounded


def round_units(values, bounds):
    units = values.shape[0]
    shape = (None,) + values.shape[1:]

    def piece_spec(begin, end):
        return pl.BlockSpec(shape, lambda i: (jnp.clip(i - begin, 0, end - begin - 1), 0, 0, 0))

    return pl.pallas_call(
        functools.partial(round_kernel, bounds),
        grid=(units,),
        in_specs=[pl.BlockSpec(shape, lambda i: (i, 0, 0, 0))],
        out_specs=[pl.BlockSpec(shape, lambda i: (i, 0, 0, 0))]
        + [piece_spec(begin, end) for begin, end in bounds],
        out_shape=[jax.ShapeDtypeStruct(values.shape, jnp.bfloat16)]
        + [
            jax.ShapeDtypeStruct((end - begin,) + values.shape[1:], jnp.bfloat16)
            for begin, end in bounds
        ],
        cost_estimate=SMALL,
        name="round_units",
    )(values)


def attention_backward(length, branch_low, w_output, q2, k2, v, lse, cosine, sine, deps=()):
    rows = branch_low.shape[0]
    kv_here = k2.shape[1] // LANES
    low = jnp.bfloat16
    return pl.pallas_call(
        attention_backward_kernel,
        grid=(kv_here,),
        in_specs=[
            SCALARS,
            whole((rows, D)),
            columns(D, LANES),
            columns(rows, 256),
            columns(rows, LANES),
            columns(rows, LANES),
            pl.BlockSpec((16, rows), lambda h: (h, 0)),
            whole((rows, LANES)),
            whole((rows, LANES)),
        ]
        + [pl.BlockSpec(memory_space=pl.ANY)] * len(deps),
        out_specs=[columns(rows, LANES), columns(rows, LANES)],
        out_shape=[
            jax.ShapeDtypeStruct((rows, kv_here * LANES), low),
            jax.ShapeDtypeStruct((rows, kv_here * LANES), low),
        ],
        scratch_shapes=[pltpu.VMEM((rows, LANES), jnp.float32)] * 3,
        compiler_params=pltpu.CompilerParams(vmem_limit_bytes=50 * MIB),
        cost_estimate=SMALL,
        name="attention_backward",
    )(length, branch_low, w_output, q2, k2, v, lse, cosine, sine, *deps)


CHUNK = 512
UNIT_ROWS = 64


def first_unit(piece_refs, piece):
    return sum(p.shape[0] for p in piece_refs[:piece])


def piece_copy(piece_refs, weights, arrived, piece, kind):
    units = piece_refs[piece].shape[0]
    return pltpu.make_async_copy(
        piece_refs[piece].at[:, kind],
        weights.at[kind, pl.ds(first_unit(piece_refs, piece), units)],
        arrived.at[piece, kind],
    )


def row_copy(row_refs, rows_all, landed, index):
    count = len(row_refs) - 1
    rows = row_refs[0].shape[0]
    source = row_refs[index // 2]
    if index % 2:
        source = row_refs[count].at[pl.ds(index // 2 * rows, rows)]
    return pltpu.make_async_copy(
        source, rows_all.at[pl.ds(index * rows, rows)], landed.at[index]
    )


def fetch(kinds, piece_refs, weights, arrived, row_refs=(None,), rows_all=None, landed=None):
    @pl.when(pl.program_id(0) == 0)
    def _():
        for index in range(2 * len(row_refs) - 2):
            row_copy(row_refs, rows_all, landed, index).start()
        for early in kinds:
            for piece in range(len(piece_refs)):
                for kind in early:
                    piece_copy(piece_refs, weights, arrived, piece, kind).start()


def await_weights(kinds, piece_refs, weights, arrived, chunk=None):
    places = range(len(piece_refs))
    if chunk is not None:
        per_chunk = CHUNK // UNIT_ROWS
        places = [p for p in places if first_unit(piece_refs, p) // per_chunk == chunk]

    @pl.when(pl.program_id(0) == 0)
    def _():
        for piece in places:
            for kind in kinds:
                piece_copy(piece_refs, weights, arrived, piece, kind).wait()


def await_rows(row_refs, rows_all, landed):
    step = pl.program_id(0)
    for index in range(2 * len(row_refs) - 2):

        @pl.when(step == index)
        def _(index=index):
            row_copy(row_refs, rows_all, landed, index).wait()


def chunk_weights(weights, kind, chunk):
    units = CHUNK // UNIT_ROWS
    return weights[kind, chunk * units : (chunk + 1) * units].reshape(CHUNK, D)


def spread_weights(route_ref, column, per_unit):
    rows = route_ref.shape[0]
    units = CHUNK // UNIT_ROWS
    count = units if per_unit else units // 4
    width = CHUNK // count
    pieces = [
        jnp.broadcast_to(route_ref[:, column * count + j : column * count + j + 1], (rows, width))
        for j in range(count)
    ]
    return jnp.concatenate(pieces, axis=1)


def store_step(out_refs, values):
    step = pl.program_id(0)
    for index, out_ref in enumerate(out_refs):

        @pl.when(step == index)
        def _(out_ref=out_ref):
            out_ref[...] = values


def expert_hidden(x, route_ref, weights, piece_refs, arrived, first_column, per_unit, outs):
    low = jnp.bfloat16
    slope_ref, silu_ref, inner_ref = outs
    for chunk in range(slope_ref.shape[1] // CHUNK):
        here = slice(chunk * CHUNK, (chunk + 1) * CHUNK)
        await_weights((0, 1), piece_refs, weights, arrived, chunk)
        gate = dot(x, chunk_weights(weights, 0, chunk), 1, 1)
        upper = dot(x, chunk_weights(weights, 1, chunk), 1, 1)
        sigmoid = 0.5 * jnp.tanh(0.5 * gate) + 0.5
        silu = gate * sigmoid
        weight = spread_weights(route_ref, first_column + chunk, per_unit)
        weighted_upper = weight * upper
        slope_ref[:, here] = (weighted_upper * (sigmoid + silu * (1.0 - sigmoid))).astype(low)
        silu_ref[:, here] = (weight * silu).astype(low)
        inner_ref[:, here] = (silu * weighted_upper).astype(low)
    await_weights((2,), piece_refs, weights, arrived)
    return dot(inner_ref[...], weights[2].reshape(-1, D), 1, 0)


def expert_first_kernel(count, pieces, per_unit, *refs):
    parts = count // 2 + 1
    row_refs, route_ref = refs[:parts], refs[parts]
    piece_refs = refs[parts + 1 : parts + 1 + pieces]
    x_ref, mixed_ref, slope_ref, silu_ref, inner_ref = refs[-9:-4]
    weights, arrived, rows_all, landed = refs[-4:]
    fetch(((0, 1), (2,)), piece_refs, weights, arrived, row_refs, rows_all, landed)
    await_rows(row_refs, rows_all, landed)
    rows = x_ref.shape[0]
    x = rows_all[pl.ds(pl.multiple_of(pl.program_id(0) * rows, rows), rows), :]
    x_ref[...] = x
    outs = (slope_ref, silu_ref, inner_ref)
    mixed_ref[...] = expert_hidden(
        x, route_ref, weights, piece_refs, arrived, 0, per_unit, outs
    ).astype(jnp.bfloat16)


def expert_second_kernel(count, pieces, per_unit, first_column, *refs):
    x_ref, mixed_ref, route_ref = refs[:3]
    piece_refs = refs[3 : 3 + pieces]
    out_refs = refs[-5 - count : -5]
    weights, arrived = refs[-2:]
    fetch(((0, 1), (2,)), piece_refs, weights, arrived)
    part = expert_hidden(
        x_ref[...], route_ref, weights, piece_refs, arrived, first_column, per_unit, refs[-5:-2]
    )
    store_step(out_refs, (part + mixed_ref[...].astype(jnp.float32)).astype(jnp.bfloat16))


def expert_backward_kernel(count, pieces, *refs):
    parts = count // 2 + 1
    row_refs = refs[:parts]
    slope_refs, silu_refs = refs[parts : parts + 2], refs[parts + 2 : parts + 4]
    piece_refs = refs[parts + 4 : parts + 4 + pieces]
    out_refs = refs[-9 - count : -9]
    grad_ref = refs[-9]
    gate_refs, upper_refs = refs[-8:-6], refs[-6:-4]
    weights, arrived, rows_all, landed = refs[-4:]
    low = jnp.bfloat16
    fetch(((2,), (0,), (1,)), piece_refs, weights, arrived, row_refs, rows_all, landed)
    await_rows(row_refs, rows_all, landed)
    rows = grad_ref.shape[0]
    grad = rows_all[pl.ds(pl.multiple_of(pl.program_id(0) * rows, rows), rows), :]
    grad_ref[...] = grad
    chunks = slope_refs[0].shape[1] // CHUNK
    for chunk in range(2 * chunks):
        half, place = chunk // chunks, chunk % chunks
        here = slice(place * CHUNK, (place + 1) * CHUNK)
        await_weights((2,), piece_refs, weights, arrived, chunk)
        inner_grad = dot(grad, chunk_weights(weights, 2, chunk), 1, 1)
        slope, silu = slope_refs[half][:, here], silu_refs[half][:, here]
        gate_refs[half][:, here] = (inner_grad * slope.astype(jnp.float32)).astype(low)
        upper_refs[half][:, here] = (inner_grad * silu.astype(jnp.float32)).astype(low)
    units = weights.shape[1] // 2
    await_weights((0, 1), piece_refs, weights, arrived)
    total = None
    for half in range(2):
        mine = pl.ds(half * units, units)
        part = dot(gate_refs[half][...], weights[0, mine].reshape(-1, D), 1, 0)
        part = part + dot(upper_refs[half][...], weights[1, mine].reshape(-1, D), 1, 0)
        total = part if total is None else total + part
    store_step(out_refs, total.astype(low))


def fixed(shape):
    return pl.BlockSpec(shape, lambda i: (0,) * len(shape))


def token_block(rows, width, first=0):
    return pl.BlockSpec((rows, width), lambda i: (first + i, 0))


def expert_scratch(pieces, count=0, rows=0):
    units = sum(p.shape[0] for p in pieces)
    scratch = [
        pltpu.VMEM((3, units, UNIT_ROWS, D), jnp.bfloat16),
        pltpu.SemaphoreType.DMA((len(pieces), 3)),
    ]
    if count:
        scratch += [
            pltpu.VMEM((count * rows, D), jnp.bfloat16),
            pltpu.SemaphoreType.DMA((count,)),
        ]
    return scratch


def expert_call(
    kernel, name, steps, operands, specs, out_specs, widths, singles, kept, scratch, estimate=SMALL
):
    rows, total_rows = singles[1], singles[2]
    low = jnp.bfloat16
    operands, specs = list(operands), list(specs)
    aliases = {}
    if kept is not None:
        for index, buffer in enumerate(kept):
            aliases[len(operands)] = singles[0] + index
            operands.append(buffer)
            specs.append(ANYWHERE)
    outs = pl.pallas_call(
        kernel,
        grid=(steps,),
        in_specs=specs,
        out_specs=[fixed((rows, D))] * singles[0] + out_specs,
        out_shape=[jax.ShapeDtypeStruct((rows, D), low)] * singles[0]
        + [jax.ShapeDtypeStruct((total_rows, w), low) for w in widths],
        scratch_shapes=scratch,
        input_output_aliases=aliases,
        compiler_params=pltpu.CompilerParams(vmem_limit_bytes=60 * MIB),
        cost_estimate=estimate,
        name=name,
    )(*operands)
    return outs[: singles[0]], outs[singles[0] :]


def expert_first(row_parts, route_columns, per_unit, pieces, deps):
    count, rows = 2 * len(row_parts) - 2, row_parts[0].shape[0]
    width = sum(p.shape[0] for p in pieces) * UNIT_ROWS
    widths = [D, D, width, width, width]
    return expert_call(
        functools.partial(expert_first_kernel, count, len(pieces), per_unit),
        "expert_first",
        count,
        list(row_parts) + [route_columns] + list(pieces) + list(deps),
        [ANYWHERE] * len(row_parts)
        + [token_block(rows, route_columns.shape[1])]
        + [ANYWHERE] * (len(pieces) + len(deps)),
        [token_block(rows, w) for w in widths],
        widths,
        (0, rows, count * rows),
        None,
        expert_scratch(pieces, count, rows),
        cost(6 * count * rows * width * D),
    )[1]


def expert_second(count, rows, x, mixed, route_columns, per_unit, pieces, deps):
    width = sum(p.shape[0] for p in pieces) * UNIT_ROWS
    return expert_call(
        functools.partial(expert_second_kernel, count, len(pieces), per_unit, width // CHUNK),
        "expert_second",
        count,
        [x, mixed, route_columns] + list(pieces) + list(deps),
        [
            token_block(rows, D),
            token_block(rows, D),
            token_block(rows, route_columns.shape[1]),
        ]
        + [ANYWHERE] * (len(pieces) + len(deps)),
        [token_block(rows, width)] * 3,
        [width] * 3,
        (count, rows, x.shape[0]),
        None,
        expert_scratch(pieces),
    )


def expert_backward(first, row_parts, slopes, silus, pieces, kept):
    count, rows = 2 * len(row_parts) - 2, row_parts[0].shape[0]
    width = slopes[0].shape[1]
    widths = [D] + [width] * 4
    return expert_call(
        functools.partial(expert_backward_kernel, count, len(pieces)),
        "expert_backward",
        count,
        list(row_parts) + list(slopes) + list(silus) + list(pieces),
        [ANYWHERE] * len(row_parts)
        + [token_block(rows, width, first)] * 4
        + [ANYWHERE] * len(pieces),
        [token_block(rows, w, first) for w in widths],
        widths,
        (count, rows, slopes[0].shape[0]),
        kept,
        expert_scratch(pieces, count, rows),
    )


def weight_grad_kernel(count, *refs):
    right_ref = refs[count]
    outs = refs[-2 * count :]
    step = pl.program_id(0)
    for index in range(count):
        for slot in range(2):

            @pl.when(step == 2 * index + slot)
            def _(index=index, slot=slot):
                outs[2 * index + slot][...] = dot(refs[index][...], right_ref[...], 0, 0).astype(
                    jnp.bfloat16
                )


def weight_grads(lefts, right, deps=(), estimate=SMALL):
    rows = right.shape[0]
    columns_here = lefts[0].shape[1] // 2
    count = len(lefts)

    def left_spec(index):
        return pl.BlockSpec(
            (rows, columns_here), lambda i: (0, 1 - jnp.clip(i - 2 * index, 0, 1))
        )

    return pl.pallas_call(
        functools.partial(weight_grad_kernel, count),
        grid=(2 * count,),
        in_specs=[left_spec(index) for index in range(count)]
        + [pl.BlockSpec((rows, D), lambda i: (0, 0), pipeline_mode=pl.Buffered(1))]
        + [ANYWHERE] * len(deps),
        out_specs=[fixed((columns_here, D))] * (2 * count),
        out_shape=[jax.ShapeDtypeStruct((columns_here, D), jnp.bfloat16)] * (2 * count),
        compiler_params=pltpu.CompilerParams(vmem_limit_bytes=56 * MIB),
        cost_estimate=estimate,
        name="weight_grads",
    )(*lefts, right, *deps)


def update_blocks(grads, lefts, rights, left_roots, right_roots, left_outs, right_outs, step_outs):
    low = jnp.bfloat16
    grads = [grad.astype(low) for grad in grads]
    firsts = [
        dot(root[...].astype(low), grad, 1, 0).astype(low) for root, grad in zip(left_roots, grads)
    ]
    for grad, left, out in zip(grads, lefts, left_outs):
        out[...] = stat_decay * left[...] + dot(grad, grad, 1, 1)
    for first, root, (out, master) in zip(firsts, right_roots, step_outs):
        out[...] = master[...] - D ** (-0.5) * dot(first, root[...].astype(low), 1, 0)
    for grad, right, out in zip(grads, rights, right_outs):
        out[...] = stat_decay * right[...] + dot(grad, grad, 0, 0)


def expert_update_kernel(count, *refs):
    parts = refs[:count]
    master, left, right, left_root, right_root = refs[count : count + 5]
    grad_out, left_out, right_out, new_out = refs[-4:]
    units, rows, _ = grad_out.shape
    grad = parts[0][...].astype(jnp.float32)
    for part in parts[1:]:
        grad = grad + part[...].astype(jnp.float32)
    grad = grad.reshape(units, rows, D)
    grad_out[...] = grad
    blocks = [(u, b) for u in range(units) for b in range(D // BLOCK)]

    def wide(ref):
        return [ref.at[u, :, b * BLOCK : (b + 1) * BLOCK] for u, b in blocks]

    def square(ref):
        return [ref.at[u, b] for u, b in blocks]

    update_blocks(
        [grad[u, :, b * BLOCK : (b + 1) * BLOCK] for u, b in blocks],
        square(left),
        square(right),
        square(left_root),
        square(right_root),
        square(left_out),
        square(right_out),
        list(zip(wide(new_out), wide(master))),
    )


def expert_update(kind, parts, state, kept, deps=()):
    master, left, right, left_root, right_root = state
    units, _, rows, _ = master.shape
    step = min(units, 2)
    flat = pl.BlockSpec((step, None, rows, D), lambda i: (i, kind, 0, 0))
    lefts = pl.BlockSpec((step, None) + left.shape[2:], lambda i: (i, kind, 0, 0, 0))
    rights = pl.BlockSpec((step, None) + right.shape[2:], lambda i: (i, kind, 0, 0, 0))
    operands = list(parts) + list(state) + list(deps)
    specs = [pl.BlockSpec((step * rows, D), lambda i: (i, 0))] * len(parts)
    specs += [flat, lefts, rights, lefts, rights] + [ANYWHERE] * len(deps)
    aliases = {}
    if kept is not None:
        for index, buffer in enumerate(kept):
            aliases[len(operands)] = index
            operands.append(buffer)
            specs.append(ANYWHERE)
    return pl.pallas_call(
        functools.partial(expert_update_kernel, len(parts)),
        grid=(units // step,),
        in_specs=specs,
        out_specs=[flat, lefts, rights, flat],
        out_shape=[jax.ShapeDtypeStruct(a.shape, jnp.float32) for a in (master, left, right, master)],
        input_output_aliases=aliases,
        compiler_params=pltpu.CompilerParams(vmem_limit_bytes=56 * MIB),
        cost_estimate=cost(12e9),
        name="expert_update",
    )(*operands)


def attention_update_kernel(qkv_ref, wo_ref, master, left, right, left_root, right_root, *outs):
    grad_out, left_out, right_out, new_out = outs
    heads = qkv_ref.shape[1] // 256
    rows = qkv_ref.shape[0]
    low_lanes = lax.broadcasted_iota(jnp.int32, (rows, LANES), 1) < HEAD_DIM
    grad = qkv_ref[...].astype(jnp.float32)
    queries = heads * LANES
    keys = queries // 2
    for head in range(heads):
        grad_out[:, head * LANES : (head + 1) * LANES] = grad[:, head * 256 : head * 256 + LANES]
    for pair in range(heads // 2):
        begin = pair * 512 + LANES
        one, two = grad[:, begin : begin + LANES], grad[:, begin + 256 : begin + 256 + LANES]
        place = queries + pair * LANES
        grad_out[:, place : place + LANES] = jnp.where(low_lanes, one, pltpu.roll(two, HEAD_DIM, 1))
        place = place + keys
        grad_out[:, place : place + LANES] = jnp.where(low_lanes, pltpu.roll(one, HEAD_DIM, 1), two)
    grad_out[:, queries + 2 * keys :] = wo_ref[...].astype(jnp.float32)
    blocks = range(grad_out.shape[1] // BLOCK)

    def wide(ref):
        return [ref.at[:, b * BLOCK : (b + 1) * BLOCK] for b in blocks]

    def square(ref):
        return [ref.at[b] for b in blocks]

    update_blocks(
        [part[...] for part in wide(grad_out)],
        square(left),
        square(right),
        square(left_root),
        square(right_root),
        square(left_out),
        square(right_out),
        list(zip(wide(new_out), wide(master))),
    )


def attention_update(qkv_part, output_part, state):
    inside = pl.BlockSpec(memory_space=pltpu.VMEM)
    master, left, right = state[:3]
    return pl.pallas_call(
        attention_update_kernel,
        in_specs=[inside] * 7,
        out_specs=[inside] * 4,
        out_shape=[jax.ShapeDtypeStruct(a.shape, jnp.float32) for a in (master, left, right, master)],
        compiler_params=pltpu.CompilerParams(vmem_limit_bytes=40 * MIB),
        cost_estimate=SMALL,
        name="attention_update",
    )(qkv_part, output_part, *state)


def spread_tokens(own, relay):
    beside, across, both = TOKEN_MASKS[1:]
    rows = [own, swap_dp(own, beside), swap_dp(own, across)]
    return rows + [swap_dp(rows[2], beside) if relay else swap_dp(own, both)]


def with_other(own_rows):
    return list(own_rows) + [swap_core(jnp.concatenate(own_rows, axis=0))]


def sum_cores(place, parts):
    own, other = parts
    total = own.astype(jnp.float32) + swap_core(other).astype(jnp.float32)
    return total if place == 0 else total.astype(jnp.bfloat16)


def return_tokens(sums):
    total = sums[0]
    for rows, mask in zip(sums[1:], TOKEN_MASKS[1:]):
        total = total + swap_dp(rows, mask).astype(jnp.float32)
    return total


def extra_masks():
    count = lax.axis_size("dp")
    used = sum(WEIGHT_BITS) + TOKEN_MASKS[-1]
    masks = []
    mask = 1
    while mask < count:
        if not mask & used:
            masks.append(mask)
        mask *= 2
    return masks


def gather_attention(own, count, qkv_cols, deps):
    low = jnp.bfloat16
    high_digit = jnp.floor(count / 64.0)
    digits = jnp.stack([high_digit, count - 64.0 * high_digit]).astype(low)
    digits = jnp.pad(digits[None, :], ((0, 7), (0, own.shape[1] - 2)))
    own = jnp.concatenate([own, digits], axis=0)
    slot_rows = own.shape[0]
    masks = list(range(0, lax.axis_size("dp"), 4))
    line = jnp.concatenate([own] + [swap_dp(own, mask) for mask in masks[1:]], axis=0)
    line = after(line, *deps)
    inner, outer = line[:, :qkv_cols], line[:, qkv_cols:]
    inner = [inner] + [swap_dp(inner, mask) for mask in (1, 2, 3)]
    outer = [outer] + [swap_dp(outer, mask) for mask in (1, 2, 3)]
    table = jnp.array([[group ^ mask for mask in masks] for group in range(4)], jnp.int32)
    total = 0.0
    for group in inner:
        digits = group.reshape(len(masks), slot_rows, -1)[:, slot_rows - 8, :2]
        digits = jnp.sum(digits.astype(jnp.float32), axis=0)
        total = total + 64.0 * digits[0] + digits[1]
    total = total.reshape(1, 1)
    return line, inner, outer, lax.axis_index("dp") ^ table, (total + swap_core(total))[0, 0]


FAR_PIECES = ((0, 4), (4, 8))
NEAR_PIECES = ((0, 3), (3, 8))


def round_weights(master):
    bounds = FAR_PIECES + NEAR_PIECES
    extra = extra_masks()
    if not extra:
        shard, *pieces = round_units(master, bounds)
    else:
        shard = round_units(master, ())[0]
        for mask in extra:
            shard = jnp.concatenate([shard, swap_dp(shard, mask)], axis=0)
        pieces = [shard[begin:end] for begin, end in bounds]
    return shard, pieces[: len(FAR_PIECES)], pieces[len(FAR_PIECES) :]


def unit_owners():
    masks = [0]
    for mask in extra_masks():
        masks = masks + [m ^ mask for m in masks]
    first, second = WEIGHT_BITS
    masks = [m ^ k for k in (0, first, second, first ^ second) for m in masks]
    return lax.axis_index("dp") ^ jnp.array(masks, jnp.int32)


def add_grads(far, both):
    return (far.astype(jnp.float32) + swap_dp(both, WEIGHT_BITS[0]).astype(jnp.float32)).astype(
        jnp.bfloat16
    )


def grad_terms(own, near, far):
    parts = [own, swap_dp(near, WEIGHT_BITS[0]), far]
    masks = extra_masks()
    if not masks:
        return parts
    total = sum(p.astype(jnp.float32) for p in parts)
    for mask in reversed(masks):
        half = total.shape[0] // 2
        sent = swap_dp(total[half:].astype(jnp.bfloat16), mask)
        total = total[:half] + sent.astype(jnp.float32)
    return [total]


def on_device(
    activations,
    targets,
    lengths,
    token_mask,
    routes,
    route_weights,
    norm_gains,
    attention_master,
    expert_master,
    attention_left,
    attention_right,
    attention_left_root,
    attention_right_root,
    expert_left,
    expert_right,
    expert_left_root,
    expert_right_root,
):
    low = jnp.bfloat16
    own_rows = activations.shape[0]
    tensor_size = lax.axis_size("tensor")
    core = lax.axis_index("tensor")
    tokens_total = own_rows * tensor_size * lax.axis_size("dp")
    seq_length = lengths[0]
    position = core * own_rows + jnp.arange(own_rows, dtype=jnp.int32)
    valid_rows = ((token_mask == 1) & (position < seq_length)).astype(jnp.float32)
    valid_here = jnp.sum(valid_rows)

    routing = jnp.concatenate([routes.T.astype(jnp.float32), route_weights.T], axis=0)
    routing_parts = [routing] + [swap_dp(routing, mask) for mask in TOKEN_MASKS[1:]]
    heads_here = HEADS // tensor_size
    kv_here = KV_HEADS // tensor_size
    query_cols = heads_here * HEAD_DIM
    key_cols = kv_here * HEAD_DIM
    qkv_cols = query_cols + 2 * key_cols
    rows_here = attention_master.shape[0]

    def by_head(values):
        rows = values.shape[0]
        query = values[:, :query_cols].reshape(rows, kv_here, LANES)
        key = values[:, query_cols : query_cols + key_cols].reshape(rows, kv_here, HEAD_DIM)
        value = values[:, query_cols + key_cols : qkv_cols].reshape(rows, kv_here, HEAD_DIM)
        return jnp.concatenate([query, key, value], axis=2).reshape(rows, qkv_cols)

    attention_low = attention_master.astype(low)
    own_columns = jnp.concatenate([by_head(attention_low), attention_low[:, qkv_cols:]], axis=1)
    shard, for_far, for_near = round_weights(expert_master)
    line, w_inner, w_outer, devices, valid_total = gather_attention(
        own_columns, valid_here, qkv_cols, [shard] + routing_parts[1:]
    )
    starts = devices * rows_here
    hidden = activations.astype(jnp.float32)
    normed_own, attention_scaling = normalize(hidden, norm_gains[0])
    normed_own = normed_own.astype(low)
    normed = in_order(normed_own, swap_core(normed_own))

    near_bit, far_bit = WEIGHT_BITS
    for_near[0] = after(for_near[0], *w_inner[1:])
    near = [swap_dp(piece, near_bit) for piece in for_near]
    far = [swap_dp(after(piece, line), far_bit) for piece in for_far]

    seq_rows = normed.shape[0]
    half_width = HEAD_DIM // 2
    frequency = theta_base ** (-jnp.arange(half_width, dtype=jnp.float32) * 2.0 / HEAD_DIM)
    angles = jnp.arange(seq_rows, dtype=jnp.float32)[:, None] * frequency[None, :]
    cosine = jnp.tile(jnp.cos(angles), (1, LANES // half_width))
    sine = jnp.tile(jnp.sin(angles), (1, LANES // half_width))
    q2, k2, v_high, attended, w_qkv, log_totals = attention_forward(
        lengths,
        starts,
        normed,
        w_inner,
        cosine,
        sine,
    )
    branch, branch_other, w_output = output_projection(
        starts, core.reshape(1).astype(jnp.int32), attended, w_outer, far[:1] + near[:1]
    )
    branch = branch + swap_core(branch_other).astype(jnp.float32)
    middle = hidden + branch
    mix_own, mix_scaling = normalize(middle, norm_gains[1])

    routing = jnp.stack(routing_parts).reshape(len(TOKEN_MASKS), 2 * TOPK, 2, own_rows)
    routing = jnp.stack(
        [
            lax.dynamic_index_in_dim(routing, core, 2, keepdims=False),
            lax.dynamic_index_in_dim(routing, 1 - core, 2, keepdims=False),
        ],
        axis=1,
    )
    unit_here = expert_master.shape[0]
    unit_ids = (unit_owners()[:, None] * unit_here + jnp.arange(unit_here)[None, :]).reshape(-1)
    expert_of = unit_ids // GROUPS
    per_unit = unit_here % 4 != 0
    if not per_unit:
        expert_of = expert_of[::4]
    named = (
        routing[:, :, None, :TOPK] == expert_of.astype(jnp.float32)[None, None, :, None, None]
    )
    route_columns = jnp.sum(jnp.where(named, routing[:, :, None, TOPK:], 0.0), axis=3)
    route_columns = route_columns.transpose(0, 1, 3, 2).reshape(-1, expert_of.shape[0])

    spread = spread_tokens(mix_own.astype(low), True)
    both = [swap_dp(piece, near_bit) for piece in far]
    later = [after(spread[1], far[1], near[1]), spread[2], after(spread[3], both[0])]
    mix_rows = with_other(spread[:1] + later)
    mix, mixed, *firsts = expert_first(
        mix_rows, route_columns, per_unit, [shard] + near, []
    )
    pieces = [shard] + near + far + both
    mixed_parts, seconds = expert_second(
        2 * len(spread), own_rows, mix, mixed, route_columns, per_unit, far + both, []
    )
    slopes, silus, inners = ([firsts[i], seconds[i]] for i in range(3))
    sums = [sum_cores(i, mixed_parts[2 * i : 2 * i + 2]) for i in range(len(TOKEN_MASKS))]
    output = middle + return_tokens(sums)
    residual_error = output - targets
    loss_part = jnp.sum(valid_rows[:, None] * residual_error * residual_error)
    output_grad = 2.0 / valid_total * valid_rows[:, None] * residual_error

    spread = spread_tokens(output_grad.astype(low), False)
    backward = functools.partial(expert_backward, slopes=slopes, silus=silus, pieces=pieces)
    parts0, kept = backward(0, [spread[0], swap_core(spread[0])], kept=None)
    later = [after(rows, parts0[0]) for rows in spread[1:]]
    parts1, kept = backward(2, with_other(later), kept=kept)
    parts = list(parts0) + list(parts1)
    sums = [sum_cores(i, parts[2 * i : 2 * i + 2]) for i in range(len(TOKEN_MASKS))]
    sent = return_tokens(sums)
    output_low = kept[0]
    gates, uppers = kept[1:3], kept[3:5]
    full = cost(30e9)
    down_far = weight_grads([inners[1]], output_low, (), full)
    gate_far = weight_grads([gates[1]], mix, [down_far[0]] + sums[1:], full)
    down_sum = add_grads(down_far[1], down_far[0])
    upper_far = weight_grads([uppers[1]], mix, [gate_far[0], down_sum], full)
    gate_sum = add_grads(gate_far[1], gate_far[0])
    upper_sum = add_grads(upper_far[1], upper_far[0])
    far_gate, far_upper, far_down = (
        swap_dp(rows, far_bit) for rows in (gate_sum, upper_sum, down_sum)
    )
    mix_back, gain_mix = normalize_back(middle, mix_scaling, norm_gains[1], sent)
    middle_grad = output_grad + mix_back
    branch_own = middle_grad.astype(low)
    branch_low = in_order(branch_own, swap_core(branch_own))
    dq, dkv = attention_backward(
        lengths, branch_low, w_output, q2, k2, v_high, log_totals, cosine, sine,
        [upper_far[0], gate_sum],
    )
    qkv_grad = jnp.concatenate(
        [dq.reshape(seq_rows, kv_here, LANES), dkv.reshape(seq_rows, kv_here, LANES)], axis=2
    ).reshape(seq_rows, qkv_cols)
    qkv_part = dot(normed, qkv_grad, 0, 0).astype(low)
    output_part = dot(branch_low, attended, 0, 0).astype(low)
    down_near = weight_grads([inners[0]], output_low, [qkv_part, upper_sum, far_down], full)
    gate_up_near = weight_grads(
        [gates[0], uppers[0]], mix, [down_near[0], output_part], full
    )
    qkv_part = lax.psum_scatter(qkv_part, "dp", scatter_dimension=0, tiled=True)
    output_part = lax.psum_scatter(output_part, "dp", scatter_dimension=0, tiled=True)
    normed_grad_other = dot(other_half(qkv_grad), w_qkv, 1, 1).astype(low)
    normed_grad = dot(own_half(qkv_grad), w_qkv, 1, 1)
    normed_grad = normed_grad + swap_core(normed_grad_other).astype(jnp.float32)
    attention_back, gain_attention = normalize_back(
        hidden, attention_scaling, norm_gains[0], normed_grad
    )
    input_grad = middle_grad + attention_back
    parts = {
        2: grad_terms(down_near[1], down_near[0], far_down),
        0: grad_terms(gate_up_near[1], gate_up_near[0], far_gate),
        1: grad_terms(gate_up_near[3], gate_up_near[2], far_upper),
    }
    state = (expert_master, expert_left, expert_right, expert_left_root, expert_right_root)
    updated = expert_update(2, parts[2], state, None, [input_grad, far_gate])
    updated = expert_update(0, parts[0], state, updated, [far_upper])
    loss_row = jnp.full((1, D), loss_part)
    sums = jnp.concatenate([gain_attention[None], gain_mix[None], loss_row], axis=0)
    sums = sum_everywhere(after(sums, updated[0]))
    updated = expert_update(1, parts[1], state, updated, [sums])
    expert_grad, expert_left_new, expert_right_new, expert_new = updated
    gain_grad = sums[:2]
    mean_loss = sums[2, 0] / valid_total
    gains_new = norm_gains - gain_rate * tokens_total**0.5 * gain_grad

    attention_grad, attention_left_new, attention_right_new, attention_new = attention_update(
        qkv_part,
        output_part,
        (
            attention_master,
            attention_left[0],
            attention_right[0],
            attention_left_root[0],
            attention_right_root[0],
        ),
    )
    return (
        output,
        mean_loss,
        input_grad,
        gain_grad,
        gains_new,
        attention_grad,
        attention_left_new[None],
        attention_right_new[None],
        attention_new,
        expert_grad,
        expert_left_new,
        expert_right_new,
        expert_new,
    )


def solution(mesh):
    return jax.shard_map(
        on_device,
        mesh=mesh,
        in_specs=(
            P(("dp", "tensor"), None),
            P(("dp", "tensor"), None),
            P("dp"),
            P(("dp", "tensor")),
            P("dp", None),
            P("dp", None),
            P(),
            P("dp", "tensor"),
            P("dp", None, "tensor", None),
            P("dp", "tensor", None, None),
            P("dp", "tensor", None, None),
            P("dp", "tensor", None, None),
            P("dp", "tensor", None, None),
            P("dp", None, None, "tensor", None),
            P("dp", None, "tensor", None, None),
            P("dp", None, None, "tensor", None),
            P("dp", None, "tensor", None, None),
        ),
        out_specs=(
            P(("dp", "tensor"), None),
            P(),
            P(("dp", "tensor"), None),
            P(),
            P(),
            P("dp", "tensor"),
            P("dp", "tensor", None, None),
            P("dp", "tensor", None, None),
            P("dp", "tensor"),
            P("dp", None, "tensor", None),
            P("dp", None, None, "tensor", None),
            P("dp", None, "tensor", None, None),
            P("dp", None, "tensor", None),
        ),
        check_vma=False,
    )
```

```python
import functools

import jax
import jax.numpy as jnp
from jax import lax
from jax.experimental import pallas as pl
from jax.experimental.pallas import tpu as pltpu
from jax.sharding import PartitionSpec as P

D = 1024
HEADS = 16
KV_HEADS = 8
HEAD_DIM = 64
EXPERTS = 32
TOPK = 8
BLK = 256
GROUPS = 4
BLOCK = 256
LANES = 128

epsilon = 1e-05
stat_decay = 0.9
gain_rate = 0.02
theta_base = 10000.0
masked_score = -1e30
MIB = 1 << 20
SMALL = pl.CostEstimate(flops=1000, bytes_accessed=1000, transcendentals=0)


def cost(flops):
    return pl.CostEstimate(flops=int(flops), bytes_accessed=1000, transcendentals=0)


ANYWHERE = pl.BlockSpec(memory_space=pl.ANY)
SCALARS = pl.BlockSpec(memory_space=pltpu.SMEM)

TOKEN_MASKS = (0, 1, 4, 5)
WEIGHT_BITS = (2, 8)


def dot(left, right, left_dim, right_dim):
    return lax.dot_general(
        left, right, (((left_dim,), (right_dim,)), ((), ())), preferred_element_type=jnp.float32
    )


def normalize(hidden, gain):
    scaling = lax.rsqrt(jnp.mean(hidden * hidden, axis=-1, keepdims=True) + epsilon)
    return (hidden * scaling * gain, scaling)


def normalize_back(hidden, scaling, gain, upstream):
    weighted = upstream * gain
    center = jnp.mean(weighted * hidden, axis=-1, keepdims=True)
    input_part = scaling * weighted - hidden * (scaling * scaling * scaling) * center
    return (input_part, jnp.sum(upstream * hidden * scaling, axis=0))


def swap_dp(values, mask):
    count = lax.axis_size("dp")
    return lax.ppermute(values, "dp", [(i, i ^ mask) for i in range(count)])


def swap_core(values):
    count = lax.axis_size("tensor")
    return lax.ppermute(values, "tensor", [(i, i ^ 1) for i in range(count)])


def sum_everywhere(values):
    values = values + swap_core(values)
    own = sum(values if mask == 0 else swap_dp(values, mask) for mask in TOKEN_MASKS)
    masks = [m for m in range(1, lax.axis_size("dp")) if not m & TOKEN_MASKS[-1]]
    return own + sum(swap_dp(own, mask) for mask in masks)


def in_order(own, other):
    first = lax.axis_index("tensor") == 0
    return jnp.concatenate([jnp.where(first, own, other), jnp.where(first, other, own)], axis=0)


def own_half(values):
    half = values.shape[0] // 2
    return lax.dynamic_slice_in_dim(values, lax.axis_index("tensor") * half, half, 0)


def other_half(values):
    half = values.shape[0] // 2
    return lax.dynamic_slice_in_dim(values, (1 - lax.axis_index("tensor")) * half, half, 0)


def turn(values):
    lane = lax.broadcasted_iota(jnp.int32, values.shape, 1)
    half = HEAD_DIM // 2
    return jnp.where(
        lane % HEAD_DIM < half,
        -pltpu.roll(values, LANES - half, 1),
        pltpu.roll(values, half, 1),
    )


def place_rows(starts_ref, source_refs, target_ref):
    for group, source_ref in enumerate(source_refs):
        count = starts_ref.shape[1]
        slot_rows = source_ref.shape[0] // count
        rows = target_ref.shape[0] // count // len(source_refs)
        for slot in range(count):
            start = pl.multiple_of(starts_ref[group, slot], rows)
            begin = slot * slot_rows
            target_ref[pl.ds(start, rows), :] = source_ref[begin : begin + rows, :]


def attention_forward_kernel(*refs):
    length_ref, starts_ref, x_ref, w0_ref, w1_ref, w2_ref, w3_ref, cos_ref, sin_ref = refs[:9]
    q_ref, k_ref, v_ref, att_ref, w_ref, lse_ref = refs[-6:]
    rows = x_ref.shape[0]
    place_rows(starts_ref, (w0_ref, w1_ref, w2_ref, w3_ref), w_ref)
    low = jnp.bfloat16
    cosine, sine = cos_ref[...], sin_ref[...]
    lane = lax.broadcasted_iota(jnp.int32, (rows, LANES), 1)
    left = lane < HEAD_DIM
    projected = dot(x_ref[...], w_ref[...], 1, 0)
    q_raw = projected[:, :LANES]
    q_turn = turn(q_raw)
    scale = HEAD_DIM ** (-0.5)
    q_rot = (q_raw * cosine + q_turn * sine) * scale
    q_rot_turn = (q_turn * cosine - q_raw * sine) * scale
    q_ref[:, :LANES] = jnp.where(left, q_rot, pltpu.roll(q_rot_turn, HEAD_DIM, 1)).astype(low)
    q_ref[:, LANES:] = jnp.where(left, pltpu.roll(q_rot, HEAD_DIM, 1), q_rot_turn).astype(low)
    kv_raw = projected[:, LANES:]
    k_turn = turn(kv_raw)
    k_rot = kv_raw * cosine + k_turn * sine
    k_rot_turn = k_turn * cosine - kv_raw * sine
    k_ref[...] = jnp.where(left, k_rot, pltpu.roll(k_rot_turn, HEAD_DIM, 1)).astype(low)
    v_high = jnp.where(left, 0.0, kv_raw)
    v_ref[...] = v_high.astype(low)
    v_low = pltpu.roll(v_high, HEAD_DIM, 1).astype(low)
    v_high = v_high.astype(low)
    k_only = jnp.where(left, k_rot, 0.0).astype(low)
    place = lax.broadcasted_iota(jnp.int32, (1, rows), 1)
    bias = jnp.where(place < length_ref[0], 0.0, masked_score)
    for block in range(rows // BLK):
        here = pl.ds(block * BLK, BLK)
        keys = (block + 1) * BLK
        total = None
        for head in range(2):
            q_block = q_ref[here, head * LANES : (head + 1) * LANES]
            scores = dot(q_block, k_only[:keys], 1, 1) + bias[:, :keys]
            top = jnp.max(scores, axis=1, keepdims=True)
            exponent = jnp.exp(scores - top)
            denominator = jnp.sum(exponent, axis=1, keepdims=True)
            weights = (exponent * (1.0 / denominator)).astype(low)
            value = v_high if head else v_low
            part = dot(weights, value[:keys], 1, 0)
            total = part if total is None else total + part
            log_total = jnp.broadcast_to(top + jnp.log(denominator), (BLK, LANES))
            lse_ref[head * 8 : (head + 1) * 8, here] = log_total.T[:8]
        att_ref[here, :] = total.astype(low)


def attention_backward_kernel(*refs):
    length_ref, branch_ref, wo_ref, q_ref, k_ref, v_ref, lse_ref, cos_ref, sin_ref = refs[:9]
    dq_ref, dkv_ref, dk_sum, d0_sum, d1_sum = refs[-5:]
    rows = branch_ref.shape[0]
    low = jnp.bfloat16
    lane = lax.broadcasted_iota(jnp.int32, (rows, LANES), 1)
    left = lane < HEAD_DIM
    grad = dot(branch_ref[...], wo_ref[...], 1, 0).astype(low)
    k_only = jnp.where(left, k_ref[...].astype(jnp.float32), 0.0).astype(low)
    v_high = v_ref[...]
    v_low = pltpu.roll(v_high.astype(jnp.float32), HEAD_DIM, 1).astype(low)
    place = lax.broadcasted_iota(jnp.int32, (rows, BLK), 0)
    seen = place < length_ref[0]
    dk_sum[...] = jnp.zeros_like(dk_sum)
    d0_sum[...] = jnp.zeros_like(d0_sum)
    d1_sum[...] = jnp.zeros_like(d1_sum)
    scale = HEAD_DIM ** (-0.5)
    for block in range(rows // BLK):
        here = pl.ds(block * BLK, BLK)
        keys = (block + 1) * BLK
        grad_block = grad[block * BLK : keys]
        query_grads = []
        for head in range(2):
            q_block = q_ref[here, head * LANES : (head + 1) * LANES]
            value = v_high if head else v_low
            scores = dot(k_only[:keys], q_block, 1, 1)
            log_total = lse_ref[head * 8 : head * 8 + 1, here]
            scores = jnp.where(seen[:keys], scores, masked_score)
            probability = jnp.exp(scores - log_total)
            prob_grad = dot(value[:keys], grad_block, 1, 1)
            weighted = probability * prob_grad
            center = jnp.sum(weighted, axis=0, keepdims=True)
            score_grad = (weighted - probability * center).astype(low)
            d_sum = d1_sum if head else d0_sum
            d_sum[:keys] += dot(probability.astype(low), grad_block, 1, 0)
            dk_sum[:keys] += dot(score_grad, q_block, 1, 0)
            query_grads.append(dot(score_grad, k_ref[:keys], 0, 0))
        cosine, sine = cos_ref[here, :] * scale, sin_ref[here, :] * scale
        zero, one = query_grads
        left_here = left[:BLK]
        straight = jnp.where(left_here, zero, pltpu.roll(one, HEAD_DIM, 1))
        turned = jnp.where(left_here, pltpu.roll(zero, HEAD_DIM, 1), one)
        dq_ref[here, :] = (straight * cosine - turned * sine).astype(low)
    dk_all = dk_sum[...]
    dk_rot = dk_all * cos_ref[...] - pltpu.roll(dk_all, HEAD_DIM, 1) * sin_ref[...]
    dv_all = pltpu.roll(d0_sum[...], HEAD_DIM, 1) + d1_sum[...]
    dkv_ref[...] = jnp.where(left, dk_rot, dv_all).astype(low)


def whole(shape):
    return pl.BlockSpec(shape, lambda h: (0,) * len(shape))


def columns(rows, width):
    return pl.BlockSpec((rows, width), lambda h: (0, h))


def attention_forward(length, starts, normed, w_groups, cosine, sine, deps=()):
    rows = normed.shape[0]
    kv_here = w_groups[0].shape[1] // 256
    low = jnp.bfloat16
    return pl.pallas_call(
        attention_forward_kernel,
        grid=(kv_here,),
        in_specs=[SCALARS, SCALARS, whole((rows, D))]
        + [columns(w.shape[0], 256) for w in w_groups]
        + [whole((rows, LANES))] * 2
        + [ANYWHERE] * len(deps),
        out_specs=[
            columns(rows, 256),
            columns(rows, LANES),
            columns(rows, LANES),
            columns(rows, LANES),
            columns(D, 256),
            pl.BlockSpec((16, rows), lambda h: (h, 0)),
        ],
        out_shape=[
            jax.ShapeDtypeStruct((rows, kv_here * 256), low),
            jax.ShapeDtypeStruct((rows, kv_here * LANES), low),
            jax.ShapeDtypeStruct((rows, kv_here * LANES), low),
            jax.ShapeDtypeStruct((rows, kv_here * LANES), low),
            jax.ShapeDtypeStruct((D, kv_here * 256), low),
            jax.ShapeDtypeStruct((kv_here * 16, rows), jnp.float32),
        ],
        compiler_params=pltpu.CompilerParams(vmem_limit_bytes=50 * MIB),
        cost_estimate=SMALL,
        name="attention_forward",
    )(length, starts, normed, *w_groups, cosine, sine, *deps)


def output_projection_kernel(*refs):
    starts_ref, core_ref, att_ref, w0_ref, w1_ref, w2_ref, w3_ref = refs[:7]
    own_ref, other_ref, w_ref = refs[-3:]
    place_rows(starts_ref, (w0_ref, w1_ref, w2_ref, w3_ref), w_ref)
    half = own_ref.shape[0]
    mine = pl.multiple_of(core_ref[0] * half, half)
    others = pl.multiple_of((1 - core_ref[0]) * half, half)
    other_ref[...] = dot(att_ref[pl.ds(others, half), :], w_ref[...], 1, 1).astype(jnp.bfloat16)
    own_ref[...] = dot(att_ref[pl.ds(mine, half), :], w_ref[...], 1, 1)


def output_projection(starts, core, attended, w_groups, deps=()):
    rows, width = attended.shape
    inside = pl.BlockSpec(memory_space=pltpu.VMEM)
    return pl.pallas_call(
        output_projection_kernel,
        in_specs=[SCALARS, SCALARS] + [inside] * 5 + [ANYWHERE] * len(deps),
        out_specs=[inside] * 3,
        out_shape=[
            jax.ShapeDtypeStruct((rows // 2, D), jnp.float32),
            jax.ShapeDtypeStruct((rows // 2, D), jnp.bfloat16),
            jax.ShapeDtypeStruct((D, width), jnp.bfloat16),
        ],
        compiler_params=pltpu.CompilerParams(vmem_limit_bytes=32 * MIB),
        cost_estimate=SMALL,
        name="output_projection",
    )(starts, core, attended, *w_groups, *deps)


def nothing(*refs):
    return None


def after(values, *deps):
    return pl.pallas_call(
        nothing,
        in_specs=[ANYWHERE] * (1 + len(deps)),
        out_specs=ANYWHERE,
        out_shape=jax.ShapeDtypeStruct(values.shape, values.dtype),
        input_output_aliases={0: 0},
        cost_estimate=SMALL,
        name="after",
    )(values, *deps)


def round_kernel(bounds, values_ref, whole_ref, *piece_refs):
    step = pl.program_id(0)
    rounded = values_ref[...].astype(jnp.bfloat16)
    whole_ref[...] = rounded
    for (begin, end), piece_ref in zip(bounds, piece_refs):

        @pl.when((step >= begin) & (step < end))
        def _(piece_ref=piece_ref):
            piece_ref[...] = rounded


def round_units(values, bounds):
    units = values.shape[0]
    shape = (None,) + values.shape[1:]

    def piece_spec(begin, end):
        return pl.BlockSpec(shape, lambda i: (jnp.clip(i - begin, 0, end - begin - 1), 0, 0, 0))

    return pl.pallas_call(
        functools.partial(round_kernel, bounds),
        grid=(units,),
        in_specs=[pl.BlockSpec(shape, lambda i: (i, 0, 0, 0))],
        out_specs=[pl.BlockSpec(shape, lambda i: (i, 0, 0, 0))]
        + [piece_spec(begin, end) for begin, end in bounds],
        out_shape=[jax.ShapeDtypeStruct(values.shape, jnp.bfloat16)]
        + [
            jax.ShapeDtypeStruct((end - begin,) + values.shape[1:], jnp.bfloat16)
            for begin, end in bounds
        ],
        cost_estimate=SMALL,
        name="round_units",
    )(values)


def attention_backward(length, branch_low, w_output, q2, k2, v, lse, cosine, sine, deps=()):
    rows = branch_low.shape[0]
    kv_here = k2.shape[1] // LANES
    low = jnp.bfloat16
    return pl.pallas_call(
        attention_backward_kernel,
        grid=(kv_here,),
        in_specs=[
            SCALARS,
            whole((rows, D)),
            columns(D, LANES),
            columns(rows, 256),
            columns(rows, LANES),
            columns(rows, LANES),
            pl.BlockSpec((16, rows), lambda h: (h, 0)),
            whole((rows, LANES)),
            whole((rows, LANES)),
        ]
        + [pl.BlockSpec(memory_space=pl.ANY)] * len(deps),
        out_specs=[columns(rows, LANES), columns(rows, LANES)],
        out_shape=[
            jax.ShapeDtypeStruct((rows, kv_here * LANES), low),
            jax.ShapeDtypeStruct((rows, kv_here * LANES), low),
        ],
        scratch_shapes=[pltpu.VMEM((rows, LANES), jnp.float32)] * 3,
        compiler_params=pltpu.CompilerParams(vmem_limit_bytes=50 * MIB),
        cost_estimate=SMALL,
        name="attention_backward",
    )(length, branch_low, w_output, q2, k2, v, lse, cosine, sine, *deps)


CHUNK = 512
UNIT_ROWS = 64


def first_unit(piece_refs, piece):
    return sum(p.shape[0] for p in piece_refs[:piece])


def piece_copy(piece_refs, weights, arrived, piece, kind):
    units = piece_refs[piece].shape[0]
    return pltpu.make_async_copy(
        piece_refs[piece].at[:, kind],
        weights.at[kind, pl.ds(first_unit(piece_refs, piece), units)],
        arrived.at[piece, kind],
    )


def row_copy(row_refs, rows_all, landed, index):
    count = len(row_refs) - 1
    rows = row_refs[0].shape[0]
    source = row_refs[index // 2]
    if index % 2:
        source = row_refs[count].at[pl.ds(index // 2 * rows, rows)]
    return pltpu.make_async_copy(
        source, rows_all.at[pl.ds(index * rows, rows)], landed.at[index]
    )


def fetch(piece_refs, weights, arrived, row_refs=(None,), rows_all=None, landed=None):
    @pl.when(pl.program_id(0) == 0)
    def _():
        copies = [
            row_copy(row_refs, rows_all, landed, index) for index in range(2 * len(row_refs) - 2)
        ]
        copies += [
            piece_copy(piece_refs, weights, arrived, piece, kind)
            for piece in range(len(piece_refs))
            for kind in range(3)
        ]
        for copy in copies:
            copy.start()
        for copy in copies:
            copy.wait()


def chunk_weights(weights, kind, chunk):
    units = CHUNK // UNIT_ROWS
    return weights[kind, chunk * units : (chunk + 1) * units].reshape(CHUNK, D)


def spread_weights(route_ref, column, per_unit):
    rows = route_ref.shape[0]
    units = CHUNK // UNIT_ROWS
    count = units if per_unit else units // 4
    width = CHUNK // count
    pieces = [
        jnp.broadcast_to(route_ref[:, column * count + j : column * count + j + 1], (rows, width))
        for j in range(count)
    ]
    return jnp.concatenate(pieces, axis=1)


def store_step(out_refs, values):
    step = pl.program_id(0)
    for index, out_ref in enumerate(out_refs):

        @pl.when(step == index)
        def _(out_ref=out_ref):
            out_ref[...] = values


def expert_hidden(x, route_ref, weights, first_column, per_unit, outs):
    low = jnp.bfloat16
    slope_ref, silu_ref, inner_ref = outs
    for chunk in range(slope_ref.shape[1] // CHUNK):
        here = slice(chunk * CHUNK, (chunk + 1) * CHUNK)
        gate = dot(x, chunk_weights(weights, 0, chunk), 1, 1)
        upper = dot(x, chunk_weights(weights, 1, chunk), 1, 1)
        sigmoid = 0.5 * jnp.tanh(0.5 * gate) + 0.5
        silu = gate * sigmoid
        weight = spread_weights(route_ref, first_column + chunk, per_unit)
        weighted_upper = weight * upper
        slope_ref[:, here] = (weighted_upper * (sigmoid + silu * (1.0 - sigmoid))).astype(low)
        silu_ref[:, here] = (weight * silu).astype(low)
        inner_ref[:, here] = (silu * weighted_upper).astype(low)
    return dot(inner_ref[...], weights[2].reshape(-1, D), 1, 0)


def expert_first_kernel(count, pieces, per_unit, *refs):
    parts = count // 2 + 1
    row_refs, route_ref = refs[:parts], refs[parts]
    piece_refs = refs[parts + 1 : parts + 1 + pieces]
    x_ref, mixed_ref, slope_ref, silu_ref, inner_ref = refs[-9:-4]
    weights, arrived, rows_all, landed = refs[-4:]
    fetch(piece_refs, weights, arrived, row_refs, rows_all, landed)
    rows = x_ref.shape[0]
    x = rows_all[pl.ds(pl.multiple_of(pl.program_id(0) * rows, rows), rows), :]
    x_ref[...] = x
    outs = (slope_ref, silu_ref, inner_ref)
    mixed_ref[...] = expert_hidden(
        x, route_ref, weights, 0, per_unit, outs
    ).astype(jnp.bfloat16)


def expert_second_kernel(count, pieces, per_unit, first_column, *refs):
    x_ref, mixed_ref, route_ref = refs[:3]
    piece_refs = refs[3 : 3 + pieces]
    out_refs = refs[-5 - count : -5]
    weights, arrived = refs[-2:]
    fetch(piece_refs, weights, arrived)
    part = expert_hidden(
        x_ref[...], route_ref, weights, first_column, per_unit, refs[-5:-2]
    )
    store_step(out_refs, (part + mixed_ref[...].astype(jnp.float32)).astype(jnp.bfloat16))


def expert_backward_kernel(count, pieces, *refs):
    parts = count // 2 + 1
    row_refs = refs[:parts]
    slope_refs, silu_refs = refs[parts : parts + 2], refs[parts + 2 : parts + 4]
    piece_refs = refs[parts + 4 : parts + 4 + pieces]
    out_refs = refs[-9 - count : -9]
    grad_ref = refs[-9]
    gate_refs, upper_refs = refs[-8:-6], refs[-6:-4]
    weights, arrived, rows_all, landed = refs[-4:]
    low = jnp.bfloat16
    fetch(piece_refs, weights, arrived, row_refs, rows_all, landed)
    rows = grad_ref.shape[0]
    grad = rows_all[pl.ds(pl.multiple_of(pl.program_id(0) * rows, rows), rows), :]
    grad_ref[...] = grad
    chunks = slope_refs[0].shape[1] // CHUNK
    for chunk in range(2 * chunks):
        half, place = chunk // chunks, chunk % chunks
        here = slice(place * CHUNK, (place + 1) * CHUNK)
        inner_grad = dot(grad, chunk_weights(weights, 2, chunk), 1, 1)
        slope, silu = slope_refs[half][:, here], silu_refs[half][:, here]
        gate_refs[half][:, here] = (inner_grad * slope.astype(jnp.float32)).astype(low)
        upper_refs[half][:, here] = (inner_grad * silu.astype(jnp.float32)).astype(low)
    units = weights.shape[1] // 2
    total = None
    for half in range(2):
        mine = pl.ds(half * units, units)
        part = dot(gate_refs[half][...], weights[0, mine].reshape(-1, D), 1, 0)
        part = part + dot(upper_refs[half][...], weights[1, mine].reshape(-1, D), 1, 0)
        total = part if total is None else total + part
    store_step(out_refs, total.astype(low))


def fixed(shape):
    return pl.BlockSpec(shape, lambda i: (0,) * len(shape))


def token_block(rows, width, first=0):
    return pl.BlockSpec((rows, width), lambda i: (first + i, 0))


def expert_scratch(pieces, count=0, rows=0):
    units = sum(p.shape[0] for p in pieces)
    scratch = [
        pltpu.VMEM((3, units, UNIT_ROWS, D), jnp.bfloat16),
        pltpu.SemaphoreType.DMA((len(pieces), 3)),
    ]
    if count:
        scratch += [
            pltpu.VMEM((count * rows, D), jnp.bfloat16),
            pltpu.SemaphoreType.DMA((count,)),
        ]
    return scratch


def expert_call(
    kernel, name, steps, operands, specs, out_specs, widths, singles, kept, scratch, estimate=SMALL
):
    rows, total_rows = singles[1], singles[2]
    low = jnp.bfloat16
    operands, specs = list(operands), list(specs)
    aliases = {}
    if kept is not None:
        for index, buffer in enumerate(kept):
            aliases[len(operands)] = singles[0] + index
            operands.append(buffer)
            specs.append(ANYWHERE)
    outs = pl.pallas_call(
        kernel,
        grid=(steps,),
        in_specs=specs,
        out_specs=[fixed((rows, D))] * singles[0] + out_specs,
        out_shape=[jax.ShapeDtypeStruct((rows, D), low)] * singles[0]
        + [jax.ShapeDtypeStruct((total_rows, w), low) for w in widths],
        scratch_shapes=scratch,
        input_output_aliases=aliases,
        compiler_params=pltpu.CompilerParams(vmem_limit_bytes=60 * MIB),
        cost_estimate=estimate,
        name=name,
    )(*operands)
    return outs[: singles[0]], outs[singles[0] :]


def expert_first(row_parts, route_columns, per_unit, pieces, deps):
    count, rows = 2 * len(row_parts) - 2, row_parts[0].shape[0]
    width = sum(p.shape[0] for p in pieces) * UNIT_ROWS
    widths = [D, D, width, width, width]
    return expert_call(
        functools.partial(expert_first_kernel, count, len(pieces), per_unit),
        "expert_first",
        count,
        list(row_parts) + [route_columns] + list(pieces) + list(deps),
        [ANYWHERE] * len(row_parts)
        + [token_block(rows, route_columns.shape[1])]
        + [ANYWHERE] * (len(pieces) + len(deps)),
        [token_block(rows, w) for w in widths],
        widths,
        (0, rows, count * rows),
        None,
        expert_scratch(pieces, count, rows),
        cost(6 * count * rows * width * D),
    )[1]


def expert_second(count, rows, x, mixed, route_columns, per_unit, pieces, deps):
    width = sum(p.shape[0] for p in pieces) * UNIT_ROWS
    return expert_call(
        functools.partial(expert_second_kernel, count, len(pieces), per_unit, width // CHUNK),
        "expert_second",
        count,
        [x, mixed, route_columns] + list(pieces) + list(deps),
        [
            token_block(rows, D),
            token_block(rows, D),
            token_block(rows, route_columns.shape[1]),
        ]
        + [ANYWHERE] * (len(pieces) + len(deps)),
        [token_block(rows, width)] * 3,
        [width] * 3,
        (count, rows, x.shape[0]),
        None,
        expert_scratch(pieces),
    )


def expert_backward(first, row_parts, slopes, silus, pieces, kept):
    count, rows = 2 * len(row_parts) - 2, row_parts[0].shape[0]
    width = slopes[0].shape[1]
    widths = [D] + [width] * 4
    return expert_call(
        functools.partial(expert_backward_kernel, count, len(pieces)),
        "expert_backward",
        count,
        list(row_parts) + list(slopes) + list(silus) + list(pieces),
        [ANYWHERE] * len(row_parts)
        + [token_block(rows, width, first)] * 4
        + [ANYWHERE] * len(pieces),
        [token_block(rows, w, first) for w in widths],
        widths,
        (count, rows, slopes[0].shape[0]),
        kept,
        expert_scratch(pieces, count, rows),
    )


def weight_grad_kernel(count, *refs):
    right_ref = refs[count]
    outs = refs[-2 * count :]
    step = pl.program_id(0)
    for index in range(count):
        for slot in range(2):

            @pl.when(step == 2 * index + slot)
            def _(index=index, slot=slot):
                outs[2 * index + slot][...] = dot(refs[index][...], right_ref[...], 0, 0).astype(
                    jnp.bfloat16
                )


def weight_grads(lefts, right, deps=(), estimate=SMALL):
    rows = right.shape[0]
    columns_here = lefts[0].shape[1] // 2
    count = len(lefts)

    def left_spec(index):
        return pl.BlockSpec(
            (rows, columns_here), lambda i: (0, 1 - jnp.clip(i - 2 * index, 0, 1))
        )

    return pl.pallas_call(
        functools.partial(weight_grad_kernel, count),
        grid=(2 * count,),
        in_specs=[left_spec(index) for index in range(count)]
        + [pl.BlockSpec((rows, D), lambda i: (0, 0), pipeline_mode=pl.Buffered(1))]
        + [ANYWHERE] * len(deps),
        out_specs=[fixed((columns_here, D))] * (2 * count),
        out_shape=[jax.ShapeDtypeStruct((columns_here, D), jnp.bfloat16)] * (2 * count),
        compiler_params=pltpu.CompilerParams(vmem_limit_bytes=56 * MIB),
        cost_estimate=estimate,
        name="weight_grads",
    )(*lefts, right, *deps)


def update_blocks(grads, lefts, rights, left_roots, right_roots, left_outs, right_outs, step_outs):
    low = jnp.bfloat16
    grads = [grad.astype(low) for grad in grads]
    firsts = [
        dot(root[...].astype(low), grad, 1, 0).astype(low) for root, grad in zip(left_roots, grads)
    ]
    for grad, left, out in zip(grads, lefts, left_outs):
        out[...] = stat_decay * left[...] + dot(grad, grad, 1, 1)
    for first, root, (out, master) in zip(firsts, right_roots, step_outs):
        out[...] = master[...] - D ** (-0.5) * dot(first, root[...].astype(low), 1, 0)
    for grad, right, out in zip(grads, rights, right_outs):
        out[...] = stat_decay * right[...] + dot(grad, grad, 0, 0)


def expert_update_kernel(count, *refs):
    parts = refs[:count]
    master, left, right, left_root, right_root = refs[count : count + 5]
    grad_out, left_out, right_out, new_out = refs[-4:]
    units, rows, _ = grad_out.shape
    grad = parts[0][...].astype(jnp.float32)
    for part in parts[1:]:
        grad = grad + part[...].astype(jnp.float32)
    grad = grad.reshape(units, rows, D)
    grad_out[...] = grad
    blocks = [(u, b) for u in range(units) for b in range(D // BLOCK)]

    def wide(ref):
        return [ref.at[u, :, b * BLOCK : (b + 1) * BLOCK] for u, b in blocks]

    def square(ref):
        return [ref.at[u, b] for u, b in blocks]

    update_blocks(
        [grad[u, :, b * BLOCK : (b + 1) * BLOCK] for u, b in blocks],
        square(left),
        square(right),
        square(left_root),
        square(right_root),
        square(left_out),
        square(right_out),
        list(zip(wide(new_out), wide(master))),
    )


def expert_update(kind, parts, state, kept, deps=()):
    master, left, right, left_root, right_root = state
    units, _, rows, _ = master.shape
    step = min(units, 2)
    flat = pl.BlockSpec((step, None, rows, D), lambda i: (i, kind, 0, 0))
    lefts = pl.BlockSpec((step, None) + left.shape[2:], lambda i: (i, kind, 0, 0, 0))
    rights = pl.BlockSpec((step, None) + right.shape[2:], lambda i: (i, kind, 0, 0, 0))
    operands = list(parts) + list(state) + list(deps)
    specs = [pl.BlockSpec((step * rows, D), lambda i: (i, 0))] * len(parts)
    specs += [flat, lefts, rights, lefts, rights] + [ANYWHERE] * len(deps)
    aliases = {}
    if kept is not None:
        for index, buffer in enumerate(kept):
            aliases[len(operands)] = index
            operands.append(buffer)
            specs.append(ANYWHERE)
    return pl.pallas_call(
        functools.partial(expert_update_kernel, len(parts)),
        grid=(units // step,),
        in_specs=specs,
        out_specs=[flat, lefts, rights, flat],
        out_shape=[jax.ShapeDtypeStruct(a.shape, jnp.float32) for a in (master, left, right, master)],
        input_output_aliases=aliases,
        compiler_params=pltpu.CompilerParams(vmem_limit_bytes=56 * MIB),
        cost_estimate=cost(12e9),
        name="expert_update",
    )(*operands)


def attention_update_kernel(qkv_ref, wo_ref, master, left, right, left_root, right_root, *outs):
    grad_out, left_out, right_out, new_out = outs
    heads = qkv_ref.shape[1] // 256
    rows = qkv_ref.shape[0]
    low_lanes = lax.broadcasted_iota(jnp.int32, (rows, LANES), 1) < HEAD_DIM
    grad = qkv_ref[...].astype(jnp.float32)
    queries = heads * LANES
    keys = queries // 2
    for head in range(heads):
        grad_out[:, head * LANES : (head + 1) * LANES] = grad[:, head * 256 : head * 256 + LANES]
    for pair in range(heads // 2):
        begin = pair * 512 + LANES
        one, two = grad[:, begin : begin + LANES], grad[:, begin + 256 : begin + 256 + LANES]
        place = queries + pair * LANES
        grad_out[:, place : place + LANES] = jnp.where(low_lanes, one, pltpu.roll(two, HEAD_DIM, 1))
        place = place + keys
        grad_out[:, place : place + LANES] = jnp.where(low_lanes, pltpu.roll(one, HEAD_DIM, 1), two)
    grad_out[:, queries + 2 * keys :] = wo_ref[...].astype(jnp.float32)
    blocks = range(grad_out.shape[1] // BLOCK)

    def wide(ref):
        return [ref.at[:, b * BLOCK : (b + 1) * BLOCK] for b in blocks]

    def square(ref):
        return [ref.at[b] for b in blocks]

    update_blocks(
        [part[...] for part in wide(grad_out)],
        square(left),
        square(right),
        square(left_root),
        square(right_root),
        square(left_out),
        square(right_out),
        list(zip(wide(new_out), wide(master))),
    )


def attention_update(qkv_part, output_part, state):
    inside = pl.BlockSpec(memory_space=pltpu.VMEM)
    master, left, right = state[:3]
    return pl.pallas_call(
        attention_update_kernel,
        in_specs=[inside] * 7,
        out_specs=[inside] * 4,
        out_shape=[jax.ShapeDtypeStruct(a.shape, jnp.float32) for a in (master, left, right, master)],
        compiler_params=pltpu.CompilerParams(vmem_limit_bytes=40 * MIB),
        cost_estimate=SMALL,
        name="attention_update",
    )(qkv_part, output_part, *state)


def spread_tokens(own, relay):
    beside, across, both = TOKEN_MASKS[1:]
    rows = [own, swap_dp(own, beside), swap_dp(own, across)]
    return rows + [swap_dp(rows[2], beside) if relay else swap_dp(own, both)]


def with_other(own_rows):
    return list(own_rows) + [swap_core(jnp.concatenate(own_rows, axis=0))]


def sum_cores(place, parts):
    own, other = parts
    total = own.astype(jnp.float32) + swap_core(other).astype(jnp.float32)
    return total if place == 0 else total.astype(jnp.bfloat16)


def return_tokens(sums):
    return [swap_dp(rows, mask) for rows, mask in zip(sums[1:], TOKEN_MASKS[1:])]


def add_all(first, others):
    for rows in others:
        first = first + rows.astype(jnp.float32)
    return first


def extra_masks():
    count = lax.axis_size("dp")
    used = sum(WEIGHT_BITS) + TOKEN_MASKS[-1]
    masks = []
    mask = 1
    while mask < count:
        if not mask & used:
            masks.append(mask)
        mask *= 2
    return masks


def gather_attention(own, count, qkv_cols, deps):
    low = jnp.bfloat16
    high_digit = jnp.floor(count / 64.0)
    digits = jnp.stack([high_digit, count - 64.0 * high_digit]).astype(low)
    digits = jnp.pad(digits[None, :], ((0, 7), (0, own.shape[1] - 2)))
    own = jnp.concatenate([own, digits], axis=0)
    slot_rows = own.shape[0]
    masks, line, mask = [0], own, lax.axis_size("dp") // 2
    while mask > 2:
        line = jnp.concatenate([line, swap_dp(line, mask)], axis=0)
        masks = masks + [m ^ mask for m in masks]
        mask //= 2
    line = after(line, *deps)
    inner, outer = line[:, :qkv_cols], line[:, qkv_cols:]
    inner = [inner] + [swap_dp(inner, mask) for mask in (1, 2, 3)]
    outer = [outer] + [swap_dp(outer, mask) for mask in (1, 2, 3)]
    table = jnp.array([[group ^ mask for mask in masks] for group in range(4)], jnp.int32)
    total = 0.0
    for group in inner:
        digits = group.reshape(len(masks), slot_rows, -1)[:, slot_rows - 8, :2]
        digits = jnp.sum(digits.astype(jnp.float32), axis=0)
        total = total + 64.0 * digits[0] + digits[1]
    total = total.reshape(1, 1)
    return line, inner, outer, lax.axis_index("dp") ^ table, (total + swap_core(total))[0, 0]


FAR_PIECES = ((0, 4), (4, 8))
NEAR_PIECES = ((0, 3), (3, 8))


def round_weights(master):
    bounds = FAR_PIECES + NEAR_PIECES
    extra = extra_masks()
    if not extra:
        shard, *pieces = round_units(master, bounds)
    else:
        shard = round_units(master, ())[0]
        for mask in extra:
            shard = jnp.concatenate([shard, swap_dp(shard, mask)], axis=0)
        pieces = [shard[begin:end] for begin, end in bounds]
    return shard, pieces[: len(FAR_PIECES)], pieces[len(FAR_PIECES) :]


def unit_owners():
    masks = [0]
    for mask in extra_masks():
        masks = masks + [m ^ mask for m in masks]
    first, second = WEIGHT_BITS
    masks = [m ^ k for k in (0, first, second, first ^ second) for m in masks]
    return lax.axis_index("dp") ^ jnp.array(masks, jnp.int32)


def add_grads(far, both):
    return (far.astype(jnp.float32) + swap_dp(both, WEIGHT_BITS[0]).astype(jnp.float32)).astype(
        jnp.bfloat16
    )


def grad_terms(own, near, far):
    parts = [own, swap_dp(near, WEIGHT_BITS[0]), far]
    masks = extra_masks()
    if not masks:
        return parts
    total = sum(p.astype(jnp.float32) for p in parts)
    for mask in reversed(masks):
        half = total.shape[0] // 2
        sent = swap_dp(total[half:].astype(jnp.bfloat16), mask)
        total = total[:half] + sent.astype(jnp.float32)
    return [total]


def on_device(
    activations,
    targets,
    lengths,
    token_mask,
    routes,
    route_weights,
    norm_gains,
    attention_master,
    expert_master,
    attention_left,
    attention_right,
    attention_left_root,
    attention_right_root,
    expert_left,
    expert_right,
    expert_left_root,
    expert_right_root,
):
    low = jnp.bfloat16
    own_rows = activations.shape[0]
    tensor_size = lax.axis_size("tensor")
    core = lax.axis_index("tensor")
    tokens_total = own_rows * tensor_size * lax.axis_size("dp")
    seq_length = lengths[0]
    position = core * own_rows + jnp.arange(own_rows, dtype=jnp.int32)
    valid_rows = ((token_mask == 1) & (position < seq_length)).astype(jnp.float32)
    valid_here = jnp.sum(valid_rows)

    routing = jnp.concatenate([routes.T.astype(jnp.float32), route_weights.T], axis=0)
    routing_parts = [routing] + [swap_dp(routing, mask) for mask in TOKEN_MASKS[1:]]
    heads_here = HEADS // tensor_size
    kv_here = KV_HEADS // tensor_size
    query_cols = heads_here * HEAD_DIM
    key_cols = kv_here * HEAD_DIM
    qkv_cols = query_cols + 2 * key_cols
    rows_here = attention_master.shape[0]

    def by_head(values):
        rows = values.shape[0]
        query = values[:, :query_cols].reshape(rows, kv_here, LANES)
        key = values[:, query_cols : query_cols + key_cols].reshape(rows, kv_here, HEAD_DIM)
        value = values[:, query_cols + key_cols : qkv_cols].reshape(rows, kv_here, HEAD_DIM)
        return jnp.concatenate([query, key, value], axis=2).reshape(rows, qkv_cols)

    attention_low = attention_master.astype(low)
    hidden = activations.astype(jnp.float32)
    normed_own, attention_scaling = normalize(hidden, norm_gains[0])
    normed_own = normed_own.astype(low)
    normed = in_order(normed_own, swap_core(normed_own))

    seq_rows = normed.shape[0]
    half_width = HEAD_DIM // 2
    frequency = theta_base ** (-jnp.arange(half_width, dtype=jnp.float32) * 2.0 / HEAD_DIM)
    angles = jnp.arange(seq_rows, dtype=jnp.float32)[:, None] * frequency[None, :]
    cosine = jnp.tile(jnp.cos(angles), (1, LANES // half_width))
    sine = jnp.tile(jnp.sin(angles), (1, LANES // half_width))
    own_columns = jnp.concatenate([by_head(attention_low), attention_low[:, qkv_cols:]], axis=1)
    shard, for_far, for_near = round_weights(expert_master)
    line, w_inner, w_outer, devices, valid_total = gather_attention(
        own_columns,
        valid_here,
        qkv_cols,
        [shard, normed, cosine, sine] + routing_parts[1:],
    )
    starts = devices * rows_here
    near_bit, far_bit = WEIGHT_BITS
    for_near[0] = after(for_near[0], *w_inner[1:])
    near = [swap_dp(piece, near_bit) for piece in for_near]
    far = [swap_dp(after(piece, line), far_bit) for piece in for_far]

    q2, k2, v_high, attended, w_qkv, log_totals = attention_forward(
        lengths,
        starts,
        normed,
        w_inner,
        cosine,
        sine,
    )
    branch, branch_other, w_output = output_projection(
        starts, core.reshape(1).astype(jnp.int32), attended, w_outer, far[:1] + near[:1]
    )
    branch = branch + swap_core(branch_other).astype(jnp.float32)
    middle = hidden + branch
    mix_own, mix_scaling = normalize(middle, norm_gains[1])

    routing = jnp.stack(routing_parts).reshape(len(TOKEN_MASKS), 2 * TOPK, 2, own_rows)
    routing = jnp.stack(
        [
            lax.dynamic_index_in_dim(routing, core, 2, keepdims=False),
            lax.dynamic_index_in_dim(routing, 1 - core, 2, keepdims=False),
        ],
        axis=1,
    )
    unit_here = expert_master.shape[0]
    unit_ids = (unit_owners()[:, None] * unit_here + jnp.arange(unit_here)[None, :]).reshape(-1)
    expert_of = unit_ids // GROUPS
    per_unit = unit_here % 4 != 0
    if not per_unit:
        expert_of = expert_of[::4]
    named = (
        routing[:, :, None, :TOPK] == expert_of.astype(jnp.float32)[None, None, :, None, None]
    )
    route_columns = jnp.sum(jnp.where(named, routing[:, :, None, TOPK:], 0.0), axis=3)
    route_columns = route_columns.transpose(0, 1, 3, 2).reshape(-1, expert_of.shape[0])

    spread = spread_tokens(mix_own.astype(low), True)
    both = [swap_dp(piece, near_bit) for piece in far]
    later = [after(spread[1], far[1], near[1]), spread[2], after(spread[3], both[0])]
    mix_rows = with_other(spread[:1] + later)
    mix, mixed, *firsts = expert_first(
        mix_rows, route_columns, per_unit, [shard] + near, []
    )
    pieces = [shard] + near + far + both
    mixed_parts, seconds = expert_second(
        2 * len(spread), own_rows, mix, mixed, route_columns, per_unit, far + both, []
    )
    slopes, silus, inners = ([firsts[i], seconds[i]] for i in range(3))
    sums = [sum_cores(i, mixed_parts[2 * i : 2 * i + 2]) for i in range(len(TOKEN_MASKS))]
    output = middle + add_all(sums[0], return_tokens(sums))
    residual_error = output - targets
    loss_part = jnp.sum(valid_rows[:, None] * residual_error * residual_error)
    output_grad = 2.0 / valid_total * valid_rows[:, None] * residual_error

    spread = spread_tokens(output_grad.astype(low), False)
    backward = functools.partial(expert_backward, slopes=slopes, silus=silus, pieces=pieces)
    parts0, kept = backward(0, [spread[0], swap_core(spread[0])], kept=None)
    later = [after(rows, parts0[0]) for rows in spread[1:]]
    parts1, kept = backward(2, with_other(later), kept=kept)
    parts = list(parts0) + list(parts1)
    sums = [sum_cores(i, parts[2 * i : 2 * i + 2]) for i in range(len(TOKEN_MASKS))]
    returned = return_tokens(sums)
    output_low = kept[0]
    gates, uppers = kept[1:3], kept[3:5]
    full = cost(30e9)
    down_far = weight_grads([inners[1]], output_low, (), full)
    gate_far = weight_grads([gates[1]], mix, [down_far[0]] + sums[1:], full)
    down_sum = add_grads(down_far[1], down_far[0])
    upper_far = weight_grads([uppers[1]], mix, [gate_far[0], down_sum], full)
    gate_sum = add_grads(gate_far[1], gate_far[0])
    upper_sum = add_grads(upper_far[1], upper_far[0])
    returned[2] = after(returned[2], upper_far[0], gate_sum)
    sent = add_all(sums[0], returned)
    far_gate, far_upper, far_down = (
        swap_dp(rows, far_bit) for rows in (gate_sum, upper_sum, down_sum)
    )
    mix_back, gain_mix = normalize_back(middle, mix_scaling, norm_gains[1], sent)
    middle_grad = output_grad + mix_back
    branch_own = middle_grad.astype(low)
    branch_low = in_order(branch_own, swap_core(branch_own))
    dq, dkv = attention_backward(
        lengths, branch_low, w_output, q2, k2, v_high, log_totals, cosine, sine,
        [upper_far[0], gate_sum],
    )
    qkv_grad = jnp.concatenate(
        [dq.reshape(seq_rows, kv_here, LANES), dkv.reshape(seq_rows, kv_here, LANES)], axis=2
    ).reshape(seq_rows, qkv_cols)
    qkv_part = dot(normed, qkv_grad, 0, 0).astype(low)
    output_part = dot(branch_low, attended, 0, 0).astype(low)
    gate_up_near = weight_grads([gates[0], uppers[0]], mix, [qkv_part, output_part, upper_sum])
    down_near = weight_grads(
        [inners[0]], output_low, [gate_up_near[0], far_down, far_gate]
    )
    qkv_part = lax.psum_scatter(qkv_part, "dp", scatter_dimension=0, tiled=True)
    output_part = lax.psum_scatter(output_part, "dp", scatter_dimension=0, tiled=True)
    normed_grad_other = dot(other_half(qkv_grad), w_qkv, 1, 1).astype(low)
    normed_grad = dot(own_half(qkv_grad), w_qkv, 1, 1)
    normed_grad = normed_grad + swap_core(normed_grad_other).astype(jnp.float32)
    attention_back, gain_attention = normalize_back(
        hidden, attention_scaling, norm_gains[0], normed_grad
    )
    input_grad = middle_grad + attention_back
    parts = {
        2: grad_terms(down_near[1], down_near[0], far_down),
        0: grad_terms(gate_up_near[1], gate_up_near[0], far_gate),
        1: grad_terms(gate_up_near[3], gate_up_near[2], far_upper),
    }
    state = (expert_master, expert_left, expert_right, expert_left_root, expert_right_root)
    updated = expert_update(0, parts[0], state, None, [input_grad])
    updated = expert_update(1, parts[1], state, updated)
    loss_row = jnp.full((1, D), loss_part)
    sums = jnp.concatenate([gain_attention[None], gain_mix[None], loss_row], axis=0)
    sums = sum_everywhere(after(sums, updated[0]))
    updated = expert_update(2, parts[2], state, updated, [sums])
    expert_grad, expert_left_new, expert_right_new, expert_new = updated
    attention_grad, attention_left_new, attention_right_new, attention_new = attention_update(
        qkv_part,
        output_part,
        (
            attention_master,
            attention_left[0],
            attention_right[0],
            attention_left_root[0],
            attention_right_root[0],
        ),
    )
    gain_grad = sums[:2]
    mean_loss = sums[2, 0] / valid_total
    gains_new = norm_gains - gain_rate * tokens_total**0.5 * gain_grad

    return (
        output,
        mean_loss,
        input_grad,
        gain_grad,
        gains_new,
        attention_grad,
        attention_left_new[None],
        attention_right_new[None],
        attention_new,
        expert_grad,
        expert_left_new,
        expert_right_new,
        expert_new,
    )


def solution(mesh):
    return jax.shard_map(
        on_device,
        mesh=mesh,
        in_specs=(
            P(("dp", "tensor"), None),
            P(("dp", "tensor"), None),
            P("dp"),
            P(("dp", "tensor")),
            P("dp", None),
            P("dp", None),
            P(),
            P("dp", "tensor"),
            P("dp", None, "tensor", None),
            P("dp", "tensor", None, None),
            P("dp", "tensor", None, None),
            P("dp", "tensor", None, None),
            P("dp", "tensor", None, None),
            P("dp", None, None, "tensor", None),
            P("dp", None, "tensor", None, None),
            P("dp", None, None, "tensor", None),
            P("dp", None, "tensor", None, None),
        ),
        out_specs=(
            P(("dp", "tensor"), None),
            P(),
            P(("dp", "tensor"), None),
            P(),
            P(),
            P("dp", "tensor"),
            P("dp", "tensor", None, None),
            P("dp", "tensor", None, None),
            P("dp", "tensor"),
            P("dp", None, "tensor", None),
            P("dp", None, None, "tensor", None),
            P("dp", None, "tensor", None, None),
            P("dp", None, "tensor", None),
        ),
        check_vma=False,
    )
```

```python
import functools

import jax
import jax.numpy as jnp
from jax import lax
from jax.experimental import pallas as pl
from jax.experimental.pallas import tpu as pltpu
from jax.sharding import PartitionSpec as P

D = 1024
HEADS = 16
KV_HEADS = 8
HEAD_DIM = 64
EXPERTS = 32
TOPK = 8
BLK = 256
GROUPS = 4
BLOCK = 256
LANES = 128

epsilon = 1e-05
stat_decay = 0.9
gain_rate = 0.02
theta_base = 10000.0
masked_score = -1e30
MIB = 1 << 20
SMALL = pl.CostEstimate(flops=1000, bytes_accessed=1000, transcendentals=0)


def cost(flops):
    return pl.CostEstimate(flops=int(flops), bytes_accessed=1000, transcendentals=0)


ANYWHERE = pl.BlockSpec(memory_space=pl.ANY)
SCALARS = pl.BlockSpec(memory_space=pltpu.SMEM)

TOKEN_MASKS = (0, 1, 4, 5)
WEIGHT_BITS = (2, 8)


def dot(left, right, left_dim, right_dim):
    return lax.dot_general(
        left, right, (((left_dim,), (right_dim,)), ((), ())), preferred_element_type=jnp.float32
    )


def normalize(hidden, gain):
    scaling = lax.rsqrt(jnp.mean(hidden * hidden, axis=-1, keepdims=True) + epsilon)
    return (hidden * scaling * gain, scaling)


def normalize_back(hidden, scaling, gain, upstream):
    weighted = upstream * gain
    center = jnp.mean(weighted * hidden, axis=-1, keepdims=True)
    input_part = scaling * weighted - hidden * (scaling * scaling * scaling) * center
    return (input_part, jnp.sum(upstream * hidden * scaling, axis=0))


def swap_dp(values, mask):
    count = lax.axis_size("dp")
    return lax.ppermute(values, "dp", [(i, i ^ mask) for i in range(count)])


def swap_core(values):
    count = lax.axis_size("tensor")
    return lax.ppermute(values, "tensor", [(i, i ^ 1) for i in range(count)])


def sum_everywhere(values):
    values = values + swap_core(values)
    own = sum(values if mask == 0 else swap_dp(values, mask) for mask in TOKEN_MASKS)
    masks = [m for m in range(1, lax.axis_size("dp")) if not m & TOKEN_MASKS[-1]]
    return own + sum(swap_dp(own, mask) for mask in masks)


def in_order(own, other):
    first = lax.axis_index("tensor") == 0
    return jnp.concatenate([jnp.where(first, own, other), jnp.where(first, other, own)], axis=0)


def own_half(values):
    half = values.shape[0] // 2
    return lax.dynamic_slice_in_dim(values, lax.axis_index("tensor") * half, half, 0)


def other_half(values):
    half = values.shape[0] // 2
    return lax.dynamic_slice_in_dim(values, (1 - lax.axis_index("tensor")) * half, half, 0)


def turn(values):
    lane = lax.broadcasted_iota(jnp.int32, values.shape, 1)
    half = HEAD_DIM // 2
    return jnp.where(
        lane % HEAD_DIM < half,
        -pltpu.roll(values, LANES - half, 1),
        pltpu.roll(values, half, 1),
    )


def place_rows(starts_ref, source_refs, target_ref):
    for group, source_ref in enumerate(source_refs):
        count = starts_ref.shape[1]
        slot_rows = source_ref.shape[0] // count
        rows = target_ref.shape[0] // count // len(source_refs)
        for slot in range(count):
            start = pl.multiple_of(starts_ref[group, slot], rows)
            begin = slot * slot_rows
            target_ref[pl.ds(start, rows), :] = source_ref[begin : begin + rows, :]


def attention_forward_kernel(*refs):
    length_ref, starts_ref, x_ref, w0_ref, w1_ref, w2_ref, w3_ref, cos_ref, sin_ref = refs[:9]
    q_ref, k_ref, v_ref, att_ref, w_ref, lse_ref = refs[-6:]
    rows = x_ref.shape[0]
    place_rows(starts_ref, (w0_ref, w1_ref, w2_ref, w3_ref), w_ref)
    low = jnp.bfloat16
    cosine, sine = cos_ref[...], sin_ref[...]
    lane = lax.broadcasted_iota(jnp.int32, (rows, LANES), 1)
    left = lane < HEAD_DIM
    projected = dot(x_ref[...], w_ref[...], 1, 0)
    q_raw = projected[:, :LANES]
    q_turn = turn(q_raw)
    scale = HEAD_DIM ** (-0.5)
    q_rot = (q_raw * cosine + q_turn * sine) * scale
    q_rot_turn = (q_turn * cosine - q_raw * sine) * scale
    q_ref[:, :LANES] = jnp.where(left, q_rot, pltpu.roll(q_rot_turn, HEAD_DIM, 1)).astype(low)
    q_ref[:, LANES:] = jnp.where(left, pltpu.roll(q_rot, HEAD_DIM, 1), q_rot_turn).astype(low)
    kv_raw = projected[:, LANES:]
    k_turn = turn(kv_raw)
    k_rot = kv_raw * cosine + k_turn * sine
    k_rot_turn = k_turn * cosine - kv_raw * sine
    k_ref[...] = jnp.where(left, k_rot, pltpu.roll(k_rot_turn, HEAD_DIM, 1)).astype(low)
    v_high = jnp.where(left, 0.0, kv_raw)
    v_ref[...] = v_high.astype(low)
    v_low = pltpu.roll(v_high, HEAD_DIM, 1).astype(low)
    v_high = v_high.astype(low)
    k_only = jnp.where(left, k_rot, 0.0).astype(low)
    place = lax.broadcasted_iota(jnp.int32, (1, rows), 1)
    bias = jnp.where(place < length_ref[0], 0.0, masked_score)
    for block in range(rows // BLK):
        here = pl.ds(block * BLK, BLK)
        keys = (block + 1) * BLK
        total = None
        for head in range(2):
            q_block = q_ref[here, head * LANES : (head + 1) * LANES]
            scores = dot(q_block, k_only[:keys], 1, 1) + bias[:, :keys]
            top = jnp.max(scores, axis=1, keepdims=True)
            exponent = jnp.exp(scores - top)
            denominator = jnp.sum(exponent, axis=1, keepdims=True)
            weights = (exponent * (1.0 / denominator)).astype(low)
            value = v_high if head else v_low
            part = dot(weights, value[:keys], 1, 0)
            total = part if total is None else total + part
            log_total = jnp.broadcast_to(top + jnp.log(denominator), (BLK, LANES))
            lse_ref[head * 8 : (head + 1) * 8, here] = log_total.T[:8]
        att_ref[here, :] = total.astype(low)


def attention_backward_kernel(*refs):
    length_ref, branch_ref, wo_ref, q_ref, k_ref, v_ref, lse_ref, cos_ref, sin_ref = refs[:9]
    dq_ref, dkv_ref, dk_sum, d0_sum, d1_sum = refs[-5:]
    rows = branch_ref.shape[0]
    low = jnp.bfloat16
    lane = lax.broadcasted_iota(jnp.int32, (rows, LANES), 1)
    left = lane < HEAD_DIM
    grad = dot(branch_ref[...], wo_ref[...], 1, 0).astype(low)
    k_only = jnp.where(left, k_ref[...].astype(jnp.float32), 0.0).astype(low)
    v_high = v_ref[...]
    v_low = pltpu.roll(v_high.astype(jnp.float32), HEAD_DIM, 1).astype(low)
    place = lax.broadcasted_iota(jnp.int32, (rows, BLK), 0)
    seen = place < length_ref[0]
    dk_sum[...] = jnp.zeros_like(dk_sum)
    d0_sum[...] = jnp.zeros_like(d0_sum)
    d1_sum[...] = jnp.zeros_like(d1_sum)
    scale = HEAD_DIM ** (-0.5)
    for block in range(rows // BLK):
        here = pl.ds(block * BLK, BLK)
        keys = (block + 1) * BLK
        grad_block = grad[block * BLK : keys]
        query_grads = []
        for head in range(2):
            q_block = q_ref[here, head * LANES : (head + 1) * LANES]
            value = v_high if head else v_low
            scores = dot(k_only[:keys], q_block, 1, 1)
            log_total = lse_ref[head * 8 : head * 8 + 1, here]
            scores = jnp.where(seen[:keys], scores, masked_score)
            probability = jnp.exp(scores - log_total)
            prob_grad = dot(value[:keys], grad_block, 1, 1)
            weighted = probability * prob_grad
            center = jnp.sum(weighted, axis=0, keepdims=True)
            score_grad = (weighted - probability * center).astype(low)
            d_sum = d1_sum if head else d0_sum
            d_sum[:keys] += dot(probability.astype(low), grad_block, 1, 0)
            dk_sum[:keys] += dot(score_grad, q_block, 1, 0)
            query_grads.append(dot(score_grad, k_ref[:keys], 0, 0))
        cosine, sine = cos_ref[here, :] * scale, sin_ref[here, :] * scale
        zero, one = query_grads
        left_here = left[:BLK]
        straight = jnp.where(left_here, zero, pltpu.roll(one, HEAD_DIM, 1))
        turned = jnp.where(left_here, pltpu.roll(zero, HEAD_DIM, 1), one)
        dq_ref[here, :] = (straight * cosine - turned * sine).astype(low)
    dk_all = dk_sum[...]
    dk_rot = dk_all * cos_ref[...] - pltpu.roll(dk_all, HEAD_DIM, 1) * sin_ref[...]
    dv_all = pltpu.roll(d0_sum[...], HEAD_DIM, 1) + d1_sum[...]
    dkv_ref[...] = jnp.where(left, dk_rot, dv_all).astype(low)


def whole(shape):
    return pl.BlockSpec(shape, lambda h: (0,) * len(shape))


def columns(rows, width):
    return pl.BlockSpec((rows, width), lambda h: (0, h))


def attention_forward(length, starts, normed, w_groups, cosine, sine, deps=()):
    rows = normed.shape[0]
    kv_here = w_groups[0].shape[1] // 256
    low = jnp.bfloat16
    return pl.pallas_call(
        attention_forward_kernel,
        grid=(kv_here,),
        in_specs=[SCALARS, SCALARS, whole((rows, D))]
        + [columns(w.shape[0], 256) for w in w_groups]
        + [whole((rows, LANES))] * 2
        + [ANYWHERE] * len(deps),
        out_specs=[
            columns(rows, 256),
            columns(rows, LANES),
            columns(rows, LANES),
            columns(rows, LANES),
            columns(D, 256),
            pl.BlockSpec((16, rows), lambda h: (h, 0)),
        ],
        out_shape=[
            jax.ShapeDtypeStruct((rows, kv_here * 256), low),
            jax.ShapeDtypeStruct((rows, kv_here * LANES), low),
            jax.ShapeDtypeStruct((rows, kv_here * LANES), low),
            jax.ShapeDtypeStruct((rows, kv_here * LANES), low),
            jax.ShapeDtypeStruct((D, kv_here * 256), low),
            jax.ShapeDtypeStruct((kv_here * 16, rows), jnp.float32),
        ],
        compiler_params=pltpu.CompilerParams(vmem_limit_bytes=50 * MIB),
        cost_estimate=SMALL,
        name="attention_forward",
    )(length, starts, normed, *w_groups, cosine, sine, *deps)


def output_projection_kernel(*refs):
    starts_ref, core_ref, att_ref, w0_ref, w1_ref, w2_ref, w3_ref = refs[:7]
    own_ref, other_ref, w_ref = refs[-3:]
    place_rows(starts_ref, (w0_ref, w1_ref, w2_ref, w3_ref), w_ref)
    half = own_ref.shape[0]
    mine = pl.multiple_of(core_ref[0] * half, half)
    others = pl.multiple_of((1 - core_ref[0]) * half, half)
    other_ref[...] = dot(att_ref[pl.ds(others, half), :], w_ref[...], 1, 1).astype(jnp.bfloat16)
    own_ref[...] = dot(att_ref[pl.ds(mine, half), :], w_ref[...], 1, 1)


def output_projection(starts, core, attended, w_groups, deps=()):
    rows, width = attended.shape
    inside = pl.BlockSpec(memory_space=pltpu.VMEM)
    return pl.pallas_call(
        output_projection_kernel,
        in_specs=[SCALARS, SCALARS] + [inside] * 5 + [ANYWHERE] * len(deps),
        out_specs=[inside] * 3,
        out_shape=[
            jax.ShapeDtypeStruct((rows // 2, D), jnp.float32),
            jax.ShapeDtypeStruct((rows // 2, D), jnp.bfloat16),
            jax.ShapeDtypeStruct((D, width), jnp.bfloat16),
        ],
        compiler_params=pltpu.CompilerParams(vmem_limit_bytes=32 * MIB),
        cost_estimate=SMALL,
        name="output_projection",
    )(starts, core, attended, *w_groups, *deps)


def nothing(*refs):
    return None


def after(values, *deps):
    return pl.pallas_call(
        nothing,
        in_specs=[ANYWHERE] * (1 + len(deps)),
        out_specs=ANYWHERE,
        out_shape=jax.ShapeDtypeStruct(values.shape, values.dtype),
        input_output_aliases={0: 0},
        cost_estimate=SMALL,
        name="after",
    )(values, *deps)


def round_kernel(bounds, values_ref, whole_ref, *piece_refs):
    step = pl.program_id(0)
    rounded = values_ref[...].astype(jnp.bfloat16)
    whole_ref[...] = rounded
    for (begin, end), piece_ref in zip(bounds, piece_refs):

        @pl.when((step >= begin) & (step < end))
        def _(piece_ref=piece_ref):
            piece_ref[...] = rounded


def round_units(values, bounds):
    units = values.shape[0]
    shape = (None,) + values.shape[1:]

    def piece_spec(begin, end):
        return pl.BlockSpec(shape, lambda i: (jnp.clip(i - begin, 0, end - begin - 1), 0, 0, 0))

    return pl.pallas_call(
        functools.partial(round_kernel, bounds),
        grid=(units,),
        in_specs=[pl.BlockSpec(shape, lambda i: (i, 0, 0, 0))],
        out_specs=[pl.BlockSpec(shape, lambda i: (i, 0, 0, 0))]
        + [piece_spec(begin, end) for begin, end in bounds],
        out_shape=[jax.ShapeDtypeStruct(values.shape, jnp.bfloat16)]
        + [
            jax.ShapeDtypeStruct((end - begin,) + values.shape[1:], jnp.bfloat16)
            for begin, end in bounds
        ],
        cost_estimate=SMALL,
        name="round_units",
    )(values)


def attention_backward(length, branch_low, w_output, q2, k2, v, lse, cosine, sine, deps=()):
    rows = branch_low.shape[0]
    kv_here = k2.shape[1] // LANES
    low = jnp.bfloat16
    return pl.pallas_call(
        attention_backward_kernel,
        grid=(kv_here,),
        in_specs=[
            SCALARS,
            whole((rows, D)),
            columns(D, LANES),
            columns(rows, 256),
            columns(rows, LANES),
            columns(rows, LANES),
            pl.BlockSpec((16, rows), lambda h: (h, 0)),
            whole((rows, LANES)),
            whole((rows, LANES)),
        ]
        + [pl.BlockSpec(memory_space=pl.ANY)] * len(deps),
        out_specs=[columns(rows, LANES), columns(rows, LANES)],
        out_shape=[
            jax.ShapeDtypeStruct((rows, kv_here * LANES), low),
            jax.ShapeDtypeStruct((rows, kv_here * LANES), low),
        ],
        scratch_shapes=[pltpu.VMEM((rows, LANES), jnp.float32)] * 3,
        compiler_params=pltpu.CompilerParams(vmem_limit_bytes=50 * MIB),
        cost_estimate=SMALL,
        name="attention_backward",
    )(length, branch_low, w_output, q2, k2, v, lse, cosine, sine, *deps)


CHUNK = 512
UNIT_ROWS = 64


def first_unit(piece_refs, piece):
    return sum(p.shape[0] for p in piece_refs[:piece])


def piece_copy(piece_refs, weights, arrived, piece, kind):
    units = piece_refs[piece].shape[0]
    return pltpu.make_async_copy(
        piece_refs[piece].at[:, kind],
        weights.at[kind, pl.ds(first_unit(piece_refs, piece), units)],
        arrived.at[piece, kind],
    )


def row_copy(row_refs, rows_all, landed, index):
    count = len(row_refs) - 1
    rows = row_refs[0].shape[0]
    source = row_refs[index // 2]
    if index % 2:
        source = row_refs[count].at[pl.ds(index // 2 * rows, rows)]
    return pltpu.make_async_copy(
        source, rows_all.at[pl.ds(index * rows, rows)], landed.at[index]
    )


def fetch(piece_refs, weights, arrived, row_refs=(None,), rows_all=None, landed=None):
    @pl.when(pl.program_id(0) == 0)
    def _():
        copies = [
            row_copy(row_refs, rows_all, landed, index) for index in range(2 * len(row_refs) - 2)
        ]
        copies += [
            piece_copy(piece_refs, weights, arrived, piece, kind)
            for piece in range(len(piece_refs))
            for kind in range(3)
        ]
        for copy in copies:
            copy.start()
        for copy in copies:
            copy.wait()


def chunk_weights(weights, kind, chunk):
    units = CHUNK // UNIT_ROWS
    return weights[kind, chunk * units : (chunk + 1) * units].reshape(CHUNK, D)


def spread_weights(route_ref, column, per_unit):
    rows = route_ref.shape[0]
    units = CHUNK // UNIT_ROWS
    count = units if per_unit else units // 4
    width = CHUNK // count
    pieces = [
        jnp.broadcast_to(route_ref[:, column * count + j : column * count + j + 1], (rows, width))
        for j in range(count)
    ]
    return jnp.concatenate(pieces, axis=1)


def store_step(out_refs, values):
    step = pl.program_id(0)
    for index, out_ref in enumerate(out_refs):

        @pl.when(step == index)
        def _(out_ref=out_ref):
            out_ref[...] = values


def expert_hidden(x, route_ref, weights, first_column, per_unit, outs):
    low = jnp.bfloat16
    slope_ref, silu_ref, inner_ref = outs
    for chunk in range(slope_ref.shape[1] // CHUNK):
        here = slice(chunk * CHUNK, (chunk + 1) * CHUNK)
        gate = dot(x, chunk_weights(weights, 0, chunk), 1, 1)
        upper = dot(x, chunk_weights(weights, 1, chunk), 1, 1)
        sigmoid = 0.5 * jnp.tanh(0.5 * gate) + 0.5
        silu = gate * sigmoid
        weight = spread_weights(route_ref, first_column + chunk, per_unit)
        weighted_upper = weight * upper
        slope_ref[:, here] = (weighted_upper * (sigmoid + silu * (1.0 - sigmoid))).astype(low)
        silu_ref[:, here] = (weight * silu).astype(low)
        inner_ref[:, here] = (silu * weighted_upper).astype(low)
    return dot(inner_ref[...], weights[2].reshape(-1, D), 1, 0)


def expert_first_kernel(count, pieces, per_unit, *refs):
    parts = count // 2 + 1
    row_refs, route_ref = refs[:parts], refs[parts]
    piece_refs = refs[parts + 1 : parts + 1 + pieces]
    x_ref, mixed_ref, slope_ref, silu_ref, inner_ref = refs[-9:-4]
    weights, arrived, rows_all, landed = refs[-4:]
    fetch(piece_refs, weights, arrived, row_refs, rows_all, landed)
    rows = x_ref.shape[0]
    x = rows_all[pl.ds(pl.multiple_of(pl.program_id(0) * rows, rows), rows), :]
    x_ref[...] = x
    outs = (slope_ref, silu_ref, inner_ref)
    mixed_ref[...] = expert_hidden(
        x, route_ref, weights, 0, per_unit, outs
    ).astype(jnp.bfloat16)


def expert_second_kernel(count, pieces, per_unit, first_column, *refs):
    x_ref, mixed_ref, route_ref = refs[:3]
    piece_refs = refs[3 : 3 + pieces]
    out_refs = refs[-5 - count : -5]
    weights, arrived = refs[-2:]
    fetch(piece_refs, weights, arrived)
    part = expert_hidden(
        x_ref[...], route_ref, weights, first_column, per_unit, refs[-5:-2]
    )
    store_step(out_refs, (part + mixed_ref[...].astype(jnp.float32)).astype(jnp.bfloat16))


def expert_backward_kernel(count, pieces, *refs):
    parts = count // 2 + 1
    row_refs = refs[:parts]
    slope_refs, silu_refs = refs[parts : parts + 2], refs[parts + 2 : parts + 4]
    piece_refs = refs[parts + 4 : parts + 4 + pieces]
    out_refs = refs[-9 - count : -9]
    grad_ref = refs[-9]
    gate_refs, upper_refs = refs[-8:-6], refs[-6:-4]
    weights, arrived, rows_all, landed = refs[-4:]
    low = jnp.bfloat16
    fetch(piece_refs, weights, arrived, row_refs, rows_all, landed)
    rows = grad_ref.shape[0]
    grad = rows_all[pl.ds(pl.multiple_of(pl.program_id(0) * rows, rows), rows), :]
    grad_ref[...] = grad
    chunks = slope_refs[0].shape[1] // CHUNK
    for chunk in range(2 * chunks):
        half, place = chunk // chunks, chunk % chunks
        here = slice(place * CHUNK, (place + 1) * CHUNK)
        inner_grad = dot(grad, chunk_weights(weights, 2, chunk), 1, 1)
        slope, silu = slope_refs[half][:, here], silu_refs[half][:, here]
        gate_refs[half][:, here] = (inner_grad * slope.astype(jnp.float32)).astype(low)
        upper_refs[half][:, here] = (inner_grad * silu.astype(jnp.float32)).astype(low)
    units = weights.shape[1] // 2
    total = None
    for half in range(2):
        mine = pl.ds(half * units, units)
        part = dot(gate_refs[half][...], weights[0, mine].reshape(-1, D), 1, 0)
        part = part + dot(upper_refs[half][...], weights[1, mine].reshape(-1, D), 1, 0)
        total = part if total is None else total + part
    store_step(out_refs, total.astype(low))


def fixed(shape):
    return pl.BlockSpec(shape, lambda i: (0,) * len(shape))


def token_block(rows, width, first=0):
    return pl.BlockSpec((rows, width), lambda i: (first + i, 0))


def expert_scratch(pieces, count=0, rows=0):
    units = sum(p.shape[0] for p in pieces)
    scratch = [
        pltpu.VMEM((3, units, UNIT_ROWS, D), jnp.bfloat16),
        pltpu.SemaphoreType.DMA((len(pieces), 3)),
    ]
    if count:
        scratch += [
            pltpu.VMEM((count * rows, D), jnp.bfloat16),
            pltpu.SemaphoreType.DMA((count,)),
        ]
    return scratch


def expert_call(
    kernel, name, steps, operands, specs, out_specs, widths, singles, kept, scratch, estimate=SMALL
):
    rows, total_rows = singles[1], singles[2]
    low = jnp.bfloat16
    operands, specs = list(operands), list(specs)
    aliases = {}
    if kept is not None:
        for index, buffer in enumerate(kept):
            aliases[len(operands)] = singles[0] + index
            operands.append(buffer)
            specs.append(ANYWHERE)
    outs = pl.pallas_call(
        kernel,
        grid=(steps,),
        in_specs=specs,
        out_specs=[fixed((rows, D))] * singles[0] + out_specs,
        out_shape=[jax.ShapeDtypeStruct((rows, D), low)] * singles[0]
        + [jax.ShapeDtypeStruct((total_rows, w), low) for w in widths],
        scratch_shapes=scratch,
        input_output_aliases=aliases,
        compiler_params=pltpu.CompilerParams(vmem_limit_bytes=60 * MIB),
        cost_estimate=estimate,
        name=name,
    )(*operands)
    return outs[: singles[0]], outs[singles[0] :]


def expert_first(row_parts, route_columns, per_unit, pieces, deps):
    count, rows = 2 * len(row_parts) - 2, row_parts[0].shape[0]
    width = sum(p.shape[0] for p in pieces) * UNIT_ROWS
    widths = [D, D, width, width, width]
    return expert_call(
        functools.partial(expert_first_kernel, count, len(pieces), per_unit),
        "expert_first",
        count,
        list(row_parts) + [route_columns] + list(pieces) + list(deps),
        [ANYWHERE] * len(row_parts)
        + [token_block(rows, route_columns.shape[1])]
        + [ANYWHERE] * (len(pieces) + len(deps)),
        [token_block(rows, w) for w in widths],
        widths,
        (0, rows, count * rows),
        None,
        expert_scratch(pieces, count, rows),
        cost(6 * count * rows * width * D),
    )[1]


def expert_second(count, rows, x, mixed, route_columns, per_unit, pieces, deps):
    width = sum(p.shape[0] for p in pieces) * UNIT_ROWS
    return expert_call(
        functools.partial(expert_second_kernel, count, len(pieces), per_unit, width // CHUNK),
        "expert_second",
        count,
        [x, mixed, route_columns] + list(pieces) + list(deps),
        [
            token_block(rows, D),
            token_block(rows, D),
            token_block(rows, route_columns.shape[1]),
        ]
        + [ANYWHERE] * (len(pieces) + len(deps)),
        [token_block(rows, width)] * 3,
        [width] * 3,
        (count, rows, x.shape[0]),
        None,
        expert_scratch(pieces),
    )


def expert_backward(first, row_parts, slopes, silus, pieces, kept):
    count, rows = 2 * len(row_parts) - 2, row_parts[0].shape[0]
    width = slopes[0].shape[1]
    widths = [D] + [width] * 4
    return expert_call(
        functools.partial(expert_backward_kernel, count, len(pieces)),
        "expert_backward",
        count,
        list(row_parts) + list(slopes) + list(silus) + list(pieces),
        [ANYWHERE] * len(row_parts)
        + [token_block(rows, width, first)] * 4
        + [ANYWHERE] * len(pieces),
        [token_block(rows, w, first) for w in widths],
        widths,
        (count, rows, slopes[0].shape[0]),
        kept,
        expert_scratch(pieces, count, rows),
    )


def weight_grad_kernel(count, *refs):
    right_ref = refs[count]
    outs = refs[-2 * count :]
    step = pl.program_id(0)
    for index in range(count):
        for slot in range(2):

            @pl.when(step == 2 * index + slot)
            def _(index=index, slot=slot):
                outs[2 * index + slot][...] = dot(refs[index][...], right_ref[...], 0, 0).astype(
                    jnp.bfloat16
                )


def weight_grads(lefts, right, deps=(), estimate=SMALL):
    rows = right.shape[0]
    columns_here = lefts[0].shape[1] // 2
    count = len(lefts)

    def left_spec(index):
        return pl.BlockSpec(
            (rows, columns_here), lambda i: (0, 1 - jnp.clip(i - 2 * index, 0, 1))
        )

    return pl.pallas_call(
        functools.partial(weight_grad_kernel, count),
        grid=(2 * count,),
        in_specs=[left_spec(index) for index in range(count)]
        + [pl.BlockSpec((rows, D), lambda i: (0, 0), pipeline_mode=pl.Buffered(1))]
        + [ANYWHERE] * len(deps),
        out_specs=[fixed((columns_here, D))] * (2 * count),
        out_shape=[jax.ShapeDtypeStruct((columns_here, D), jnp.bfloat16)] * (2 * count),
        compiler_params=pltpu.CompilerParams(vmem_limit_bytes=56 * MIB),
        cost_estimate=estimate,
        name="weight_grads",
    )(*lefts, right, *deps)


def update_blocks(grads, lefts, rights, left_roots, right_roots, left_outs, right_outs, step_outs):
    low = jnp.bfloat16
    grads = [grad.astype(low) for grad in grads]
    firsts = [
        dot(root[...].astype(low), grad, 1, 0).astype(low) for root, grad in zip(left_roots, grads)
    ]
    for grad, left, out in zip(grads, lefts, left_outs):
        out[...] = stat_decay * left[...] + dot(grad, grad, 1, 1)
    for first, root, (out, master) in zip(firsts, right_roots, step_outs):
        out[...] = master[...] - D ** (-0.5) * dot(first, root[...].astype(low), 1, 0)
    for grad, right, out in zip(grads, rights, right_outs):
        out[...] = stat_decay * right[...] + dot(grad, grad, 0, 0)


def expert_update_kernel(count, *refs):
    parts = refs[:count]
    master, left, right, left_root, right_root = refs[count : count + 5]
    grad_out, left_out, right_out, new_out = refs[-4:]
    units, rows, _ = grad_out.shape
    grad = parts[0][...].astype(jnp.float32)
    for part in parts[1:]:
        grad = grad + part[...].astype(jnp.float32)
    grad = grad.reshape(units, rows, D)
    grad_out[...] = grad
    blocks = [(u, b) for u in range(units) for b in range(D // BLOCK)]

    def wide(ref):
        return [ref.at[u, :, b * BLOCK : (b + 1) * BLOCK] for u, b in blocks]

    def square(ref):
        return [ref.at[u, b] for u, b in blocks]

    update_blocks(
        [grad[u, :, b * BLOCK : (b + 1) * BLOCK] for u, b in blocks],
        square(left),
        square(right),
        square(left_root),
        square(right_root),
        square(left_out),
        square(right_out),
        list(zip(wide(new_out), wide(master))),
    )


def expert_update(kind, parts, state, kept, deps=()):
    master, left, right, left_root, right_root = state
    units, _, rows, _ = master.shape
    step = min(units, 2)
    flat = pl.BlockSpec((step, None, rows, D), lambda i: (i, kind, 0, 0))
    lefts = pl.BlockSpec((step, None) + left.shape[2:], lambda i: (i, kind, 0, 0, 0))
    rights = pl.BlockSpec((step, None) + right.shape[2:], lambda i: (i, kind, 0, 0, 0))
    operands = list(parts) + list(state) + list(deps)
    specs = [pl.BlockSpec((step * rows, D), lambda i: (i, 0))] * len(parts)
    specs += [flat, lefts, rights, lefts, rights] + [ANYWHERE] * len(deps)
    aliases = {}
    if kept is not None:
        for index, buffer in enumerate(kept):
            aliases[len(operands)] = index
            operands.append(buffer)
            specs.append(ANYWHERE)
    return pl.pallas_call(
        functools.partial(expert_update_kernel, len(parts)),
        grid=(units // step,),
        in_specs=specs,
        out_specs=[flat, lefts, rights, flat],
        out_shape=[jax.ShapeDtypeStruct(a.shape, jnp.float32) for a in (master, left, right, master)],
        input_output_aliases=aliases,
        compiler_params=pltpu.CompilerParams(vmem_limit_bytes=56 * MIB),
        cost_estimate=cost(12e9),
        name="expert_update",
    )(*operands)


def attention_update_kernel(qkv_ref, wo_ref, master, left, right, left_root, right_root, *outs):
    grad_out, left_out, right_out, new_out = outs
    heads = qkv_ref.shape[1] // 256
    rows = qkv_ref.shape[0]
    low_lanes = lax.broadcasted_iota(jnp.int32, (rows, LANES), 1) < HEAD_DIM
    grad = qkv_ref[...].astype(jnp.float32)
    queries = heads * LANES
    keys = queries // 2
    for head in range(heads):
        grad_out[:, head * LANES : (head + 1) * LANES] = grad[:, head * 256 : head * 256 + LANES]
    for pair in range(heads // 2):
        begin = pair * 512 + LANES
        one, two = grad[:, begin : begin + LANES], grad[:, begin + 256 : begin + 256 + LANES]
        place = queries + pair * LANES
        grad_out[:, place : place + LANES] = jnp.where(low_lanes, one, pltpu.roll(two, HEAD_DIM, 1))
        place = place + keys
        grad_out[:, place : place + LANES] = jnp.where(low_lanes, pltpu.roll(one, HEAD_DIM, 1), two)
    grad_out[:, queries + 2 * keys :] = wo_ref[...].astype(jnp.float32)
    blocks = range(grad_out.shape[1] // BLOCK)

    def wide(ref):
        return [ref.at[:, b * BLOCK : (b + 1) * BLOCK] for b in blocks]

    def square(ref):
        return [ref.at[b] for b in blocks]

    update_blocks(
        [part[...] for part in wide(grad_out)],
        square(left),
        square(right),
        square(left_root),
        square(right_root),
        square(left_out),
        square(right_out),
        list(zip(wide(new_out), wide(master))),
    )


def attention_update(qkv_part, output_part, state):
    inside = pl.BlockSpec(memory_space=pltpu.VMEM)
    master, left, right = state[:3]
    return pl.pallas_call(
        attention_update_kernel,
        in_specs=[inside] * 7,
        out_specs=[inside] * 4,
        out_shape=[jax.ShapeDtypeStruct(a.shape, jnp.float32) for a in (master, left, right, master)],
        compiler_params=pltpu.CompilerParams(vmem_limit_bytes=40 * MIB),
        cost_estimate=SMALL,
        name="attention_update",
    )(qkv_part, output_part, *state)


def spread_tokens(own, relay):
    beside, across, both = TOKEN_MASKS[1:]
    rows = [own, swap_dp(own, beside), swap_dp(own, across)]
    return rows + [swap_dp(rows[2], beside) if relay else swap_dp(own, both)]


def with_other(own_rows):
    return list(own_rows) + [swap_core(jnp.concatenate(own_rows, axis=0))]


def sum_cores(place, parts):
    own, other = parts
    total = own.astype(jnp.float32) + swap_core(other).astype(jnp.float32)
    return total if place == 0 else total.astype(jnp.bfloat16)


def return_tokens(sums):
    return [swap_dp(rows, mask) for rows, mask in zip(sums[1:], TOKEN_MASKS[1:])]


def add_all(first, others):
    for rows in others:
        first = first + rows.astype(jnp.float32)
    return first


def extra_masks():
    count = lax.axis_size("dp")
    used = sum(WEIGHT_BITS) + TOKEN_MASKS[-1]
    masks = []
    mask = 1
    while mask < count:
        if not mask & used:
            masks.append(mask)
        mask *= 2
    return masks


def gather_attention(own, count, qkv_cols, deps):
    low = jnp.bfloat16
    high_digit = jnp.floor(count / 64.0)
    digits = jnp.stack([high_digit, count - 64.0 * high_digit]).astype(low)
    digits = jnp.pad(digits[None, :], ((0, 7), (0, own.shape[1] - 2)))
    own = jnp.concatenate([own, digits], axis=0)
    slot_rows = own.shape[0]
    masks, line, mask = [0], own, lax.axis_size("dp") // 2
    while mask > 2:
        line = jnp.concatenate([line, swap_dp(line, mask)], axis=0)
        masks = masks + [m ^ mask for m in masks]
        mask //= 2
    line = after(line, *deps)
    inner, outer = line[:, :qkv_cols], line[:, qkv_cols:]
    inner = [inner] + [swap_dp(inner, mask) for mask in (1, 2, 3)]
    outer = [outer] + [swap_dp(outer, mask) for mask in (1, 2, 3)]
    table = jnp.array([[group ^ mask for mask in masks] for group in range(4)], jnp.int32)
    total = 0.0
    for group in inner:
        digits = group.reshape(len(masks), slot_rows, -1)[:, slot_rows - 8, :2]
        digits = jnp.sum(digits.astype(jnp.float32), axis=0)
        total = total + 64.0 * digits[0] + digits[1]
    total = total.reshape(1, 1)
    return line, inner, outer, lax.axis_index("dp") ^ table, (total + swap_core(total))[0, 0]


FAR_PIECES = ((0, 4), (4, 8))
NEAR_PIECES = ((0, 3), (3, 8))


def round_weights(master):
    bounds = FAR_PIECES + NEAR_PIECES
    extra = extra_masks()
    if not extra:
        shard, *pieces = round_units(master, bounds)
    else:
        shard = round_units(master, ())[0]
        for mask in extra:
            shard = jnp.concatenate([shard, swap_dp(shard, mask)], axis=0)
        pieces = [shard[begin:end] for begin, end in bounds]
    return shard, pieces[: len(FAR_PIECES)], pieces[len(FAR_PIECES) :]


def unit_owners():
    masks = [0]
    for mask in extra_masks():
        masks = masks + [m ^ mask for m in masks]
    first, second = WEIGHT_BITS
    masks = [m ^ k for k in (0, first, second, first ^ second) for m in masks]
    return lax.axis_index("dp") ^ jnp.array(masks, jnp.int32)


def scatter_rows(values):
    low = jnp.bfloat16
    count = lax.axis_size("dp")
    bits = count.bit_length() - 1
    values = values.reshape((2,) * bits + (values.shape[0] // count, values.shape[1]))
    left = list(range(bits - 1, -1, -1))
    order = [0, 2, 1] + list(range(3, bits))
    stages = []
    for bit in order:
        axis = left.index(bit)
        left.pop(axis)
        here = (lax.axis_index("dp") >> bit) & 1
        mine = lax.dynamic_index_in_dim(values, here, axis, keepdims=False)
        other = lax.dynamic_index_in_dim(values, 1 - here, axis, keepdims=False)
        sent = swap_dp(other, 1 << bit)
        values = (mine.astype(jnp.float32) + sent.astype(jnp.float32)).astype(low)
        stages.append(values)
    return stages


def add_grads(far, both):
    return (far.astype(jnp.float32) + swap_dp(both, WEIGHT_BITS[0]).astype(jnp.float32)).astype(
        jnp.bfloat16
    )


def grad_terms(own, near, far):
    parts = [own, swap_dp(near, WEIGHT_BITS[0]), far]
    masks = extra_masks()
    if not masks:
        return parts
    total = sum(p.astype(jnp.float32) for p in parts)
    for mask in reversed(masks):
        half = total.shape[0] // 2
        sent = swap_dp(total[half:].astype(jnp.bfloat16), mask)
        total = total[:half] + sent.astype(jnp.float32)
    return [total]


def on_device(
    activations,
    targets,
    lengths,
    token_mask,
    routes,
    route_weights,
    norm_gains,
    attention_master,
    expert_master,
    attention_left,
    attention_right,
    attention_left_root,
    attention_right_root,
    expert_left,
    expert_right,
    expert_left_root,
    expert_right_root,
):
    low = jnp.bfloat16
    own_rows = activations.shape[0]
    tensor_size = lax.axis_size("tensor")
    core = lax.axis_index("tensor")
    tokens_total = own_rows * tensor_size * lax.axis_size("dp")
    seq_length = lengths[0]
    position = core * own_rows + jnp.arange(own_rows, dtype=jnp.int32)
    valid_rows = ((token_mask == 1) & (position < seq_length)).astype(jnp.float32)
    valid_here = jnp.sum(valid_rows)

    routing = jnp.concatenate([routes.T.astype(jnp.float32), route_weights.T], axis=0)
    routing_parts = [routing] + [swap_dp(routing, mask) for mask in TOKEN_MASKS[1:]]
    heads_here = HEADS // tensor_size
    kv_here = KV_HEADS // tensor_size
    query_cols = heads_here * HEAD_DIM
    key_cols = kv_here * HEAD_DIM
    qkv_cols = query_cols + 2 * key_cols
    rows_here = attention_master.shape[0]

    def by_head(values):
        rows = values.shape[0]
        query = values[:, :query_cols].reshape(rows, kv_here, LANES)
        key = values[:, query_cols : query_cols + key_cols].reshape(rows, kv_here, HEAD_DIM)
        value = values[:, query_cols + key_cols : qkv_cols].reshape(rows, kv_here, HEAD_DIM)
        return jnp.concatenate([query, key, value], axis=2).reshape(rows, qkv_cols)

    attention_low = attention_master.astype(low)
    hidden = activations.astype(jnp.float32)
    normed_own, attention_scaling = normalize(hidden, norm_gains[0])
    normed_own = normed_own.astype(low)
    normed = in_order(normed_own, swap_core(normed_own))

    seq_rows = normed.shape[0]
    half_width = HEAD_DIM // 2
    frequency = theta_base ** (-jnp.arange(half_width, dtype=jnp.float32) * 2.0 / HEAD_DIM)
    angles = jnp.arange(seq_rows, dtype=jnp.float32)[:, None] * frequency[None, :]
    cosine = jnp.tile(jnp.cos(angles), (1, LANES // half_width))
    sine = jnp.tile(jnp.sin(angles), (1, LANES // half_width))
    own_columns = jnp.concatenate([by_head(attention_low), attention_low[:, qkv_cols:]], axis=1)
    shard, for_far, for_near = round_weights(expert_master)
    line, w_inner, w_outer, devices, valid_total = gather_attention(
        own_columns,
        valid_here,
        qkv_cols,
        [shard, normed, cosine, sine] + routing_parts[1:],
    )
    starts = devices * rows_here
    near_bit, far_bit = WEIGHT_BITS
    for_near[0] = after(for_near[0], *w_inner[1:])
    near = [swap_dp(piece, near_bit) for piece in for_near]
    far = [swap_dp(after(piece, line), far_bit) for piece in for_far]

    q2, k2, v_high, attended, w_qkv, log_totals = attention_forward(
        lengths,
        starts,
        normed,
        w_inner,
        cosine,
        sine,
    )
    branch, branch_other, w_output = output_projection(
        starts, core.reshape(1).astype(jnp.int32), attended, w_outer, far[:1] + near[:1]
    )
    branch = branch + swap_core(branch_other).astype(jnp.float32)
    middle = hidden + branch
    mix_own, mix_scaling = normalize(middle, norm_gains[1])

    routing = jnp.stack(routing_parts).reshape(len(TOKEN_MASKS), 2 * TOPK, 2, own_rows)
    routing = jnp.stack(
        [
            lax.dynamic_index_in_dim(routing, core, 2, keepdims=False),
            lax.dynamic_index_in_dim(routing, 1 - core, 2, keepdims=False),
        ],
        axis=1,
    )
    unit_here = expert_master.shape[0]
    unit_ids = (unit_owners()[:, None] * unit_here + jnp.arange(unit_here)[None, :]).reshape(-1)
    expert_of = unit_ids // GROUPS
    per_unit = unit_here % 4 != 0
    if not per_unit:
        expert_of = expert_of[::4]
    named = (
        routing[:, :, None, :TOPK] == expert_of.astype(jnp.float32)[None, None, :, None, None]
    )
    route_columns = jnp.sum(jnp.where(named, routing[:, :, None, TOPK:], 0.0), axis=3)
    route_columns = route_columns.transpose(0, 1, 3, 2).reshape(-1, expert_of.shape[0])

    spread = spread_tokens(mix_own.astype(low), True)
    both = [swap_dp(piece, near_bit) for piece in far]
    later = [after(spread[1], far[1], near[1]), spread[2], after(spread[3], both[0])]
    mix_rows = with_other(spread[:1] + later)
    mix, mixed, *firsts = expert_first(
        mix_rows, route_columns, per_unit, [shard] + near, []
    )
    pieces = [shard] + near + far + both
    mixed_parts, seconds = expert_second(
        2 * len(spread), own_rows, mix, mixed, route_columns, per_unit, far + both, []
    )
    slopes, silus, inners = ([firsts[i], seconds[i]] for i in range(3))
    sums = [sum_cores(i, mixed_parts[2 * i : 2 * i + 2]) for i in range(len(TOKEN_MASKS))]
    output = middle + add_all(sums[0], return_tokens(sums))
    residual_error = output - targets
    loss_part = jnp.sum(valid_rows[:, None] * residual_error * residual_error)
    output_grad = 2.0 / valid_total * valid_rows[:, None] * residual_error

    spread = spread_tokens(output_grad.astype(low), False)
    backward = functools.partial(expert_backward, slopes=slopes, silus=silus, pieces=pieces)
    parts0, kept = backward(0, [spread[0], swap_core(spread[0])], kept=None)
    later = [after(rows, parts0[0]) for rows in spread[1:]]
    parts1, kept = backward(2, with_other(later), kept=kept)
    parts = list(parts0) + list(parts1)
    sums = [sum_cores(i, parts[2 * i : 2 * i + 2]) for i in range(len(TOKEN_MASKS))]
    returned = return_tokens(sums)
    output_low = kept[0]
    gates, uppers = kept[1:3], kept[3:5]
    full = cost(30e9)
    down_far = weight_grads([inners[1]], output_low, (), full)
    gate_far = weight_grads([gates[1]], mix, [down_far[0]] + sums[1:], full)
    down_sum = add_grads(down_far[1], down_far[0])
    upper_far = weight_grads([uppers[1]], mix, [gate_far[0], down_sum], full)
    gate_sum = add_grads(gate_far[1], gate_far[0])
    upper_sum = add_grads(upper_far[1], upper_far[0])
    returned[2] = after(returned[2], upper_far[0], gate_sum)
    sent = add_all(sums[0], returned)
    far_gate, far_upper, far_down = (
        swap_dp(rows, far_bit) for rows in (gate_sum, upper_sum, down_sum)
    )
    mix_back, gain_mix = normalize_back(middle, mix_scaling, norm_gains[1], sent)
    middle_grad = output_grad + mix_back
    branch_own = middle_grad.astype(low)
    branch_low = in_order(branch_own, swap_core(branch_own))
    dq, dkv = attention_backward(
        lengths, branch_low, w_output, q2, k2, v_high, log_totals, cosine, sine,
        [upper_far[0], gate_sum],
    )
    qkv_grad = jnp.concatenate(
        [dq.reshape(seq_rows, kv_here, LANES), dkv.reshape(seq_rows, kv_here, LANES)], axis=2
    ).reshape(seq_rows, qkv_cols)
    qkv_part = dot(normed, qkv_grad, 0, 0).astype(low)
    output_part = dot(branch_low, attended, 0, 0).astype(low)
    gate_up_near = weight_grads([gates[0], uppers[0]], mix, [qkv_part, output_part, upper_sum])
    qkv_stages = scatter_rows(qkv_part)
    qkv_part = qkv_stages[-1]
    down_near = weight_grads(
        [inners[0]], output_low, [gate_up_near[0]]
    )
    output_part = lax.psum_scatter(output_part, "dp", scatter_dimension=0, tiled=True)
    normed_grad_other = dot(other_half(qkv_grad), w_qkv, 1, 1).astype(low)
    normed_grad = dot(own_half(qkv_grad), w_qkv, 1, 1)
    normed_grad = normed_grad + swap_core(normed_grad_other).astype(jnp.float32)
    attention_back, gain_attention = normalize_back(
        hidden, attention_scaling, norm_gains[0], normed_grad
    )
    input_grad = middle_grad + attention_back
    parts = {
        2: grad_terms(down_near[1], down_near[0], far_down),
        0: grad_terms(gate_up_near[1], gate_up_near[0], far_gate),
        1: grad_terms(gate_up_near[3], gate_up_near[2], far_upper),
    }
    state = (expert_master, expert_left, expert_right, expert_left_root, expert_right_root)
    updated = expert_update(
        0, parts[0], state, None, [far_down, far_gate, qkv_stages[0]]
    )
    updated = expert_update(1, parts[1], state, updated, [input_grad, qkv_stages[1]] + parts[2][1:2])
    loss_row = jnp.full((1, D), loss_part)
    sums = jnp.concatenate([gain_attention[None], gain_mix[None], loss_row], axis=0)
    sums = sum_everywhere(after(sums, updated[0]))
    updated = expert_update(2, parts[2], state, updated, [sums, qkv_part, output_part])
    expert_grad, expert_left_new, expert_right_new, expert_new = updated
    attention_grad, attention_left_new, attention_right_new, attention_new = attention_update(
        qkv_part,
        output_part,
        (
            attention_master,
            attention_left[0],
            attention_right[0],
            attention_left_root[0],
            attention_right_root[0],
        ),
    )
    gain_grad = sums[:2]
    mean_loss = sums[2, 0] / valid_total
    gains_new = norm_gains - gain_rate * tokens_total**0.5 * gain_grad

    return (
        output,
        mean_loss,
        input_grad,
        gain_grad,
        gains_new,
        attention_grad,
        attention_left_new[None],
        attention_right_new[None],
        attention_new,
        expert_grad,
        expert_left_new,
        expert_right_new,
        expert_new,
    )


def solution(mesh):
    return jax.shard_map(
        on_device,
        mesh=mesh,
        in_specs=(
            P(("dp", "tensor"), None),
            P(("dp", "tensor"), None),
            P("dp"),
            P(("dp", "tensor")),
            P("dp", None),
            P("dp", None),
            P(),
            P("dp", "tensor"),
            P("dp", None, "tensor", None),
            P("dp", "tensor", None, None),
            P("dp", "tensor", None, None),
            P("dp", "tensor", None, None),
            P("dp", "tensor", None, None),
            P("dp", None, None, "tensor", None),
            P("dp", None, "tensor", None, None),
            P("dp", None, None, "tensor", None),
            P("dp", None, "tensor", None, None),
        ),
        out_specs=(
            P(("dp", "tensor"), None),
            P(),
            P(("dp", "tensor"), None),
            P(),
            P(),
            P("dp", "tensor"),
            P("dp", "tensor", None, None),
            P("dp", "tensor", None, None),
            P("dp", "tensor"),
            P("dp", None, "tensor", None),
            P("dp", None, None, "tensor", None),
            P("dp", None, "tensor", None, None),
            P("dp", None, "tensor", None),
        ),
        check_vma=False,
    )
```

```python
import functools

import jax
import jax.numpy as jnp
from jax import lax
from jax.experimental import pallas as pl
from jax.experimental.pallas import tpu as pltpu
from jax.sharding import PartitionSpec as P

D = 1024
HEADS = 16
KV_HEADS = 8
HEAD_DIM = 64
EXPERTS = 32
TOPK = 8
BLK = 256
GROUPS = 4
BLOCK = 256
LANES = 128

epsilon = 1e-05
stat_decay = 0.9
gain_rate = 0.02
theta_base = 10000.0
masked_score = -1e30
MIB = 1 << 20
SMALL = pl.CostEstimate(flops=1000, bytes_accessed=1000, transcendentals=0)


def cost(flops):
    return pl.CostEstimate(flops=int(flops), bytes_accessed=1000, transcendentals=0)


ANYWHERE = pl.BlockSpec(memory_space=pl.ANY)
SCALARS = pl.BlockSpec(memory_space=pltpu.SMEM)

TOKEN_MASKS = (0, 1, 4, 5)
WEIGHT_BITS = (2, 8)


def dot(left, right, left_dim, right_dim):
    return lax.dot_general(
        left, right, (((left_dim,), (right_dim,)), ((), ())), preferred_element_type=jnp.float32
    )


def normalize(hidden, gain):
    scaling = lax.rsqrt(jnp.mean(hidden * hidden, axis=-1, keepdims=True) + epsilon)
    return (hidden * scaling * gain, scaling)


def normalize_back(hidden, scaling, gain, upstream):
    weighted = upstream * gain
    center = jnp.mean(weighted * hidden, axis=-1, keepdims=True)
    input_part = scaling * weighted - hidden * (scaling * scaling * scaling) * center
    return (input_part, jnp.sum(upstream * hidden * scaling, axis=0))


def swap_dp(values, mask):
    count = lax.axis_size("dp")
    return lax.ppermute(values, "dp", [(i, i ^ mask) for i in range(count)])


def swap_core(values):
    count = lax.axis_size("tensor")
    return lax.ppermute(values, "tensor", [(i, i ^ 1) for i in range(count)])


def sum_group(values):
    values = values + swap_core(values)
    return sum(values if mask == 0 else swap_dp(values, mask) for mask in TOKEN_MASKS)


def sum_groups(values):
    masks = [m for m in range(1, lax.axis_size("dp")) if not m & TOKEN_MASKS[-1]]
    return values + sum(swap_dp(values, mask) for mask in masks)


def in_order(own, other):
    first = lax.axis_index("tensor") == 0
    return jnp.concatenate([jnp.where(first, own, other), jnp.where(first, other, own)], axis=0)


def own_half(values):
    half = values.shape[0] // 2
    return lax.dynamic_slice_in_dim(values, lax.axis_index("tensor") * half, half, 0)


def other_half(values):
    half = values.shape[0] // 2
    return lax.dynamic_slice_in_dim(values, (1 - lax.axis_index("tensor")) * half, half, 0)


def turn(values):
    lane = lax.broadcasted_iota(jnp.int32, values.shape, 1)
    half = HEAD_DIM // 2
    return jnp.where(
        lane % HEAD_DIM < half,
        -pltpu.roll(values, LANES - half, 1),
        pltpu.roll(values, half, 1),
    )


def place_rows(starts_ref, source_refs, target_ref):
    for group, source_ref in enumerate(source_refs):
        count = starts_ref.shape[1]
        slot_rows = source_ref.shape[0] // count
        rows = target_ref.shape[0] // count // len(source_refs)
        for slot in range(count):
            start = pl.multiple_of(starts_ref[group, slot], rows)
            begin = slot * slot_rows
            target_ref[pl.ds(start, rows), :] = source_ref[begin : begin + rows, :]


def attention_forward_kernel(*refs):
    length_ref, starts_ref, x_ref, w0_ref, w1_ref, w2_ref, w3_ref, cos_ref, sin_ref = refs[:9]
    q_ref, k_ref, v_ref, att_ref, w_ref, lse_ref = refs[-6:]
    rows = x_ref.shape[0]
    place_rows(starts_ref, (w0_ref, w1_ref, w2_ref, w3_ref), w_ref)
    low = jnp.bfloat16
    cosine, sine = cos_ref[...], sin_ref[...]
    lane = lax.broadcasted_iota(jnp.int32, (rows, LANES), 1)
    left = lane < HEAD_DIM
    projected = dot(x_ref[...], w_ref[...], 1, 0)
    q_raw = projected[:, :LANES]
    q_turn = turn(q_raw)
    scale = HEAD_DIM ** (-0.5)
    q_rot = (q_raw * cosine + q_turn * sine) * scale
    q_rot_turn = (q_turn * cosine - q_raw * sine) * scale
    q_ref[:, :LANES] = jnp.where(left, q_rot, pltpu.roll(q_rot_turn, HEAD_DIM, 1)).astype(low)
    q_ref[:, LANES:] = jnp.where(left, pltpu.roll(q_rot, HEAD_DIM, 1), q_rot_turn).astype(low)
    kv_raw = projected[:, LANES:]
    k_turn = turn(kv_raw)
    k_rot = kv_raw * cosine + k_turn * sine
    k_rot_turn = k_turn * cosine - kv_raw * sine
    k_ref[...] = jnp.where(left, k_rot, pltpu.roll(k_rot_turn, HEAD_DIM, 1)).astype(low)
    v_high = jnp.where(left, 0.0, kv_raw)
    v_ref[...] = v_high.astype(low)
    v_low = pltpu.roll(v_high, HEAD_DIM, 1).astype(low)
    v_high = v_high.astype(low)
    k_only = jnp.where(left, k_rot, 0.0).astype(low)
    place = lax.broadcasted_iota(jnp.int32, (1, rows), 1)
    bias = jnp.where(place < length_ref[0], 0.0, masked_score)
    for block in range(rows // BLK):
        here = pl.ds(block * BLK, BLK)
        keys = (block + 1) * BLK
        total = None
        for head in range(2):
            q_block = q_ref[here, head * LANES : (head + 1) * LANES]
            scores = dot(q_block, k_only[:keys], 1, 1) + bias[:, :keys]
            top = jnp.max(scores, axis=1, keepdims=True)
            exponent = jnp.exp(scores - top)
            denominator = jnp.sum(exponent, axis=1, keepdims=True)
            weights = (exponent * (1.0 / denominator)).astype(low)
            value = v_high if head else v_low
            part = dot(weights, value[:keys], 1, 0)
            total = part if total is None else total + part
            log_total = jnp.broadcast_to(top + jnp.log(denominator), (BLK, LANES))
            lse_ref[head * 8 : (head + 1) * 8, here] = log_total.T[:8]
        att_ref[here, :] = total.astype(low)


def attention_backward_kernel(*refs):
    length_ref, branch_ref, wo_ref, q_ref, k_ref, v_ref, lse_ref, cos_ref, sin_ref = refs[:9]
    dq_ref, dkv_ref, dk_sum, d0_sum, d1_sum = refs[-5:]
    rows = branch_ref.shape[0]
    low = jnp.bfloat16
    lane = lax.broadcasted_iota(jnp.int32, (rows, LANES), 1)
    left = lane < HEAD_DIM
    grad = dot(branch_ref[...], wo_ref[...], 1, 0).astype(low)
    k_only = jnp.where(left, k_ref[...].astype(jnp.float32), 0.0).astype(low)
    v_high = v_ref[...]
    v_low = pltpu.roll(v_high.astype(jnp.float32), HEAD_DIM, 1).astype(low)
    place = lax.broadcasted_iota(jnp.int32, (rows, BLK), 0)
    seen = place < length_ref[0]
    dk_sum[...] = jnp.zeros_like(dk_sum)
    d0_sum[...] = jnp.zeros_like(d0_sum)
    d1_sum[...] = jnp.zeros_like(d1_sum)
    scale = HEAD_DIM ** (-0.5)
    for block in range(rows // BLK):
        here = pl.ds(block * BLK, BLK)
        keys = (block + 1) * BLK
        grad_block = grad[block * BLK : keys]
        query_grads = []
        for head in range(2):
            q_block = q_ref[here, head * LANES : (head + 1) * LANES]
            value = v_high if head else v_low
            scores = dot(k_only[:keys], q_block, 1, 1)
            log_total = lse_ref[head * 8 : head * 8 + 1, here]
            scores = jnp.where(seen[:keys], scores, masked_score)
            probability = jnp.exp(scores - log_total)
            prob_grad = dot(value[:keys], grad_block, 1, 1)
            weighted = probability * prob_grad
            center = jnp.sum(weighted, axis=0, keepdims=True)
            score_grad = (weighted - probability * center).astype(low)
            d_sum = d1_sum if head else d0_sum
            d_sum[:keys] += dot(probability.astype(low), grad_block, 1, 0)
            dk_sum[:keys] += dot(score_grad, q_block, 1, 0)
            query_grads.append(dot(score_grad, k_ref[:keys], 0, 0))
        cosine, sine = cos_ref[here, :] * scale, sin_ref[here, :] * scale
        zero, one = query_grads
        left_here = left[:BLK]
        straight = jnp.where(left_here, zero, pltpu.roll(one, HEAD_DIM, 1))
        turned = jnp.where(left_here, pltpu.roll(zero, HEAD_DIM, 1), one)
        dq_ref[here, :] = (straight * cosine - turned * sine).astype(low)
    dk_all = dk_sum[...]
    dk_rot = dk_all * cos_ref[...] - pltpu.roll(dk_all, HEAD_DIM, 1) * sin_ref[...]
    dv_all = pltpu.roll(d0_sum[...], HEAD_DIM, 1) + d1_sum[...]
    dkv_ref[...] = jnp.where(left, dk_rot, dv_all).astype(low)


def whole(shape):
    return pl.BlockSpec(shape, lambda h: (0,) * len(shape))


def columns(rows, width):
    return pl.BlockSpec((rows, width), lambda h: (0, h))


def attention_forward(length, starts, normed, w_groups, cosine, sine, deps=()):
    rows = normed.shape[0]
    kv_here = w_groups[0].shape[1] // 256
    low = jnp.bfloat16
    return pl.pallas_call(
        attention_forward_kernel,
        grid=(kv_here,),
        in_specs=[SCALARS, SCALARS, whole((rows, D))]
        + [columns(w.shape[0], 256) for w in w_groups]
        + [whole((rows, LANES))] * 2
        + [ANYWHERE] * len(deps),
        out_specs=[
            columns(rows, 256),
            columns(rows, LANES),
            columns(rows, LANES),
            columns(rows, LANES),
            columns(D, 256),
            pl.BlockSpec((16, rows), lambda h: (h, 0)),
        ],
        out_shape=[
            jax.ShapeDtypeStruct((rows, kv_here * 256), low),
            jax.ShapeDtypeStruct((rows, kv_here * LANES), low),
            jax.ShapeDtypeStruct((rows, kv_here * LANES), low),
            jax.ShapeDtypeStruct((rows, kv_here * LANES), low),
            jax.ShapeDtypeStruct((D, kv_here * 256), low),
            jax.ShapeDtypeStruct((kv_here * 16, rows), jnp.float32),
        ],
        compiler_params=pltpu.CompilerParams(vmem_limit_bytes=50 * MIB),
        cost_estimate=SMALL,
        name="attention_forward",
    )(length, starts, normed, *w_groups, cosine, sine, *deps)


def output_projection_kernel(*refs):
    starts_ref, core_ref, att_ref, w0_ref, w1_ref, w2_ref, w3_ref = refs[:7]
    own_ref, other_ref, w_ref = refs[-3:]
    place_rows(starts_ref, (w0_ref, w1_ref, w2_ref, w3_ref), w_ref)
    half = own_ref.shape[0]
    mine = pl.multiple_of(core_ref[0] * half, half)
    others = pl.multiple_of((1 - core_ref[0]) * half, half)
    other_ref[...] = dot(att_ref[pl.ds(others, half), :], w_ref[...], 1, 1).astype(jnp.bfloat16)
    own_ref[...] = dot(att_ref[pl.ds(mine, half), :], w_ref[...], 1, 1)


def output_projection(starts, core, attended, w_groups, deps=()):
    rows, width = attended.shape
    inside = pl.BlockSpec(memory_space=pltpu.VMEM)
    return pl.pallas_call(
        output_projection_kernel,
        in_specs=[SCALARS, SCALARS] + [inside] * 5 + [ANYWHERE] * len(deps),
        out_specs=[inside] * 3,
        out_shape=[
            jax.ShapeDtypeStruct((rows // 2, D), jnp.float32),
            jax.ShapeDtypeStruct((rows // 2, D), jnp.bfloat16),
            jax.ShapeDtypeStruct((D, width), jnp.bfloat16),
        ],
        compiler_params=pltpu.CompilerParams(vmem_limit_bytes=32 * MIB),
        cost_estimate=SMALL,
        name="output_projection",
    )(starts, core, attended, *w_groups, *deps)


def nothing(*refs):
    return None


def after(values, *deps):
    return pl.pallas_call(
        nothing,
        in_specs=[ANYWHERE] * (1 + len(deps)),
        out_specs=ANYWHERE,
        out_shape=jax.ShapeDtypeStruct(values.shape, values.dtype),
        input_output_aliases={0: 0},
        cost_estimate=SMALL,
        name="after",
    )(values, *deps)


def round_kernel(bounds, values_ref, whole_ref, *piece_refs):
    step = pl.program_id(0)
    rounded = values_ref[...].astype(jnp.bfloat16)
    whole_ref[...] = rounded
    for (begin, end), piece_ref in zip(bounds, piece_refs):

        @pl.when((step >= begin) & (step < end))
        def _(piece_ref=piece_ref):
            piece_ref[...] = rounded


def round_units(values, bounds):
    units = values.shape[0]
    shape = (None,) + values.shape[1:]

    def piece_spec(begin, end):
        return pl.BlockSpec(shape, lambda i: (jnp.clip(i - begin, 0, end - begin - 1), 0, 0, 0))

    return pl.pallas_call(
        functools.partial(round_kernel, bounds),
        grid=(units,),
        in_specs=[pl.BlockSpec(shape, lambda i: (i, 0, 0, 0))],
        out_specs=[pl.BlockSpec(shape, lambda i: (i, 0, 0, 0))]
        + [piece_spec(begin, end) for begin, end in bounds],
        out_shape=[jax.ShapeDtypeStruct(values.shape, jnp.bfloat16)]
        + [
            jax.ShapeDtypeStruct((end - begin,) + values.shape[1:], jnp.bfloat16)
            for begin, end in bounds
        ],
        cost_estimate=SMALL,
        name="round_units",
    )(values)


def attention_backward(length, branch_low, w_output, q2, k2, v, lse, cosine, sine, deps=()):
    rows = branch_low.shape[0]
    kv_here = k2.shape[1] // LANES
    low = jnp.bfloat16
    return pl.pallas_call(
        attention_backward_kernel,
        grid=(kv_here,),
        in_specs=[
            SCALARS,
            whole((rows, D)),
            columns(D, LANES),
            columns(rows, 256),
            columns(rows, LANES),
            columns(rows, LANES),
            pl.BlockSpec((16, rows), lambda h: (h, 0)),
            whole((rows, LANES)),
            whole((rows, LANES)),
        ]
        + [pl.BlockSpec(memory_space=pl.ANY)] * len(deps),
        out_specs=[columns(rows, LANES), columns(rows, LANES)],
        out_shape=[
            jax.ShapeDtypeStruct((rows, kv_here * LANES), low),
            jax.ShapeDtypeStruct((rows, kv_here * LANES), low),
        ],
        scratch_shapes=[pltpu.VMEM((rows, LANES), jnp.float32)] * 3,
        compiler_params=pltpu.CompilerParams(vmem_limit_bytes=50 * MIB),
        cost_estimate=SMALL,
        name="attention_backward",
    )(length, branch_low, w_output, q2, k2, v, lse, cosine, sine, *deps)


CHUNK = 512
UNIT_ROWS = 64


def first_unit(piece_refs, piece):
    return sum(p.shape[0] for p in piece_refs[:piece])


def piece_copy(piece_refs, weights, arrived, piece, kind):
    units = piece_refs[piece].shape[0]
    return pltpu.make_async_copy(
        piece_refs[piece].at[:, kind],
        weights.at[kind, pl.ds(first_unit(piece_refs, piece), units)],
        arrived.at[piece, kind],
    )


def row_copy(row_refs, rows_all, landed, index):
    count = len(row_refs) - 1
    rows = row_refs[0].shape[0]
    source = row_refs[index // 2]
    if index % 2:
        source = row_refs[count].at[pl.ds(index // 2 * rows, rows)]
    return pltpu.make_async_copy(
        source, rows_all.at[pl.ds(index * rows, rows)], landed.at[index]
    )


def fetch(piece_refs, weights, arrived, row_refs=(None,), rows_all=None, landed=None):
    @pl.when(pl.program_id(0) == 0)
    def _():
        copies = [
            row_copy(row_refs, rows_all, landed, index) for index in range(2 * len(row_refs) - 2)
        ]
        copies += [
            piece_copy(piece_refs, weights, arrived, piece, kind)
            for piece in range(len(piece_refs))
            for kind in range(3)
        ]
        for copy in copies:
            copy.start()
        for copy in copies:
            copy.wait()


def chunk_weights(weights, kind, chunk):
    units = CHUNK // UNIT_ROWS
    return weights[kind, chunk * units : (chunk + 1) * units].reshape(CHUNK, D)


def spread_weights(route_ref, column, per_unit):
    rows = route_ref.shape[0]
    units = CHUNK // UNIT_ROWS
    count = units if per_unit else units // 4
    width = CHUNK // count
    pieces = [
        jnp.broadcast_to(route_ref[:, column * count + j : column * count + j + 1], (rows, width))
        for j in range(count)
    ]
    return jnp.concatenate(pieces, axis=1)


def store_step(out_refs, values):
    step = pl.program_id(0)
    for index, out_ref in enumerate(out_refs):

        @pl.when(step == index)
        def _(out_ref=out_ref):
            out_ref[...] = values


def expert_hidden(x, route_ref, weights, first_column, per_unit, outs):
    low = jnp.bfloat16
    slope_ref, silu_ref, inner_ref = outs
    for chunk in range(slope_ref.shape[1] // CHUNK):
        here = slice(chunk * CHUNK, (chunk + 1) * CHUNK)
        gate = dot(x, chunk_weights(weights, 0, chunk), 1, 1)
        upper = dot(x, chunk_weights(weights, 1, chunk), 1, 1)
        sigmoid = 0.5 * jnp.tanh(0.5 * gate) + 0.5
        silu = gate * sigmoid
        weight = spread_weights(route_ref, first_column + chunk, per_unit)
        weighted_upper = weight * upper
        slope_ref[:, here] = (weighted_upper * (sigmoid + silu * (1.0 - sigmoid))).astype(low)
        silu_ref[:, here] = (weight * silu).astype(low)
        inner_ref[:, here] = (silu * weighted_upper).astype(low)
    return dot(inner_ref[...], weights[2].reshape(-1, D), 1, 0)


def expert_first_kernel(count, pieces, per_unit, *refs):
    parts = count // 2 + 1
    row_refs, route_ref = refs[:parts], refs[parts]
    piece_refs = refs[parts + 1 : parts + 1 + pieces]
    x_ref, mixed_ref, slope_ref, silu_ref, inner_ref = refs[-9:-4]
    weights, arrived, rows_all, landed = refs[-4:]
    fetch(piece_refs, weights, arrived, row_refs, rows_all, landed)
    rows = x_ref.shape[0]
    x = rows_all[pl.ds(pl.multiple_of(pl.program_id(0) * rows, rows), rows), :]
    x_ref[...] = x
    outs = (slope_ref, silu_ref, inner_ref)
    mixed_ref[...] = expert_hidden(
        x, route_ref, weights, 0, per_unit, outs
    ).astype(jnp.bfloat16)


def expert_second_kernel(count, pieces, per_unit, first_column, *refs):
    x_ref, mixed_ref, route_ref = refs[:3]
    piece_refs = refs[3 : 3 + pieces]
    out_refs = refs[-5 - count : -5]
    weights, arrived = refs[-2:]
    fetch(piece_refs, weights, arrived)
    part = expert_hidden(
        x_ref[...], route_ref, weights, first_column, per_unit, refs[-5:-2]
    )
    store_step(out_refs, (part + mixed_ref[...].astype(jnp.float32)).astype(jnp.bfloat16))


def expert_backward_kernel(count, pieces, *refs):
    parts = count // 2 + 1
    row_refs = refs[:parts]
    slope_refs, silu_refs = refs[parts : parts + 2], refs[parts + 2 : parts + 4]
    piece_refs = refs[parts + 4 : parts + 4 + pieces]
    out_refs = refs[-9 - count : -9]
    grad_ref = refs[-9]
    gate_refs, upper_refs = refs[-8:-6], refs[-6:-4]
    weights, arrived, rows_all, landed = refs[-4:]
    low = jnp.bfloat16
    fetch(piece_refs, weights, arrived, row_refs, rows_all, landed)
    rows = grad_ref.shape[0]
    grad = rows_all[pl.ds(pl.multiple_of(pl.program_id(0) * rows, rows), rows), :]
    grad_ref[...] = grad
    chunks = slope_refs[0].shape[1] // CHUNK
    for chunk in range(2 * chunks):
        half, place = chunk // chunks, chunk % chunks
        here = slice(place * CHUNK, (place + 1) * CHUNK)
        inner_grad = dot(grad, chunk_weights(weights, 2, chunk), 1, 1)
        slope, silu = slope_refs[half][:, here], silu_refs[half][:, here]
        gate_refs[half][:, here] = (inner_grad * slope.astype(jnp.float32)).astype(low)
        upper_refs[half][:, here] = (inner_grad * silu.astype(jnp.float32)).astype(low)
    units = weights.shape[1] // 2
    total = None
    for half in range(2):
        mine = pl.ds(half * units, units)
        part = dot(gate_refs[half][...], weights[0, mine].reshape(-1, D), 1, 0)
        part = part + dot(upper_refs[half][...], weights[1, mine].reshape(-1, D), 1, 0)
        total = part if total is None else total + part
    store_step(out_refs, total.astype(low))


def fixed(shape):
    return pl.BlockSpec(shape, lambda i: (0,) * len(shape))


def token_block(rows, width, first=0):
    return pl.BlockSpec((rows, width), lambda i: (first + i, 0))


def expert_scratch(pieces, count=0, rows=0):
    units = sum(p.shape[0] for p in pieces)
    scratch = [
        pltpu.VMEM((3, units, UNIT_ROWS, D), jnp.bfloat16),
        pltpu.SemaphoreType.DMA((len(pieces), 3)),
    ]
    if count:
        scratch += [
            pltpu.VMEM((count * rows, D), jnp.bfloat16),
            pltpu.SemaphoreType.DMA((count,)),
        ]
    return scratch


def expert_call(
    kernel, name, steps, operands, specs, out_specs, widths, singles, kept, scratch, estimate=SMALL
):
    rows, total_rows = singles[1], singles[2]
    low = jnp.bfloat16
    operands, specs = list(operands), list(specs)
    aliases = {}
    if kept is not None:
        for index, buffer in enumerate(kept):
            aliases[len(operands)] = singles[0] + index
            operands.append(buffer)
            specs.append(ANYWHERE)
    outs = pl.pallas_call(
        kernel,
        grid=(steps,),
        in_specs=specs,
        out_specs=[fixed((rows, D))] * singles[0] + out_specs,
        out_shape=[jax.ShapeDtypeStruct((rows, D), low)] * singles[0]
        + [jax.ShapeDtypeStruct((total_rows, w), low) for w in widths],
        scratch_shapes=scratch,
        input_output_aliases=aliases,
        compiler_params=pltpu.CompilerParams(vmem_limit_bytes=60 * MIB),
        cost_estimate=estimate,
        name=name,
    )(*operands)
    return outs[: singles[0]], outs[singles[0] :]


def expert_first(row_parts, route_columns, per_unit, pieces, deps):
    count, rows = 2 * len(row_parts) - 2, row_parts[0].shape[0]
    width = sum(p.shape[0] for p in pieces) * UNIT_ROWS
    widths = [D, D, width, width, width]
    return expert_call(
        functools.partial(expert_first_kernel, count, len(pieces), per_unit),
        "expert_first",
        count,
        list(row_parts) + [route_columns] + list(pieces) + list(deps),
        [ANYWHERE] * len(row_parts)
        + [token_block(rows, route_columns.shape[1])]
        + [ANYWHERE] * (len(pieces) + len(deps)),
        [token_block(rows, w) for w in widths],
        widths,
        (0, rows, count * rows),
        None,
        expert_scratch(pieces, count, rows),
        cost(6 * count * rows * width * D),
    )[1]


def expert_second(count, rows, x, mixed, route_columns, per_unit, pieces, deps):
    width = sum(p.shape[0] for p in pieces) * UNIT_ROWS
    return expert_call(
        functools.partial(expert_second_kernel, count, len(pieces), per_unit, width // CHUNK),
        "expert_second",
        count,
        [x, mixed, route_columns] + list(pieces) + list(deps),
        [
            token_block(rows, D),
            token_block(rows, D),
            token_block(rows, route_columns.shape[1]),
        ]
        + [ANYWHERE] * (len(pieces) + len(deps)),
        [token_block(rows, width)] * 3,
        [width] * 3,
        (count, rows, x.shape[0]),
        None,
        expert_scratch(pieces),
    )


def expert_backward(first, row_parts, slopes, silus, pieces, kept):
    count, rows = 2 * len(row_parts) - 2, row_parts[0].shape[0]
    width = slopes[0].shape[1]
    widths = [D] + [width] * 4
    return expert_call(
        functools.partial(expert_backward_kernel, count, len(pieces)),
        "expert_backward",
        count,
        list(row_parts) + list(slopes) + list(silus) + list(pieces),
        [ANYWHERE] * len(row_parts)
        + [token_block(rows, width, first)] * 4
        + [ANYWHERE] * len(pieces),
        [token_block(rows, w, first) for w in widths],
        widths,
        (count, rows, slopes[0].shape[0]),
        kept,
        expert_scratch(pieces, count, rows),
    )


def weight_grad_kernel(count, *refs):
    right_ref = refs[count]
    outs = refs[-2 * count :]
    step = pl.program_id(0)
    for index in range(count):
        for slot in range(2):

            @pl.when(step == 2 * index + slot)
            def _(index=index, slot=slot):
                outs[2 * index + slot][...] = dot(refs[index][...], right_ref[...], 0, 0).astype(
                    jnp.bfloat16
                )


def weight_grads(lefts, right, deps=(), estimate=SMALL):
    rows = right.shape[0]
    columns_here = lefts[0].shape[1] // 2
    count = len(lefts)

    def left_spec(index):
        return pl.BlockSpec(
            (rows, columns_here), lambda i: (0, 1 - jnp.clip(i - 2 * index, 0, 1))
        )

    return pl.pallas_call(
        functools.partial(weight_grad_kernel, count),
        grid=(2 * count,),
        in_specs=[left_spec(index) for index in range(count)]
        + [pl.BlockSpec((rows, D), lambda i: (0, 0), pipeline_mode=pl.Buffered(1))]
        + [ANYWHERE] * len(deps),
        out_specs=[fixed((columns_here, D))] * (2 * count),
        out_shape=[jax.ShapeDtypeStruct((columns_here, D), jnp.bfloat16)] * (2 * count),
        compiler_params=pltpu.CompilerParams(vmem_limit_bytes=56 * MIB),
        cost_estimate=estimate,
        name="weight_grads",
    )(*lefts, right, *deps)


def update_blocks(grads, lefts, rights, left_roots, right_roots, left_outs, right_outs, step_outs):
    low = jnp.bfloat16
    grads = [grad.astype(low) for grad in grads]
    firsts = [
        dot(root[...].astype(low), grad, 1, 0).astype(low) for root, grad in zip(left_roots, grads)
    ]
    for grad, left, out in zip(grads, lefts, left_outs):
        out[...] = stat_decay * left[...] + dot(grad, grad, 1, 1)
    for first, root, (out, master) in zip(firsts, right_roots, step_outs):
        out[...] = master[...] - D ** (-0.5) * dot(first, root[...].astype(low), 1, 0)
    for grad, right, out in zip(grads, rights, right_outs):
        out[...] = stat_decay * right[...] + dot(grad, grad, 0, 0)


def expert_update_kernel(count, *refs):
    parts = refs[:count]
    master, left, right, left_root, right_root = refs[count : count + 5]
    grad_out, left_out, right_out, new_out = refs[-4:]
    units, rows, _ = grad_out.shape
    grad = parts[0][...].astype(jnp.float32)
    for part in parts[1:]:
        grad = grad + part[...].astype(jnp.float32)
    grad = grad.reshape(units, rows, D)
    grad_out[...] = grad
    blocks = [(u, b) for u in range(units) for b in range(D // BLOCK)]

    def wide(ref):
        return [ref.at[u, :, b * BLOCK : (b + 1) * BLOCK] for u, b in blocks]

    def square(ref):
        return [ref.at[u, b] for u, b in blocks]

    update_blocks(
        [grad[u, :, b * BLOCK : (b + 1) * BLOCK] for u, b in blocks],
        square(left),
        square(right),
        square(left_root),
        square(right_root),
        square(left_out),
        square(right_out),
        list(zip(wide(new_out), wide(master))),
    )


def expert_update(kind, parts, state, kept, deps=()):
    master, left, right, left_root, right_root = state
    units, _, rows, _ = master.shape
    step = min(units, 2)
    flat = pl.BlockSpec((step, None, rows, D), lambda i: (i, kind, 0, 0))
    lefts = pl.BlockSpec((step, None) + left.shape[2:], lambda i: (i, kind, 0, 0, 0))
    rights = pl.BlockSpec((step, None) + right.shape[2:], lambda i: (i, kind, 0, 0, 0))
    operands = list(parts) + list(state) + list(deps)
    specs = [pl.BlockSpec((step * rows, D), lambda i: (i, 0))] * len(parts)
    specs += [flat, lefts, rights, lefts, rights] + [ANYWHERE] * len(deps)
    aliases = {}
    if kept is not None:
        for index, buffer in enumerate(kept):
            aliases[len(operands)] = index
            operands.append(buffer)
            specs.append(ANYWHERE)
    return pl.pallas_call(
        functools.partial(expert_update_kernel, len(parts)),
        grid=(units // step,),
        in_specs=specs,
        out_specs=[flat, lefts, rights, flat],
        out_shape=[jax.ShapeDtypeStruct(a.shape, jnp.float32) for a in (master, left, right, master)],
        input_output_aliases=aliases,
        compiler_params=pltpu.CompilerParams(vmem_limit_bytes=56 * MIB),
        cost_estimate=cost(12e9),
        name="expert_update",
    )(*operands)


def attention_update_kernel(qkv_ref, wo_ref, master, left, right, left_root, right_root, *outs):
    grad_out, left_out, right_out, new_out = outs
    heads = qkv_ref.shape[1] // 256
    rows = qkv_ref.shape[0]
    low_lanes = lax.broadcasted_iota(jnp.int32, (rows, LANES), 1) < HEAD_DIM
    grad = qkv_ref[...].astype(jnp.float32)
    queries = heads * LANES
    keys = queries // 2
    for head in range(heads):
        grad_out[:, head * LANES : (head + 1) * LANES] = grad[:, head * 256 : head * 256 + LANES]
    for pair in range(heads // 2):
        begin = pair * 512 + LANES
        one, two = grad[:, begin : begin + LANES], grad[:, begin + 256 : begin + 256 + LANES]
        place = queries + pair * LANES
        grad_out[:, place : place + LANES] = jnp.where(low_lanes, one, pltpu.roll(two, HEAD_DIM, 1))
        place = place + keys
        grad_out[:, place : place + LANES] = jnp.where(low_lanes, pltpu.roll(one, HEAD_DIM, 1), two)
    grad_out[:, queries + 2 * keys :] = wo_ref[...].astype(jnp.float32)
    blocks = range(grad_out.shape[1] // BLOCK)

    def wide(ref):
        return [ref.at[:, b * BLOCK : (b + 1) * BLOCK] for b in blocks]

    def square(ref):
        return [ref.at[b] for b in blocks]

    update_blocks(
        [part[...] for part in wide(grad_out)],
        square(left),
        square(right),
        square(left_root),
        square(right_root),
        square(left_out),
        square(right_out),
        list(zip(wide(new_out), wide(master))),
    )


def attention_update(qkv_part, output_part, state):
    inside = pl.BlockSpec(memory_space=pltpu.VMEM)
    master, left, right = state[:3]
    return pl.pallas_call(
        attention_update_kernel,
        in_specs=[inside] * 7,
        out_specs=[inside] * 4,
        out_shape=[jax.ShapeDtypeStruct(a.shape, jnp.float32) for a in (master, left, right, master)],
        compiler_params=pltpu.CompilerParams(vmem_limit_bytes=40 * MIB),
        cost_estimate=SMALL,
        name="attention_update",
    )(qkv_part, output_part, *state)


def spread_tokens(own, relay):
    beside, across, both = TOKEN_MASKS[1:]
    rows = [own, swap_dp(own, beside), swap_dp(own, across)]
    return rows + [swap_dp(rows[2], beside) if relay else swap_dp(own, both)]


def with_other(own_rows):
    return list(own_rows) + [swap_core(jnp.concatenate(own_rows, axis=0))]


def sum_cores(place, parts):
    own, other = parts
    total = own.astype(jnp.float32) + swap_core(other).astype(jnp.float32)
    return total if place == 0 else total.astype(jnp.bfloat16)


def return_tokens(sums):
    return [swap_dp(rows, mask) for rows, mask in zip(sums[1:], TOKEN_MASKS[1:])]


def add_all(first, others):
    for rows in others:
        first = first + rows.astype(jnp.float32)
    return first


def extra_masks():
    count = lax.axis_size("dp")
    used = sum(WEIGHT_BITS) + TOKEN_MASKS[-1]
    masks = []
    mask = 1
    while mask < count:
        if not mask & used:
            masks.append(mask)
        mask *= 2
    return masks


def gather_attention(own, count, qkv_cols, deps):
    low = jnp.bfloat16
    high_digit = jnp.floor(count / 64.0)
    digits = jnp.stack([high_digit, count - 64.0 * high_digit]).astype(low)
    digits = jnp.pad(digits[None, :], ((0, 7), (0, own.shape[1] - 2)))
    own = jnp.concatenate([own, digits], axis=0)
    slot_rows = own.shape[0]
    masks, line, mask = [0], own, lax.axis_size("dp") // 2
    while mask > 2:
        line = jnp.concatenate([line, swap_dp(line, mask)], axis=0)
        masks = masks + [m ^ mask for m in masks]
        mask //= 2
    line = after(line, *deps)
    inner, outer = line[:, :qkv_cols], line[:, qkv_cols:]
    inner = [inner] + [swap_dp(inner, mask) for mask in (1, 2, 3)]
    outer = [outer] + [swap_dp(outer, mask) for mask in (1, 2, 3)]
    table = jnp.array([[group ^ mask for mask in masks] for group in range(4)], jnp.int32)
    total = 0.0
    for group in inner:
        digits = group.reshape(len(masks), slot_rows, -1)[:, slot_rows - 8, :2]
        digits = jnp.sum(digits.astype(jnp.float32), axis=0)
        total = total + 64.0 * digits[0] + digits[1]
    total = total.reshape(1, 1)
    return line, inner, outer, lax.axis_index("dp") ^ table, (total + swap_core(total))[0, 0]


FAR_PIECES = ((0, 4), (4, 8))
NEAR_PIECES = ((0, 3), (3, 8))


def round_weights(master):
    bounds = FAR_PIECES + NEAR_PIECES
    extra = extra_masks()
    if not extra:
        shard, *pieces = round_units(master, bounds)
    else:
        shard = round_units(master, ())[0]
        for mask in extra:
            shard = jnp.concatenate([shard, swap_dp(shard, mask)], axis=0)
        pieces = [shard[begin:end] for begin, end in bounds]
    return shard, pieces[: len(FAR_PIECES)], pieces[len(FAR_PIECES) :]


def unit_owners():
    masks = [0]
    for mask in extra_masks():
        masks = masks + [m ^ mask for m in masks]
    first, second = WEIGHT_BITS
    masks = [m ^ k for k in (0, first, second, first ^ second) for m in masks]
    return lax.axis_index("dp") ^ jnp.array(masks, jnp.int32)


def scatter_rows(values):
    low = jnp.bfloat16
    count = lax.axis_size("dp")
    bits = count.bit_length() - 1
    values = values.reshape((2,) * bits + (values.shape[0] // count, values.shape[1]))
    left = list(range(bits - 1, -1, -1))
    order = [0, 2, 1] + list(range(3, bits))
    stages = []
    for bit in order:
        axis = left.index(bit)
        left.pop(axis)
        here = (lax.axis_index("dp") >> bit) & 1
        mine = lax.dynamic_index_in_dim(values, here, axis, keepdims=False)
        other = lax.dynamic_index_in_dim(values, 1 - here, axis, keepdims=False)
        sent = swap_dp(other, 1 << bit)
        values = (mine.astype(jnp.float32) + sent.astype(jnp.float32)).astype(low)
        stages.append(values)
    return stages


def add_grads(far, both):
    return (far.astype(jnp.float32) + swap_dp(both, WEIGHT_BITS[0]).astype(jnp.float32)).astype(
        jnp.bfloat16
    )


def grad_terms(own, near, far):
    parts = [own, swap_dp(near, WEIGHT_BITS[0]), far]
    masks = extra_masks()
    if not masks:
        return parts
    total = sum(p.astype(jnp.float32) for p in parts)
    for mask in reversed(masks):
        half = total.shape[0] // 2
        sent = swap_dp(total[half:].astype(jnp.bfloat16), mask)
        total = total[:half] + sent.astype(jnp.float32)
    return [total]


def on_device(
    activations,
    targets,
    lengths,
    token_mask,
    routes,
    route_weights,
    norm_gains,
    attention_master,
    expert_master,
    attention_left,
    attention_right,
    attention_left_root,
    attention_right_root,
    expert_left,
    expert_right,
    expert_left_root,
    expert_right_root,
):
    low = jnp.bfloat16
    own_rows = activations.shape[0]
    tensor_size = lax.axis_size("tensor")
    core = lax.axis_index("tensor")
    tokens_total = own_rows * tensor_size * lax.axis_size("dp")
    seq_length = lengths[0]
    position = core * own_rows + jnp.arange(own_rows, dtype=jnp.int32)
    valid_rows = ((token_mask == 1) & (position < seq_length)).astype(jnp.float32)
    valid_here = jnp.sum(valid_rows)

    routing = jnp.concatenate([routes.T.astype(jnp.float32), route_weights.T], axis=0)
    routing_parts = [routing] + [swap_dp(routing, mask) for mask in TOKEN_MASKS[1:]]
    heads_here = HEADS // tensor_size
    kv_here = KV_HEADS // tensor_size
    query_cols = heads_here * HEAD_DIM
    key_cols = kv_here * HEAD_DIM
    qkv_cols = query_cols + 2 * key_cols
    rows_here = attention_master.shape[0]

    def by_head(values):
        rows = values.shape[0]
        query = values[:, :query_cols].reshape(rows, kv_here, LANES)
        key = values[:, query_cols : query_cols + key_cols].reshape(rows, kv_here, HEAD_DIM)
        value = values[:, query_cols + key_cols : qkv_cols].reshape(rows, kv_here, HEAD_DIM)
        return jnp.concatenate([query, key, value], axis=2).reshape(rows, qkv_cols)

    attention_low = attention_master.astype(low)
    hidden = activations.astype(jnp.float32)
    normed_own, attention_scaling = normalize(hidden, norm_gains[0])
    normed_own = normed_own.astype(low)
    normed = in_order(normed_own, swap_core(normed_own))

    seq_rows = normed.shape[0]
    half_width = HEAD_DIM // 2
    frequency = theta_base ** (-jnp.arange(half_width, dtype=jnp.float32) * 2.0 / HEAD_DIM)
    angles = jnp.arange(seq_rows, dtype=jnp.float32)[:, None] * frequency[None, :]
    cosine = jnp.tile(jnp.cos(angles), (1, LANES // half_width))
    sine = jnp.tile(jnp.sin(angles), (1, LANES // half_width))
    own_columns = jnp.concatenate([by_head(attention_low), attention_low[:, qkv_cols:]], axis=1)
    shard, for_far, for_near = round_weights(expert_master)
    line, w_inner, w_outer, devices, valid_total = gather_attention(
        own_columns,
        valid_here,
        qkv_cols,
        [shard, normed, cosine, sine] + routing_parts[1:],
    )
    starts = devices * rows_here
    near_bit, far_bit = WEIGHT_BITS
    for_near[0] = after(for_near[0], *w_inner[1:])
    near = [swap_dp(piece, near_bit) for piece in for_near]
    far = [swap_dp(after(piece, line), far_bit) for piece in for_far]

    q2, k2, v_high, attended, w_qkv, log_totals = attention_forward(
        lengths,
        starts,
        normed,
        w_inner,
        cosine,
        sine,
    )
    branch, branch_other, w_output = output_projection(
        starts, core.reshape(1).astype(jnp.int32), attended, w_outer, far[:1] + near[:1]
    )
    branch = branch + swap_core(branch_other).astype(jnp.float32)
    middle = hidden + branch
    mix_own, mix_scaling = normalize(middle, norm_gains[1])

    routing = jnp.stack(routing_parts).reshape(len(TOKEN_MASKS), 2 * TOPK, 2, own_rows)
    routing = jnp.stack(
        [
            lax.dynamic_index_in_dim(routing, core, 2, keepdims=False),
            lax.dynamic_index_in_dim(routing, 1 - core, 2, keepdims=False),
        ],
        axis=1,
    )
    unit_here = expert_master.shape[0]
    unit_ids = (unit_owners()[:, None] * unit_here + jnp.arange(unit_here)[None, :]).reshape(-1)
    expert_of = unit_ids // GROUPS
    per_unit = unit_here % 4 != 0
    if not per_unit:
        expert_of = expert_of[::4]
    named = (
        routing[:, :, None, :TOPK] == expert_of.astype(jnp.float32)[None, None, :, None, None]
    )
    route_columns = jnp.sum(jnp.where(named, routing[:, :, None, TOPK:], 0.0), axis=3)
    route_columns = route_columns.transpose(0, 1, 3, 2).reshape(-1, expert_of.shape[0])

    spread = spread_tokens(mix_own.astype(low), True)
    both = [swap_dp(piece, near_bit) for piece in far]
    later = [after(spread[1], far[1], near[1]), spread[2], after(spread[3], both[0])]
    mix_rows = with_other(spread[:1] + later)
    mix, mixed, *firsts = expert_first(
        mix_rows, route_columns, per_unit, [shard] + near, []
    )
    pieces = [shard] + near + far + both
    mixed_parts, seconds = expert_second(
        2 * len(spread), own_rows, mix, mixed, route_columns, per_unit, far + both, []
    )
    slopes, silus, inners = ([firsts[i], seconds[i]] for i in range(3))
    sums = [sum_cores(i, mixed_parts[2 * i : 2 * i + 2]) for i in range(len(TOKEN_MASKS))]
    output = middle + add_all(sums[0], return_tokens(sums))
    residual_error = output - targets
    loss_part = jnp.sum(valid_rows[:, None] * residual_error * residual_error)
    output_grad = 2.0 / valid_total * valid_rows[:, None] * residual_error

    spread = spread_tokens(output_grad.astype(low), False)
    backward = functools.partial(expert_backward, slopes=slopes, silus=silus, pieces=pieces)
    parts0, kept = backward(0, [spread[0], swap_core(spread[0])], kept=None)
    later = [after(rows, parts0[0]) for rows in spread[1:]]
    parts1, kept = backward(2, with_other(later), kept=kept)
    parts = list(parts0) + list(parts1)
    sums = [sum_cores(i, parts[2 * i : 2 * i + 2]) for i in range(len(TOKEN_MASKS))]
    returned = return_tokens(sums)
    output_low = kept[0]
    gates, uppers = kept[1:3], kept[3:5]
    full = cost(30e9)
    down_far = weight_grads([inners[1]], output_low, (), full)
    gate_far = weight_grads([gates[1]], mix, [down_far[0]] + sums[1:], full)
    down_sum = add_grads(down_far[1], down_far[0])
    upper_far = weight_grads([uppers[1]], mix, [gate_far[0], down_sum], full)
    gate_sum = add_grads(gate_far[1], gate_far[0])
    upper_sum = add_grads(upper_far[1], upper_far[0])
    returned[2] = after(returned[2], upper_far[0], gate_sum)
    sent = add_all(sums[0], returned)
    far_gate, far_upper, far_down = (
        swap_dp(rows, far_bit) for rows in (gate_sum, upper_sum, down_sum)
    )
    mix_back, gain_mix = normalize_back(middle, mix_scaling, norm_gains[1], sent)
    middle_grad = output_grad + mix_back
    branch_own = middle_grad.astype(low)
    branch_low = in_order(branch_own, swap_core(branch_own))
    dq, dkv = attention_backward(
        lengths, branch_low, w_output, q2, k2, v_high, log_totals, cosine, sine,
        [upper_far[0], gate_sum],
    )
    qkv_grad = jnp.concatenate(
        [dq.reshape(seq_rows, kv_here, LANES), dkv.reshape(seq_rows, kv_here, LANES)], axis=2
    ).reshape(seq_rows, qkv_cols)
    qkv_part = dot(normed, qkv_grad, 0, 0).astype(low)
    output_part = dot(branch_low, attended, 0, 0).astype(low)
    gate_up_near = weight_grads([gates[0], uppers[0]], mix, [qkv_part, output_part, upper_sum])
    qkv_stages = scatter_rows(qkv_part)
    qkv_part = qkv_stages[-1]
    down_near = weight_grads(
        [inners[0]], output_low, [gate_up_near[0]]
    )
    output_part = lax.psum_scatter(output_part, "dp", scatter_dimension=0, tiled=True)
    normed_grad_other = dot(other_half(qkv_grad), w_qkv, 1, 1).astype(low)
    normed_grad = dot(own_half(qkv_grad), w_qkv, 1, 1)
    normed_grad = normed_grad + swap_core(normed_grad_other).astype(jnp.float32)
    attention_back, gain_attention = normalize_back(
        hidden, attention_scaling, norm_gains[0], normed_grad
    )
    input_grad = middle_grad + attention_back
    parts = {
        2: grad_terms(down_near[1], down_near[0], far_down),
        0: grad_terms(gate_up_near[1], gate_up_near[0], far_gate),
        1: grad_terms(gate_up_near[3], gate_up_near[2], far_upper),
    }
    state = (expert_master, expert_left, expert_right, expert_left_root, expert_right_root)
    updated = expert_update(
        0, parts[0], state, None, [far_down, swap_core(far_gate), qkv_stages[0]] + parts[1][1:2]
    )
    loss_row = jnp.full((1, D), loss_part)
    sums = jnp.concatenate([gain_attention[None], gain_mix[None], loss_row], axis=0)
    sums = sum_group(after(sums, updated[0]))
    updated = expert_update(
        1, parts[1], state, updated, [input_grad, qkv_stages[2], sums] + parts[2][1:2]
    )
    sums = sum_groups(sums)
    updated = expert_update(2, parts[2], state, updated, [output_part])
    expert_grad, expert_left_new, expert_right_new, expert_new = updated
    attention_grad, attention_left_new, attention_right_new, attention_new = attention_update(
        qkv_part,
        output_part,
        (
            attention_master,
            attention_left[0],
            attention_right[0],
            attention_left_root[0],
            attention_right_root[0],
        ),
    )
    gain_grad = sums[:2]
    mean_loss = sums[2, 0] / valid_total
    gains_new = norm_gains - gain_rate * tokens_total**0.5 * gain_grad

    return (
        output,
        mean_loss,
        input_grad,
        gain_grad,
        gains_new,
        attention_grad,
        attention_left_new[None],
        attention_right_new[None],
        attention_new,
        expert_grad,
        expert_left_new,
        expert_right_new,
        expert_new,
    )


def solution(mesh):
    return jax.shard_map(
        on_device,
        mesh=mesh,
        in_specs=(
            P(("dp", "tensor"), None),
            P(("dp", "tensor"), None),
            P("dp"),
            P(("dp", "tensor")),
            P("dp", None),
            P("dp", None),
            P(),
            P("dp", "tensor"),
            P("dp", None, "tensor", None),
            P("dp", "tensor", None, None),
            P("dp", "tensor", None, None),
            P("dp", "tensor", None, None),
            P("dp", "tensor", None, None),
            P("dp", None, None, "tensor", None),
            P("dp", None, "tensor", None, None),
            P("dp", None, None, "tensor", None),
            P("dp", None, "tensor", None, None),
        ),
        out_specs=(
            P(("dp", "tensor"), None),
            P(),
            P(("dp", "tensor"), None),
            P(),
            P(),
            P("dp", "tensor"),
            P("dp", "tensor", None, None),
            P("dp", "tensor", None, None),
            P("dp", "tensor"),
            P("dp", None, "tensor", None),
            P("dp", None, None, "tensor", None),
            P("dp", None, "tensor", None, None),
            P("dp", None, "tensor", None),
        ),
        check_vma=False,
    )
```

```python
import functools

import jax
import jax.numpy as jnp
from jax import lax
from jax.experimental import pallas as pl
from jax.experimental.pallas import tpu as pltpu
from jax.sharding import PartitionSpec as P

D = 1024
HEADS = 16
KV_HEADS = 8
HEAD_DIM = 64
EXPERTS = 32
TOPK = 8
BLK = 256
GROUPS = 4
BLOCK = 256
LANES = 128

epsilon = 1e-05
stat_decay = 0.9
gain_rate = 0.02
theta_base = 10000.0
masked_score = -1e30
MIB = 1 << 20
SMALL = pl.CostEstimate(flops=1000, bytes_accessed=1000, transcendentals=0)


def cost(flops):
    return pl.CostEstimate(flops=int(flops), bytes_accessed=1000, transcendentals=0)


ANYWHERE = pl.BlockSpec(memory_space=pl.ANY)
SCALARS = pl.BlockSpec(memory_space=pltpu.SMEM)

TOKEN_MASKS = (0, 1, 4, 5)
WEIGHT_BITS = (2, 8)


def dot(left, right, left_dim, right_dim):
    return lax.dot_general(
        left, right, (((left_dim,), (right_dim,)), ((), ())), preferred_element_type=jnp.float32
    )


def normalize(hidden, gain):
    scaling = lax.rsqrt(jnp.mean(hidden * hidden, axis=-1, keepdims=True) + epsilon)
    return (hidden * scaling * gain, scaling)


def normalize_back(hidden, scaling, gain, upstream):
    weighted = upstream * gain
    center = jnp.mean(weighted * hidden, axis=-1, keepdims=True)
    input_part = scaling * weighted - hidden * (scaling * scaling * scaling) * center
    return (input_part, jnp.sum(upstream * hidden * scaling, axis=0))


def swap_dp(values, mask):
    count = lax.axis_size("dp")
    return lax.ppermute(values, "dp", [(i, i ^ mask) for i in range(count)])


def swap_core(values):
    count = lax.axis_size("tensor")
    return lax.ppermute(values, "tensor", [(i, i ^ 1) for i in range(count)])


def sum_everywhere(values):
    values = values + swap_core(values)
    own = sum(values if mask == 0 else swap_dp(values, mask) for mask in TOKEN_MASKS)
    masks = [m for m in range(1, lax.axis_size("dp")) if not m & TOKEN_MASKS[-1]]
    return own + sum(swap_dp(own, mask) for mask in masks)


def in_order(own, other):
    first = lax.axis_index("tensor") == 0
    return jnp.concatenate([jnp.where(first, own, other), jnp.where(first, other, own)], axis=0)


def own_half(values):
    half = values.shape[0] // 2
    return lax.dynamic_slice_in_dim(values, lax.axis_index("tensor") * half, half, 0)


def other_half(values):
    half = values.shape[0] // 2
    return lax.dynamic_slice_in_dim(values, (1 - lax.axis_index("tensor")) * half, half, 0)


def turn(values):
    lane = lax.broadcasted_iota(jnp.int32, values.shape, 1)
    half = HEAD_DIM // 2
    return jnp.where(
        lane % HEAD_DIM < half,
        -pltpu.roll(values, LANES - half, 1),
        pltpu.roll(values, half, 1),
    )


def place_rows(starts_ref, source_refs, target_ref):
    for group, source_ref in enumerate(source_refs):
        count = starts_ref.shape[1]
        slot_rows = source_ref.shape[0] // count
        rows = target_ref.shape[0] // count // len(source_refs)
        for slot in range(count):
            start = pl.multiple_of(starts_ref[group, slot], rows)
            begin = slot * slot_rows
            target_ref[pl.ds(start, rows), :] = source_ref[begin : begin + rows, :]


def attention_forward_kernel(*refs):
    length_ref, starts_ref, x_ref, w0_ref, w1_ref, w2_ref, w3_ref, cos_ref, sin_ref = refs[:9]
    q_ref, k_ref, v_ref, att_ref, w_ref, lse_ref = refs[-6:]
    rows = x_ref.shape[0]
    place_rows(starts_ref, (w0_ref, w1_ref, w2_ref, w3_ref), w_ref)
    low = jnp.bfloat16
    cosine, sine = cos_ref[...], sin_ref[...]
    lane = lax.broadcasted_iota(jnp.int32, (rows, LANES), 1)
    left = lane < HEAD_DIM
    projected = dot(x_ref[...], w_ref[...], 1, 0)
    q_raw = projected[:, :LANES]
    q_turn = turn(q_raw)
    scale = HEAD_DIM ** (-0.5)
    q_rot = (q_raw * cosine + q_turn * sine) * scale
    q_rot_turn = (q_turn * cosine - q_raw * sine) * scale
    q_ref[:, :LANES] = jnp.where(left, q_rot, pltpu.roll(q_rot_turn, HEAD_DIM, 1)).astype(low)
    q_ref[:, LANES:] = jnp.where(left, pltpu.roll(q_rot, HEAD_DIM, 1), q_rot_turn).astype(low)
    kv_raw = projected[:, LANES:]
    k_turn = turn(kv_raw)
    k_rot = kv_raw * cosine + k_turn * sine
    k_rot_turn = k_turn * cosine - kv_raw * sine
    k_ref[...] = jnp.where(left, k_rot, pltpu.roll(k_rot_turn, HEAD_DIM, 1)).astype(low)
    v_high = jnp.where(left, 0.0, kv_raw)
    v_ref[...] = v_high.astype(low)
    v_low = pltpu.roll(v_high, HEAD_DIM, 1).astype(low)
    v_high = v_high.astype(low)
    k_only = jnp.where(left, k_rot, 0.0).astype(low)
    place = lax.broadcasted_iota(jnp.int32, (1, rows), 1)
    bias = jnp.where(place < length_ref[0], 0.0, masked_score)
    for block in range(rows // BLK):
        here = pl.ds(block * BLK, BLK)
        keys = (block + 1) * BLK
        total = None
        for head in range(2):
            q_block = q_ref[here, head * LANES : (head + 1) * LANES]
            scores = dot(q_block, k_only[:keys], 1, 1) + bias[:, :keys]
            top = jnp.max(scores, axis=1, keepdims=True)
            exponent = jnp.exp(scores - top)
            denominator = jnp.sum(exponent, axis=1, keepdims=True)
            weights = (exponent * (1.0 / denominator)).astype(low)
            value = v_high if head else v_low
            part = dot(weights, value[:keys], 1, 0)
            total = part if total is None else total + part
            log_total = jnp.broadcast_to(top + jnp.log(denominator), (BLK, LANES))
            lse_ref[head * 8 : (head + 1) * 8, here] = log_total.T[:8]
        att_ref[here, :] = total.astype(low)


def attention_backward_kernel(*refs):
    length_ref, branch_ref, wo_ref, q_ref, k_ref, v_ref, lse_ref, cos_ref, sin_ref = refs[:9]
    dq_ref, dkv_ref, dk_sum, d0_sum, d1_sum = refs[-5:]
    rows = branch_ref.shape[0]
    low = jnp.bfloat16
    lane = lax.broadcasted_iota(jnp.int32, (rows, LANES), 1)
    left = lane < HEAD_DIM
    grad = dot(branch_ref[...], wo_ref[...], 1, 0).astype(low)
    k_only = jnp.where(left, k_ref[...].astype(jnp.float32), 0.0).astype(low)
    v_high = v_ref[...]
    v_low = pltpu.roll(v_high.astype(jnp.float32), HEAD_DIM, 1).astype(low)
    place = lax.broadcasted_iota(jnp.int32, (rows, BLK), 0)
    seen = place < length_ref[0]
    dk_sum[...] = jnp.zeros_like(dk_sum)
    d0_sum[...] = jnp.zeros_like(d0_sum)
    d1_sum[...] = jnp.zeros_like(d1_sum)
    scale = HEAD_DIM ** (-0.5)
    for block in range(rows // BLK):
        here = pl.ds(block * BLK, BLK)
        keys = (block + 1) * BLK
        grad_block = grad[block * BLK : keys]
        query_grads = []
        for head in range(2):
            q_block = q_ref[here, head * LANES : (head + 1) * LANES]
            value = v_high if head else v_low
            scores = dot(k_only[:keys], q_block, 1, 1)
            log_total = lse_ref[head * 8 : head * 8 + 1, here]
            scores = jnp.where(seen[:keys], scores, masked_score)
            probability = jnp.exp(scores - log_total)
            prob_grad = dot(value[:keys], grad_block, 1, 1)
            weighted = probability * prob_grad
            center = jnp.sum(weighted, axis=0, keepdims=True)
            score_grad = (weighted - probability * center).astype(low)
            d_sum = d1_sum if head else d0_sum
            d_sum[:keys] += dot(probability.astype(low), grad_block, 1, 0)
            dk_sum[:keys] += dot(score_grad, q_block, 1, 0)
            query_grads.append(dot(score_grad, k_ref[:keys], 0, 0))
        cosine, sine = cos_ref[here, :] * scale, sin_ref[here, :] * scale
        zero, one = query_grads
        left_here = left[:BLK]
        straight = jnp.where(left_here, zero, pltpu.roll(one, HEAD_DIM, 1))
        turned = jnp.where(left_here, pltpu.roll(zero, HEAD_DIM, 1), one)
        dq_ref[here, :] = (straight * cosine - turned * sine).astype(low)
    dk_all = dk_sum[...]
    dk_rot = dk_all * cos_ref[...] - pltpu.roll(dk_all, HEAD_DIM, 1) * sin_ref[...]
    dv_all = pltpu.roll(d0_sum[...], HEAD_DIM, 1) + d1_sum[...]
    dkv_ref[...] = jnp.where(left, dk_rot, dv_all).astype(low)


def whole(shape):
    return pl.BlockSpec(shape, lambda h: (0,) * len(shape))


def columns(rows, width):
    return pl.BlockSpec((rows, width), lambda h: (0, h))


def attention_forward(length, starts, normed, w_groups, cosine, sine, deps=()):
    rows = normed.shape[0]
    kv_here = w_groups[0].shape[1] // 256
    low = jnp.bfloat16
    return pl.pallas_call(
        attention_forward_kernel,
        grid=(kv_here,),
        in_specs=[SCALARS, SCALARS, whole((rows, D))]
        + [columns(w.shape[0], 256) for w in w_groups]
        + [whole((rows, LANES))] * 2
        + [ANYWHERE] * len(deps),
        out_specs=[
            columns(rows, 256),
            columns(rows, LANES),
            columns(rows, LANES),
            columns(rows, LANES),
            columns(D, 256),
            pl.BlockSpec((16, rows), lambda h: (h, 0)),
        ],
        out_shape=[
            jax.ShapeDtypeStruct((rows, kv_here * 256), low),
            jax.ShapeDtypeStruct((rows, kv_here * LANES), low),
            jax.ShapeDtypeStruct((rows, kv_here * LANES), low),
            jax.ShapeDtypeStruct((rows, kv_here * LANES), low),
            jax.ShapeDtypeStruct((D, kv_here * 256), low),
            jax.ShapeDtypeStruct((kv_here * 16, rows), jnp.float32),
        ],
        compiler_params=pltpu.CompilerParams(vmem_limit_bytes=50 * MIB),
        cost_estimate=SMALL,
        name="attention_forward",
    )(length, starts, normed, *w_groups, cosine, sine, *deps)


def output_projection_kernel(*refs):
    starts_ref, core_ref, att_ref, w0_ref, w1_ref, w2_ref, w3_ref = refs[:7]
    own_ref, other_ref, w_ref = refs[-3:]
    place_rows(starts_ref, (w0_ref, w1_ref, w2_ref, w3_ref), w_ref)
    half = own_ref.shape[0]
    mine = pl.multiple_of(core_ref[0] * half, half)
    others = pl.multiple_of((1 - core_ref[0]) * half, half)
    other_ref[...] = dot(att_ref[pl.ds(others, half), :], w_ref[...], 1, 1).astype(jnp.bfloat16)
    own_ref[...] = dot(att_ref[pl.ds(mine, half), :], w_ref[...], 1, 1)


def output_projection(starts, core, attended, w_groups, deps=()):
    rows, width = attended.shape
    inside = pl.BlockSpec(memory_space=pltpu.VMEM)
    return pl.pallas_call(
        output_projection_kernel,
        in_specs=[SCALARS, SCALARS] + [inside] * 5 + [ANYWHERE] * len(deps),
        out_specs=[inside] * 3,
        out_shape=[
            jax.ShapeDtypeStruct((rows // 2, D), jnp.float32),
            jax.ShapeDtypeStruct((rows // 2, D), jnp.bfloat16),
            jax.ShapeDtypeStruct((D, width), jnp.bfloat16),
        ],
        compiler_params=pltpu.CompilerParams(vmem_limit_bytes=32 * MIB),
        cost_estimate=SMALL,
        name="output_projection",
    )(starts, core, attended, *w_groups, *deps)


def nothing(*refs):
    return None


def after(values, *deps):
    return pl.pallas_call(
        nothing,
        in_specs=[ANYWHERE] * (1 + len(deps)),
        out_specs=ANYWHERE,
        out_shape=jax.ShapeDtypeStruct(values.shape, values.dtype),
        input_output_aliases={0: 0},
        cost_estimate=SMALL,
        name="after",
    )(values, *deps)


def round_kernel(bounds, values_ref, whole_ref, *piece_refs):
    step = pl.program_id(0)
    rounded = values_ref[...].astype(jnp.bfloat16)
    whole_ref[...] = rounded
    for (begin, end), piece_ref in zip(bounds, piece_refs):

        @pl.when((step >= begin) & (step < end))
        def _(piece_ref=piece_ref):
            piece_ref[...] = rounded


def round_units(values, bounds):
    units = values.shape[0]
    shape = (None,) + values.shape[1:]

    def piece_spec(begin, end):
        return pl.BlockSpec(shape, lambda i: (jnp.clip(i - begin, 0, end - begin - 1), 0, 0, 0))

    return pl.pallas_call(
        functools.partial(round_kernel, bounds),
        grid=(units,),
        in_specs=[pl.BlockSpec(shape, lambda i: (i, 0, 0, 0))],
        out_specs=[pl.BlockSpec(shape, lambda i: (i, 0, 0, 0))]
        + [piece_spec(begin, end) for begin, end in bounds],
        out_shape=[jax.ShapeDtypeStruct(values.shape, jnp.bfloat16)]
        + [
            jax.ShapeDtypeStruct((end - begin,) + values.shape[1:], jnp.bfloat16)
            for begin, end in bounds
        ],
        cost_estimate=SMALL,
        name="round_units",
    )(values)


def attention_backward(length, branch_low, w_output, q2, k2, v, lse, cosine, sine, deps=()):
    rows = branch_low.shape[0]
    kv_here = k2.shape[1] // LANES
    low = jnp.bfloat16
    return pl.pallas_call(
        attention_backward_kernel,
        grid=(kv_here,),
        in_specs=[
            SCALARS,
            whole((rows, D)),
            columns(D, LANES),
            columns(rows, 256),
            columns(rows, LANES),
            columns(rows, LANES),
            pl.BlockSpec((16, rows), lambda h: (h, 0)),
            whole((rows, LANES)),
            whole((rows, LANES)),
        ]
        + [pl.BlockSpec(memory_space=pl.ANY)] * len(deps),
        out_specs=[columns(rows, LANES), columns(rows, LANES)],
        out_shape=[
            jax.ShapeDtypeStruct((rows, kv_here * LANES), low),
            jax.ShapeDtypeStruct((rows, kv_here * LANES), low),
        ],
        scratch_shapes=[pltpu.VMEM((rows, LANES), jnp.float32)] * 3,
        compiler_params=pltpu.CompilerParams(vmem_limit_bytes=50 * MIB),
        cost_estimate=SMALL,
        name="attention_backward",
    )(length, branch_low, w_output, q2, k2, v, lse, cosine, sine, *deps)


CHUNK = 512
UNIT_ROWS = 64


def first_unit(piece_refs, piece):
    return sum(p.shape[0] for p in piece_refs[:piece])


def piece_copy(piece_refs, weights, arrived, piece, kind):
    units = piece_refs[piece].shape[0]
    return pltpu.make_async_copy(
        piece_refs[piece].at[:, kind],
        weights.at[kind, pl.ds(first_unit(piece_refs, piece), units)],
        arrived.at[piece, kind],
    )


def row_copy(row_refs, rows_all, landed, index):
    count = len(row_refs) - 1
    rows = row_refs[0].shape[0]
    source = row_refs[index // 2]
    if index % 2:
        source = row_refs[count].at[pl.ds(index // 2 * rows, rows)]
    return pltpu.make_async_copy(
        source, rows_all.at[pl.ds(index * rows, rows)], landed.at[index]
    )


def fetch(piece_refs, weights, arrived, row_refs=(None,), rows_all=None, landed=None):
    @pl.when(pl.program_id(0) == 0)
    def _():
        copies = [
            row_copy(row_refs, rows_all, landed, index) for index in range(2 * len(row_refs) - 2)
        ]
        copies += [
            piece_copy(piece_refs, weights, arrived, piece, kind)
            for piece in range(len(piece_refs))
            for kind in range(3)
        ]
        for copy in copies:
            copy.start()
        for copy in copies:
            copy.wait()


def chunk_weights(weights, kind, chunk):
    units = CHUNK // UNIT_ROWS
    return weights[kind, chunk * units : (chunk + 1) * units].reshape(CHUNK, D)


def spread_weights(route_ref, column, per_unit):
    rows = route_ref.shape[0]
    units = CHUNK // UNIT_ROWS
    count = units if per_unit else units // 4
    width = CHUNK // count
    pieces = [
        jnp.broadcast_to(route_ref[:, column * count + j : column * count + j + 1], (rows, width))
        for j in range(count)
    ]
    return jnp.concatenate(pieces, axis=1)


def store_step(out_refs, values):
    step = pl.program_id(0)
    for index, out_ref in enumerate(out_refs):

        @pl.when(step == index)
        def _(out_ref=out_ref):
            out_ref[...] = values


def expert_hidden(x, route_ref, weights, first_column, per_unit, outs):
    low = jnp.bfloat16
    slope_ref, silu_ref, inner_ref = outs
    for chunk in range(slope_ref.shape[1] // CHUNK):
        here = slice(chunk * CHUNK, (chunk + 1) * CHUNK)
        gate = dot(x, chunk_weights(weights, 0, chunk), 1, 1)
        upper = dot(x, chunk_weights(weights, 1, chunk), 1, 1)
        sigmoid = 0.5 * jnp.tanh(0.5 * gate) + 0.5
        silu = gate * sigmoid
        weight = spread_weights(route_ref, first_column + chunk, per_unit)
        weighted_upper = weight * upper
        slope_ref[:, here] = (weighted_upper * (sigmoid + silu * (1.0 - sigmoid))).astype(low)
        silu_ref[:, here] = (weight * silu).astype(low)
        inner_ref[:, here] = (silu * weighted_upper).astype(low)
    return dot(inner_ref[...], weights[2].reshape(-1, D), 1, 0)


def expert_first_kernel(count, pieces, per_unit, *refs):
    parts = count // 2 + 1
    row_refs, route_ref = refs[:parts], refs[parts]
    piece_refs = refs[parts + 1 : parts + 1 + pieces]
    x_ref, mixed_ref, slope_ref, silu_ref, inner_ref = refs[-9:-4]
    weights, arrived, rows_all, landed = refs[-4:]
    fetch(piece_refs, weights, arrived, row_refs, rows_all, landed)
    rows = x_ref.shape[0]
    x = rows_all[pl.ds(pl.multiple_of(pl.program_id(0) * rows, rows), rows), :]
    x_ref[...] = x
    outs = (slope_ref, silu_ref, inner_ref)
    mixed_ref[...] = expert_hidden(
        x, route_ref, weights, 0, per_unit, outs
    ).astype(jnp.bfloat16)


def expert_second_kernel(count, pieces, per_unit, first_column, *refs):
    x_ref, mixed_ref, route_ref = refs[:3]
    piece_refs = refs[3 : 3 + pieces]
    out_refs = refs[-5 - count : -5]
    weights, arrived = refs[-2:]
    fetch(piece_refs, weights, arrived)
    part = expert_hidden(
        x_ref[...], route_ref, weights, first_column, per_unit, refs[-5:-2]
    )
    store_step(out_refs, (part + mixed_ref[...].astype(jnp.float32)).astype(jnp.bfloat16))


def expert_backward_kernel(count, pieces, *refs):
    parts = count // 2 + 1
    row_refs = refs[:parts]
    slope_refs, silu_refs = refs[parts : parts + 2], refs[parts + 2 : parts + 4]
    piece_refs = refs[parts + 4 : parts + 4 + pieces]
    out_refs = refs[-9 - count : -9]
    grad_ref = refs[-9]
    gate_refs, upper_refs = refs[-8:-6], refs[-6:-4]
    weights, arrived, rows_all, landed = refs[-4:]
    low = jnp.bfloat16
    fetch(piece_refs, weights, arrived, row_refs, rows_all, landed)
    rows = grad_ref.shape[0]
    grad = rows_all[pl.ds(pl.multiple_of(pl.program_id(0) * rows, rows), rows), :]
    grad_ref[...] = grad
    chunks = slope_refs[0].shape[1] // CHUNK
    for chunk in range(2 * chunks):
        half, place = chunk // chunks, chunk % chunks
        here = slice(place * CHUNK, (place + 1) * CHUNK)
        inner_grad = dot(grad, chunk_weights(weights, 2, chunk), 1, 1)
        slope, silu = slope_refs[half][:, here], silu_refs[half][:, here]
        gate_refs[half][:, here] = (inner_grad * slope.astype(jnp.float32)).astype(low)
        upper_refs[half][:, here] = (inner_grad * silu.astype(jnp.float32)).astype(low)
    units = weights.shape[1] // 2
    total = None
    for half in range(2):
        mine = pl.ds(half * units, units)
        part = dot(gate_refs[half][...], weights[0, mine].reshape(-1, D), 1, 0)
        part = part + dot(upper_refs[half][...], weights[1, mine].reshape(-1, D), 1, 0)
        total = part if total is None else total + part
    store_step(out_refs, total.astype(low))


def fixed(shape):
    return pl.BlockSpec(shape, lambda i: (0,) * len(shape))


def token_block(rows, width, first=0):
    return pl.BlockSpec((rows, width), lambda i: (first + i, 0))


def expert_scratch(pieces, count=0, rows=0):
    units = sum(p.shape[0] for p in pieces)
    scratch = [
        pltpu.VMEM((3, units, UNIT_ROWS, D), jnp.bfloat16),
        pltpu.SemaphoreType.DMA((len(pieces), 3)),
    ]
    if count:
        scratch += [
            pltpu.VMEM((count * rows, D), jnp.bfloat16),
            pltpu.SemaphoreType.DMA((count,)),
        ]
    return scratch


def expert_call(
    kernel, name, steps, operands, specs, out_specs, widths, singles, kept, scratch, estimate=SMALL
):
    rows, total_rows = singles[1], singles[2]
    low = jnp.bfloat16
    operands, specs = list(operands), list(specs)
    aliases = {}
    if kept is not None:
        for index, buffer in enumerate(kept):
            aliases[len(operands)] = singles[0] + index
            operands.append(buffer)
            specs.append(ANYWHERE)
    outs = pl.pallas_call(
        kernel,
        grid=(steps,),
        in_specs=specs,
        out_specs=[fixed((rows, D))] * singles[0] + out_specs,
        out_shape=[jax.ShapeDtypeStruct((rows, D), low)] * singles[0]
        + [jax.ShapeDtypeStruct((total_rows, w), low) for w in widths],
        scratch_shapes=scratch,
        input_output_aliases=aliases,
        compiler_params=pltpu.CompilerParams(vmem_limit_bytes=60 * MIB),
        cost_estimate=estimate,
        name=name,
    )(*operands)
    return outs[: singles[0]], outs[singles[0] :]


def expert_first(row_parts, route_columns, per_unit, pieces, deps):
    count, rows = 2 * len(row_parts) - 2, row_parts[0].shape[0]
    width = sum(p.shape[0] for p in pieces) * UNIT_ROWS
    widths = [D, D, width, width, width]
    return expert_call(
        functools.partial(expert_first_kernel, count, len(pieces), per_unit),
        "expert_first",
        count,
        list(row_parts) + [route_columns] + list(pieces) + list(deps),
        [ANYWHERE] * len(row_parts)
        + [token_block(rows, route_columns.shape[1])]
        + [ANYWHERE] * (len(pieces) + len(deps)),
        [token_block(rows, w) for w in widths],
        widths,
        (0, rows, count * rows),
        None,
        expert_scratch(pieces, count, rows),
        cost(6 * count * rows * width * D),
    )[1]


def expert_second(count, rows, x, mixed, route_columns, per_unit, pieces, deps):
    width = sum(p.shape[0] for p in pieces) * UNIT_ROWS
    return expert_call(
        functools.partial(expert_second_kernel, count, len(pieces), per_unit, width // CHUNK),
        "expert_second",
        count,
        [x, mixed, route_columns] + list(pieces) + list(deps),
        [
            token_block(rows, D),
            token_block(rows, D),
            token_block(rows, route_columns.shape[1]),
        ]
        + [ANYWHERE] * (len(pieces) + len(deps)),
        [token_block(rows, width)] * 3,
        [width] * 3,
        (count, rows, x.shape[0]),
        None,
        expert_scratch(pieces),
    )


def expert_backward(first, row_parts, slopes, silus, pieces, kept):
    count, rows = 2 * len(row_parts) - 2, row_parts[0].shape[0]
    width = slopes[0].shape[1]
    widths = [D] + [width] * 4
    return expert_call(
        functools.partial(expert_backward_kernel, count, len(pieces)),
        "expert_backward",
        count,
        list(row_parts) + list(slopes) + list(silus) + list(pieces),
        [ANYWHERE] * len(row_parts)
        + [token_block(rows, width, first)] * 4
        + [ANYWHERE] * len(pieces),
        [token_block(rows, w, first) for w in widths],
        widths,
        (count, rows, slopes[0].shape[0]),
        kept,
        expert_scratch(pieces, count, rows),
    )


def weight_grad_kernel(count, *refs):
    right_ref = refs[count]
    outs = refs[-2 * count :]
    step = pl.program_id(0)
    for index in range(count):
        for slot in range(2):

            @pl.when(step == 2 * index + slot)
            def _(index=index, slot=slot):
                outs[2 * index + slot][...] = dot(refs[index][...], right_ref[...], 0, 0).astype(
                    jnp.bfloat16
                )


def weight_grads(lefts, right, deps=(), estimate=SMALL):
    rows = right.shape[0]
    columns_here = lefts[0].shape[1] // 2
    count = len(lefts)

    def left_spec(index):
        return pl.BlockSpec(
            (rows, columns_here), lambda i: (0, 1 - jnp.clip(i - 2 * index, 0, 1))
        )

    return pl.pallas_call(
        functools.partial(weight_grad_kernel, count),
        grid=(2 * count,),
        in_specs=[left_spec(index) for index in range(count)]
        + [pl.BlockSpec((rows, D), lambda i: (0, 0), pipeline_mode=pl.Buffered(1))]
        + [ANYWHERE] * len(deps),
        out_specs=[fixed((columns_here, D))] * (2 * count),
        out_shape=[jax.ShapeDtypeStruct((columns_here, D), jnp.bfloat16)] * (2 * count),
        compiler_params=pltpu.CompilerParams(vmem_limit_bytes=56 * MIB),
        cost_estimate=estimate,
        name="weight_grads",
    )(*lefts, right, *deps)


def update_blocks(grads, lefts, rights, left_roots, right_roots, left_outs, right_outs, step_outs):
    low = jnp.bfloat16
    grads = [grad.astype(low) for grad in grads]
    firsts = [
        dot(root[...].astype(low), grad, 1, 0).astype(low) for root, grad in zip(left_roots, grads)
    ]
    for grad, left, out in zip(grads, lefts, left_outs):
        out[...] = stat_decay * left[...] + dot(grad, grad, 1, 1)
    for first, root, (out, master) in zip(firsts, right_roots, step_outs):
        out[...] = master[...] - D ** (-0.5) * dot(first, root[...].astype(low), 1, 0)
    for grad, right, out in zip(grads, rights, right_outs):
        out[...] = stat_decay * right[...] + dot(grad, grad, 0, 0)


def expert_update_kernel(count, *refs):
    parts = refs[:count]
    master, left, right, left_root, right_root = refs[count : count + 5]
    grad_out, left_out, right_out, new_out = refs[-4:]
    units, rows, _ = grad_out.shape
    grad = parts[0][...].astype(jnp.float32)
    for part in parts[1:]:
        grad = grad + part[...].astype(jnp.float32)
    grad = grad.reshape(units, rows, D)
    grad_out[...] = grad
    blocks = [(u, b) for u in range(units) for b in range(D // BLOCK)]

    def wide(ref):
        return [ref.at[u, :, b * BLOCK : (b + 1) * BLOCK] for u, b in blocks]

    def square(ref):
        return [ref.at[u, b] for u, b in blocks]

    update_blocks(
        [grad[u, :, b * BLOCK : (b + 1) * BLOCK] for u, b in blocks],
        square(left),
        square(right),
        square(left_root),
        square(right_root),
        square(left_out),
        square(right_out),
        list(zip(wide(new_out), wide(master))),
    )


def expert_update(kind, parts, state, kept, deps=()):
    master, left, right, left_root, right_root = state
    units, _, rows, _ = master.shape
    step = min(units, 2)
    flat = pl.BlockSpec((step, None, rows, D), lambda i: (i, kind, 0, 0))
    lefts = pl.BlockSpec((step, None) + left.shape[2:], lambda i: (i, kind, 0, 0, 0))
    rights = pl.BlockSpec((step, None) + right.shape[2:], lambda i: (i, kind, 0, 0, 0))
    operands = list(parts) + list(state) + list(deps)
    specs = [pl.BlockSpec((step * rows, D), lambda i: (i, 0))] * len(parts)
    specs += [flat, lefts, rights, lefts, rights] + [ANYWHERE] * len(deps)
    aliases = {}
    if kept is not None:
        for index, buffer in enumerate(kept):
            aliases[len(operands)] = index
            operands.append(buffer)
            specs.append(ANYWHERE)
    return pl.pallas_call(
        functools.partial(expert_update_kernel, len(parts)),
        grid=(units // step,),
        in_specs=specs,
        out_specs=[flat, lefts, rights, flat],
        out_shape=[jax.ShapeDtypeStruct(a.shape, jnp.float32) for a in (master, left, right, master)],
        input_output_aliases=aliases,
        compiler_params=pltpu.CompilerParams(vmem_limit_bytes=56 * MIB),
        cost_estimate=cost(12e9),
        name="expert_update",
    )(*operands)


def attention_update_kernel(qkv_ref, wo_ref, master, left, right, left_root, right_root, *outs):
    grad_out, left_out, right_out, new_out = outs
    heads = qkv_ref.shape[1] // 256
    rows = qkv_ref.shape[0]
    low_lanes = lax.broadcasted_iota(jnp.int32, (rows, LANES), 1) < HEAD_DIM
    grad = qkv_ref[...].astype(jnp.float32)
    queries = heads * LANES
    keys = queries // 2
    for head in range(heads):
        grad_out[:, head * LANES : (head + 1) * LANES] = grad[:, head * 256 : head * 256 + LANES]
    for pair in range(heads // 2):
        begin = pair * 512 + LANES
        one, two = grad[:, begin : begin + LANES], grad[:, begin + 256 : begin + 256 + LANES]
        place = queries + pair * LANES
        grad_out[:, place : place + LANES] = jnp.where(low_lanes, one, pltpu.roll(two, HEAD_DIM, 1))
        place = place + keys
        grad_out[:, place : place + LANES] = jnp.where(low_lanes, pltpu.roll(one, HEAD_DIM, 1), two)
    grad_out[:, queries + 2 * keys :] = wo_ref[...].astype(jnp.float32)
    blocks = range(grad_out.shape[1] // BLOCK)

    def wide(ref):
        return [ref.at[:, b * BLOCK : (b + 1) * BLOCK] for b in blocks]

    def square(ref):
        return [ref.at[b] for b in blocks]

    update_blocks(
        [part[...] for part in wide(grad_out)],
        square(left),
        square(right),
        square(left_root),
        square(right_root),
        square(left_out),
        square(right_out),
        list(zip(wide(new_out), wide(master))),
    )


def attention_update(qkv_part, output_part, state):
    inside = pl.BlockSpec(memory_space=pltpu.VMEM)
    master, left, right = state[:3]
    return pl.pallas_call(
        attention_update_kernel,
        in_specs=[inside] * 7,
        out_specs=[inside] * 4,
        out_shape=[jax.ShapeDtypeStruct(a.shape, jnp.float32) for a in (master, left, right, master)],
        compiler_params=pltpu.CompilerParams(vmem_limit_bytes=40 * MIB),
        cost_estimate=SMALL,
        name="attention_update",
    )(qkv_part, output_part, *state)


def spread_tokens(own, relay):
    beside, across, both = TOKEN_MASKS[1:]
    rows = [own, swap_dp(own, beside), swap_dp(own, across)]
    return rows + [swap_dp(rows[2], beside) if relay else swap_dp(own, both)]


def with_other(own_rows):
    return list(own_rows) + [swap_core(jnp.concatenate(own_rows, axis=0))]


def sum_cores(place, parts):
    own, other = parts
    total = own.astype(jnp.float32) + swap_core(other).astype(jnp.float32)
    return total if place == 0 else total.astype(jnp.bfloat16)


def return_tokens(sums):
    return [swap_dp(rows, mask) for rows, mask in zip(sums[1:], TOKEN_MASKS[1:])]


def add_all(first, others):
    for rows in others:
        first = first + rows.astype(jnp.float32)
    return first


def extra_masks():
    count = lax.axis_size("dp")
    used = sum(WEIGHT_BITS) + TOKEN_MASKS[-1]
    masks = []
    mask = 1
    while mask < count:
        if not mask & used:
            masks.append(mask)
        mask *= 2
    return masks


def gather_attention(own, count, qkv_cols, deps):
    low = jnp.bfloat16
    high_digit = jnp.floor(count / 64.0)
    digits = jnp.stack([high_digit, count - 64.0 * high_digit]).astype(low)
    digits = jnp.pad(digits[None, :], ((0, 7), (0, own.shape[1] - 2)))
    own = jnp.concatenate([own, digits], axis=0)
    slot_rows = own.shape[0]
    masks, line, mask = [0], own, lax.axis_size("dp") // 2
    while mask > 2:
        line = jnp.concatenate([line, swap_dp(line, mask)], axis=0)
        masks = masks + [m ^ mask for m in masks]
        mask //= 2
    line = after(line, *deps)
    inner, outer = line[:, :qkv_cols], line[:, qkv_cols:]
    inner = [inner] + [swap_dp(inner, mask) for mask in (1, 2, 3)]
    outer = [outer] + [swap_dp(outer, mask) for mask in (1, 2, 3)]
    table = jnp.array([[group ^ mask for mask in masks] for group in range(4)], jnp.int32)
    total = 0.0
    for group in inner:
        digits = group.reshape(len(masks), slot_rows, -1)[:, slot_rows - 8, :2]
        digits = jnp.sum(digits.astype(jnp.float32), axis=0)
        total = total + 64.0 * digits[0] + digits[1]
    total = total.reshape(1, 1)
    return line, inner, outer, lax.axis_index("dp") ^ table, (total + swap_core(total))[0, 0]


FAR_PIECES = ((0, 4), (4, 8))
NEAR_PIECES = ((0, 3), (3, 8))


def round_weights(master):
    bounds = FAR_PIECES + NEAR_PIECES
    extra = extra_masks()
    if not extra:
        shard, *pieces = round_units(master, bounds)
    else:
        shard = round_units(master, ())[0]
        for mask in extra:
            shard = jnp.concatenate([shard, swap_dp(shard, mask)], axis=0)
        pieces = [shard[begin:end] for begin, end in bounds]
    return shard, pieces[: len(FAR_PIECES)], pieces[len(FAR_PIECES) :]


def unit_owners():
    masks = [0]
    for mask in extra_masks():
        masks = masks + [m ^ mask for m in masks]
    first, second = WEIGHT_BITS
    masks = [m ^ k for k in (0, first, second, first ^ second) for m in masks]
    return lax.axis_index("dp") ^ jnp.array(masks, jnp.int32)


def scatter_rows(values):
    low = jnp.bfloat16
    count = lax.axis_size("dp")
    bits = count.bit_length() - 1
    values = values.reshape((2,) * bits + (values.shape[0] // count, values.shape[1]))
    left = list(range(bits - 1, -1, -1))
    order = [0, 2, 1] + list(range(3, bits))
    stages = []
    for bit in order:
        axis = left.index(bit)
        left.pop(axis)
        here = (lax.axis_index("dp") >> bit) & 1
        mine = lax.dynamic_index_in_dim(values, here, axis, keepdims=False)
        other = lax.dynamic_index_in_dim(values, 1 - here, axis, keepdims=False)
        sent = swap_dp(other, 1 << bit)
        values = (mine.astype(jnp.float32) + sent.astype(jnp.float32)).astype(low)
        stages.append(values)
    return stages


def add_grads(far, both):
    return (far.astype(jnp.float32) + swap_dp(both, WEIGHT_BITS[0]).astype(jnp.float32)).astype(
        jnp.bfloat16
    )


def grad_terms(own, near, far):
    parts = [own, swap_dp(near, WEIGHT_BITS[0]), far]
    masks = extra_masks()
    if not masks:
        return parts
    total = sum(p.astype(jnp.float32) for p in parts)
    for mask in reversed(masks):
        half = total.shape[0] // 2
        sent = swap_dp(total[half:].astype(jnp.bfloat16), mask)
        total = total[:half] + sent.astype(jnp.float32)
    return [total]


def on_device(
    activations,
    targets,
    lengths,
    token_mask,
    routes,
    route_weights,
    norm_gains,
    attention_master,
    expert_master,
    attention_left,
    attention_right,
    attention_left_root,
    attention_right_root,
    expert_left,
    expert_right,
    expert_left_root,
    expert_right_root,
):
    low = jnp.bfloat16
    own_rows = activations.shape[0]
    tensor_size = lax.axis_size("tensor")
    core = lax.axis_index("tensor")
    tokens_total = own_rows * tensor_size * lax.axis_size("dp")
    seq_length = lengths[0]
    position = core * own_rows + jnp.arange(own_rows, dtype=jnp.int32)
    valid_rows = ((token_mask == 1) & (position < seq_length)).astype(jnp.float32)
    valid_here = jnp.sum(valid_rows)

    routing = jnp.concatenate([routes.T.astype(jnp.float32), route_weights.T], axis=0)
    routing_parts = [routing] + [swap_dp(routing, mask) for mask in TOKEN_MASKS[1:]]
    heads_here = HEADS // tensor_size
    kv_here = KV_HEADS // tensor_size
    query_cols = heads_here * HEAD_DIM
    key_cols = kv_here * HEAD_DIM
    qkv_cols = query_cols + 2 * key_cols
    rows_here = attention_master.shape[0]

    def by_head(values):
        rows = values.shape[0]
        query = values[:, :query_cols].reshape(rows, kv_here, LANES)
        key = values[:, query_cols : query_cols + key_cols].reshape(rows, kv_here, HEAD_DIM)
        value = values[:, query_cols + key_cols : qkv_cols].reshape(rows, kv_here, HEAD_DIM)
        return jnp.concatenate([query, key, value], axis=2).reshape(rows, qkv_cols)

    attention_low = attention_master.astype(low)
    hidden = activations.astype(jnp.float32)
    normed_own, attention_scaling = normalize(hidden, norm_gains[0])
    normed_own = normed_own.astype(low)
    normed = in_order(normed_own, swap_core(normed_own))

    seq_rows = normed.shape[0]
    half_width = HEAD_DIM // 2
    frequency = theta_base ** (-jnp.arange(half_width, dtype=jnp.float32) * 2.0 / HEAD_DIM)
    angles = jnp.arange(seq_rows, dtype=jnp.float32)[:, None] * frequency[None, :]
    cosine = jnp.tile(jnp.cos(angles), (1, LANES // half_width))
    sine = jnp.tile(jnp.sin(angles), (1, LANES // half_width))
    own_columns = jnp.concatenate([by_head(attention_low), attention_low[:, qkv_cols:]], axis=1)
    shard, for_far, for_near = round_weights(expert_master)
    line, w_inner, w_outer, devices, valid_total = gather_attention(
        own_columns,
        valid_here,
        qkv_cols,
        [shard, normed, cosine, sine] + routing_parts[1:],
    )
    starts = devices * rows_here
    near_bit, far_bit = WEIGHT_BITS
    for_near[0] = after(for_near[0], *w_inner[1:])
    near = [swap_dp(piece, near_bit) for piece in for_near]
    far = [swap_dp(after(piece, line), far_bit) for piece in for_far]

    q2, k2, v_high, attended, w_qkv, log_totals = attention_forward(
        lengths,
        starts,
        normed,
        w_inner,
        cosine,
        sine,
    )
    branch, branch_other, w_output = output_projection(
        starts, core.reshape(1).astype(jnp.int32), attended, w_outer, far[:1] + near[:1]
    )
    branch = branch + swap_core(branch_other).astype(jnp.float32)
    middle = hidden + branch
    mix_own, mix_scaling = normalize(middle, norm_gains[1])

    routing = jnp.stack(routing_parts).reshape(len(TOKEN_MASKS), 2 * TOPK, 2, own_rows)
    routing = jnp.stack(
        [
            lax.dynamic_index_in_dim(routing, core, 2, keepdims=False),
            lax.dynamic_index_in_dim(routing, 1 - core, 2, keepdims=False),
        ],
        axis=1,
    )
    unit_here = expert_master.shape[0]
    unit_ids = (unit_owners()[:, None] * unit_here + jnp.arange(unit_here)[None, :]).reshape(-1)
    expert_of = unit_ids // GROUPS
    per_unit = unit_here % 4 != 0
    if not per_unit:
        expert_of = expert_of[::4]
    named = (
        routing[:, :, None, :TOPK] == expert_of.astype(jnp.float32)[None, None, :, None, None]
    )
    route_columns = jnp.sum(jnp.where(named, routing[:, :, None, TOPK:], 0.0), axis=3)
    route_columns = route_columns.transpose(0, 1, 3, 2).reshape(-1, expert_of.shape[0])

    spread = spread_tokens(mix_own.astype(low), True)
    both = [swap_dp(piece, near_bit) for piece in far]
    later = [after(spread[1], far[1], near[1]), spread[2], after(spread[3], both[0])]
    mix_rows = with_other(spread[:1] + later)
    mix, mixed, *firsts = expert_first(
        mix_rows, route_columns, per_unit, [shard] + near, []
    )
    pieces = [shard] + near + far + both
    mixed_parts, seconds = expert_second(
        2 * len(spread), own_rows, mix, mixed, route_columns, per_unit, far + both, []
    )
    slopes, silus, inners = ([firsts[i], seconds[i]] for i in range(3))
    sums = [sum_cores(i, mixed_parts[2 * i : 2 * i + 2]) for i in range(len(TOKEN_MASKS))]
    output = middle + add_all(sums[0], return_tokens(sums))
    residual_error = output - targets
    loss_part = jnp.sum(valid_rows[:, None] * residual_error * residual_error)
    output_grad = 2.0 / valid_total * valid_rows[:, None] * residual_error

    spread = spread_tokens(output_grad.astype(low), False)
    backward = functools.partial(expert_backward, slopes=slopes, silus=silus, pieces=pieces)
    parts0, kept = backward(0, [spread[0], swap_core(spread[0])], kept=None)
    later = [after(rows, parts0[0]) for rows in spread[1:]]
    parts1, kept = backward(2, with_other(later), kept=kept)
    parts = list(parts0) + list(parts1)
    sums = [sum_cores(i, parts[2 * i : 2 * i + 2]) for i in range(len(TOKEN_MASKS))]
    returned = return_tokens(sums)
    output_low = kept[0]
    gates, uppers = kept[1:3], kept[3:5]
    full = cost(30e9)
    down_far = weight_grads([inners[1]], output_low, (), full)
    gate_far = weight_grads([gates[1]], mix, [down_far[0]] + sums[1:], full)
    down_sum = add_grads(down_far[1], down_far[0])
    upper_far = weight_grads([uppers[1]], mix, [gate_far[0], down_sum], full)
    gate_sum = add_grads(gate_far[1], gate_far[0])
    upper_sum = add_grads(upper_far[1], upper_far[0])
    returned[2] = after(returned[2], upper_far[0], gate_sum)
    sent = add_all(sums[0], returned)
    far_gate, far_upper, far_down = (
        swap_dp(rows, far_bit) for rows in (gate_sum, upper_sum, down_sum)
    )
    mix_back, gain_mix = normalize_back(middle, mix_scaling, norm_gains[1], sent)
    middle_grad = output_grad + mix_back
    branch_own = middle_grad.astype(low)
    branch_low = in_order(branch_own, swap_core(branch_own))
    dq, dkv = attention_backward(
        lengths, branch_low, w_output, q2, k2, v_high, log_totals, cosine, sine,
        [upper_far[0], gate_sum],
    )
    qkv_grad = jnp.concatenate(
        [dq.reshape(seq_rows, kv_here, LANES), dkv.reshape(seq_rows, kv_here, LANES)], axis=2
    ).reshape(seq_rows, qkv_cols)
    qkv_part = dot(normed, qkv_grad, 0, 0).astype(low)
    output_part = dot(branch_low, attended, 0, 0).astype(low)
    gate_up_near = weight_grads([gates[0], uppers[0]], mix, [qkv_part, output_part, upper_sum])
    qkv_stages = scatter_rows(qkv_part)
    qkv_part = qkv_stages[-1]
    down_near = weight_grads(
        [inners[0]], output_low, [gate_up_near[0]]
    )
    output_part = lax.psum_scatter(output_part, "dp", scatter_dimension=0, tiled=True)
    normed_grad_other = dot(other_half(qkv_grad), w_qkv, 1, 1).astype(low)
    normed_grad = dot(own_half(qkv_grad), w_qkv, 1, 1)
    normed_grad = normed_grad + swap_core(normed_grad_other).astype(jnp.float32)
    attention_back, gain_attention = normalize_back(
        hidden, attention_scaling, norm_gains[0], normed_grad
    )
    input_grad = middle_grad + attention_back
    parts = {
        2: grad_terms(down_near[1], down_near[0], far_down),
        0: grad_terms(gate_up_near[1], gate_up_near[0], far_gate),
        1: grad_terms(gate_up_near[3], gate_up_near[2], far_upper),
    }
    state = (expert_master, expert_left, expert_right, expert_left_root, expert_right_root)
    updated = expert_update(
        0, parts[0], state, None, [far_down, far_gate, qkv_stages[0]]
    )
    updated = expert_update(2, parts[2], state, updated, [input_grad, qkv_stages[1]] + parts[1][1:2])
    updated = expert_update(1, parts[1], state, updated)
    loss_row = jnp.full((1, D), loss_part)
    sums = jnp.concatenate([gain_attention[None], gain_mix[None], loss_row], axis=0)
    sums = sum_everywhere(after(sums, updated[0], output_part))
    expert_grad, expert_left_new, expert_right_new, expert_new = updated
    attention_grad, attention_left_new, attention_right_new, attention_new = attention_update(
        qkv_part,
        output_part,
        (
            attention_master,
            attention_left[0],
            attention_right[0],
            attention_left_root[0],
            attention_right_root[0],
        ),
    )
    gain_grad = sums[:2]
    mean_loss = sums[2, 0] / valid_total
    gains_new = norm_gains - gain_rate * tokens_total**0.5 * gain_grad

    return (
        output,
        mean_loss,
        input_grad,
        gain_grad,
        gains_new,
        attention_grad,
        attention_left_new[None],
        attention_right_new[None],
        attention_new,
        expert_grad,
        expert_left_new,
        expert_right_new,
        expert_new,
    )


def solution(mesh):
    return jax.shard_map(
        on_device,
        mesh=mesh,
        in_specs=(
            P(("dp", "tensor"), None),
            P(("dp", "tensor"), None),
            P("dp"),
            P(("dp", "tensor")),
            P("dp", None),
            P("dp", None),
            P(),
            P("dp", "tensor"),
            P("dp", None, "tensor", None),
            P("dp", "tensor", None, None),
            P("dp", "tensor", None, None),
            P("dp", "tensor", None, None),
            P("dp", "tensor", None, None),
            P("dp", None, None, "tensor", None),
            P("dp", None, "tensor", None, None),
            P("dp", None, None, "tensor", None),
            P("dp", None, "tensor", None, None),
        ),
        out_specs=(
            P(("dp", "tensor"), None),
            P(),
            P(("dp", "tensor"), None),
            P(),
            P(),
            P("dp", "tensor"),
            P("dp", "tensor", None, None),
            P("dp", "tensor", None, None),
            P("dp", "tensor"),
            P("dp", None, "tensor", None),
            P("dp", None, None, "tensor", None),
            P("dp", None, "tensor", None, None),
            P("dp", None, "tensor", None),
        ),
        check_vma=False,
    )
```
